32 devices in a mesh: parts: 2 (over x), lat: 16 (over z, y, core).
Axes of the slice: x: 2, y: 2, z: 4, core: 2. Of those that a mesh axis runs over, the one named last changes fastest.
Arguments:
- grid_field: float32 [368, 1440, 256], P('lat', None, 'parts'), parts along dimension 2, may hold values from -170 to 170
- norm_gain: float32 [128], P('parts'), parts along dimension 0, may hold values from 0.5 to 1.5
- filter_weight: bfloat16 [352, 2, 64, 128], P('lat', None, None, 'parts'), parts along dimension 3, may hold values from -0.5 to 0.5
Outputs:
- spectrum_out: bfloat16 [352, 352, 512], P('lat', None, 'parts'), parts along dimension 2
The draws below stay inside these ranges and needn't reach their ends.
There are 2 independent parts, one for each index of `parts`. The reference program is written for one: setup_inputs(seed, part) draws one part's arguments, and reference() takes and returns one part's arrays. A program takes and returns all parts, laid end to end along the dimension named above; each array names one. Nothing has to cross between parts.
All inputs are finite; a program needn't handle non-finite values.
Results may differ from the reference program's by a relative error of at most 0.0064.
Values may be sent and summed in bfloat16 or wider, within the bound.
A program may use at most 192 MiB of HBM per device.

```python
import math
import jax
import jax.numpy as jnp
from jax import lax

C = 64
S = 2
NLON = 1440
DEG_DEV = 22
NLAT = 368
L = 352
M = 352
N_LAT = 16


def draw_grid_field(key, part):
    noise_key = jax.random.fold_in(key, 11)
    across_key = jax.random.fold_in(key, 12)
    offset_key = jax.random.fold_in(key, 13)
    lat_fraction = jnp.arange(NLAT, dtype=jnp.float32) / (NLAT - 1)
    noise_field = jax.random.truncated_normal(noise_key, -4.0, 4.0, (NLAT, NLON, S * C), jnp.float32)
    rise_rows = jnp.exp(lat_fraction * jnp.log(10.0))
    across = jnp.exp(jax.random.uniform(across_key, (NLON,), jnp.float32, -1.15, 1.15))
    offset = jax.random.uniform(offset_key, (S * C,), jnp.float32, -2.0, 2.0)
    return noise_field * rise_rows[:, None, None] * across[None, :, None] + offset[None, None, :]


def levels(own_key, dims, split, low, top_value):
    factor_of, own = 1.0, jax.random.fold_in(own_key, 6)
    for axis_at, shards_of in split:
        heights = jnp.exp(jax.random.uniform(jax.random.fold_in(own, axis_at), (shards_of,), jnp.float32, low / len(split), top_value / len(split)))
        factor_of = factor_of * jnp.repeat(heights, dims[axis_at] // shards_of).reshape([-1 if axis == axis_at else 1 for axis in range(len(dims))])
    return factor_of


def centred(rng, extent, deviation, reach, shards=(), kind=jnp.bfloat16):
    array = deviation * jax.random.normal(rng, extent, jnp.float32)
    if shards:
        array = array * levels(rng, extent, shards, -0.22, 0.18)
    return jnp.clip(array, -reach, reach).astype(kind)


def setup_inputs(seed: int = 0, part: int = 0) -> dict:
    splits = jax.random.split(jax.random.key(seed), 4)
    part_keys = jax.random.split(jax.random.fold_in(splits[3], part), 4)
    return {
        "grid_field": draw_grid_field(jax.random.fold_in(jax.random.fold_in(splits[3], part), 71), part),
        "norm_gain": jnp.clip(1.0 + 0.1 * jax.random.normal(part_keys[1], (C,), jnp.float32), 0.5, 1.5),
        "filter_weight": centred(part_keys[2], (L, 2, C, C), (2 * C) ** -0.5, 0.5, ((0, 16),)),
    }


def legendre_table(colatitude, orders, degrees, weight_scale):
    cosine = jnp.cos(colatitude)[:, None]
    sine_rows = jnp.sin(colatitude)
    order_sq = orders * orders
    log_start = 0.5 * jnp.log((2.0 * orders + 1.0) / (4.0 * math.pi)) + 0.5 * (lax.lgamma(orders + 0.5) - lax.lgamma(orders + 1.0) - 0.5 * math.log(math.pi))
    log_diag = log_start[None, :] + orders[None, :] * jnp.log(sine_rows)[:, None]
    start_exp = 64.0 * jnp.floor(log_diag / (64.0 * math.log(2.0)))
    start_mant = jnp.exp(log_diag - start_exp * math.log(2.0))
    weights = (weight_scale * sine_rows)[:, None]
    limit = 2.0 ** 64
    shrink = 2.0 ** (-64)

    def recurrence(state, degree):
        previous, earlier, exponent = state
        degree_value = degree.astype(orders.dtype)
        upper_coef = jnp.sqrt((4.0 * degree_value * degree_value - 1.0) / jnp.maximum(degree_value * degree_value - order_sq, 1.0))
        below = degree_value - 1.0
        lower_coef = jnp.sqrt(jnp.maximum(below * below - order_sq, 0.0) / jnp.maximum(4.0 * below * below - 1.0, 1.0))
        recurred = upper_coef * (cosine * previous - lower_coef * earlier)
        at_start = degree_value == orders
        current = jnp.where(at_start, start_mant, jnp.where(degree_value > orders, recurred, 0.0))
        exponent = jnp.where(at_start, start_exp, exponent)
        value = (weights * (current * jnp.exp2(exponent))).astype(jnp.bfloat16)
        large = jnp.abs(current) > limit
        current = jnp.where(large, current * shrink, current)
        kept = jnp.where(large, previous * shrink, previous)
        exponent = jnp.where(large, exponent + 64.0, exponent)
        return ((current, kept, exponent), value)
    zero_state = jnp.zeros((colatitude.shape[0], orders.shape[0]), colatitude.dtype)
    last_state, stacked = lax.scan(recurrence, (zero_state, zero_state, zero_state), jnp.arange(degrees, dtype=jnp.int32), unroll=8)
    return stacked

def expand_filter(filter_weight):
    real_part = filter_weight[:, 0]
    imag_part = filter_weight[:, 1]
    from_real = jnp.stack([real_part, imag_part], axis=2)
    from_imag = jnp.stack([-imag_part, real_part], axis=2)
    return jnp.stack([from_real, from_imag], axis=1)

def apply_filter(coefficients, expanded):
    shaped = coefficients.reshape(coefficients.shape[0], coefficients.shape[1], 2, S, C)
    mixed = jnp.einsum('lmrsc,lrcqo->lmqso', shaped.astype(jnp.float32), expanded.astype(jnp.float32))
    return mixed.astype(jnp.bfloat16).reshape(coefficients.shape[0], coefficients.shape[1], 2 * S * C)

def reference(grid_field, norm_gain, filter_weight):
    lat_rows = jnp.arange(NLAT, dtype=jnp.int32)
    colatitude = math.pi * (lat_rows.astype(grid_field.dtype) + 0.5) / NLAT
    sine_rows = jnp.sin(colatitude)
    denominator = NLON * jnp.sum(sine_rows)
    first_moment = jnp.einsum('j,jnx->x', sine_rows, grid_field, precision=lax.Precision.HIGHEST)
    second_moment = jnp.einsum('j,jnx->x', sine_rows, grid_field * grid_field, precision=lax.Precision.HIGHEST)
    average = first_moment / denominator
    second_moment = second_moment / denominator
    spread = jnp.sqrt(second_moment - average * average + 1e-05)
    factor = jnp.tile(norm_gain, S) / spread
    transformed = jnp.fft.rfft(grid_field, axis=1)[:, :M, :]
    raw_spectrum = jnp.stack([jnp.real(transformed), jnp.imag(transformed)], axis=2)
    raw_spectrum = raw_spectrum.at[:, 0, 0, :].add(-NLON * average)
    fourier = (raw_spectrum * factor).astype(jnp.bfloat16).reshape(NLAT, M, 2 * S * C)
    expanded = expand_filter(filter_weight)
    weight_scale = math.pi ** 1.5 / math.sqrt(NLAT * NLON)

    def order_block(block_index):
        orders = (block_index * DEG_DEV + jnp.arange(DEG_DEV, dtype=jnp.int32)).astype(colatitude.dtype)
        legendre = legendre_table(colatitude, orders, L, weight_scale)
        panel_piece = lax.dynamic_slice_in_dim(fourier, block_index * DEG_DEV, DEG_DEV, 1)
        coefficients = jnp.einsum('ljm,jmx->lmx', legendre.astype(jnp.float32), panel_piece.astype(jnp.float32)).astype(jnp.bfloat16)
        return apply_filter(coefficients, expanded)
    blocks_out = lax.map(order_block, jnp.arange(N_LAT, dtype=jnp.int32))
    return jnp.transpose(blocks_out, (1, 0, 2, 3)).reshape(L, M, 2 * S * C)
```

```python
import functools
import math

import jax
import jax.numpy as jnp
import numpy as np
from jax import lax
from jax.experimental import pallas as pl
from jax.experimental.pallas import tpu as pltpu
from jax.sharding import PartitionSpec as P

C = 64
S = 2
DEG_DEV = 22
ORDER_PAD = 24
BLOCK = 16
LANES = 128


def round_up(value, step):
    return -(-value // step) * step


def legendre_kernel(
    orders_ref, cosine_ref, weights_ref, mant_ref, exp_ref, out_ref, prev_ref, early_ref, grow_ref, rows_ref
):
    block = pl.program_id(0)
    width = cosine_ref.shape[1]
    kept_width = out_ref.shape[2]

    @pl.when(block == 0)
    def _():
        prev_ref[...] = jnp.zeros_like(prev_ref)
        early_ref[...] = jnp.zeros_like(early_ref)
        grow_ref[...] = jnp.zeros_like(grow_ref)

    orders = orders_ref[...]
    narrow = orders[:, :LANES]
    order_sq = narrow * narrow
    cosine = cosine_ref[...]
    weights = weights_ref[...]
    limit = 2.0**64
    shrink = 2.0 ** (-64)
    previous, earlier, exponent = prev_ref[...], early_ref[...], grow_ref[...]
    first = (block * BLOCK).astype(jnp.float32)

    def widen(value):
        return jnp.concatenate([value] * (width // LANES), axis=1)

    for step in range(BLOCK):
        degree = first + float(step)
        upper = jnp.sqrt(
            (4.0 * degree * degree - 1.0) / jnp.maximum(degree * degree - order_sq, 1.0)
        )
        below = degree - 1.0
        lower = jnp.sqrt(
            jnp.maximum(below * below - order_sq, 0.0)
            / jnp.maximum(jnp.full_like(order_sq, 4.0 * below * below - 1.0), 1.0)
        )
        recurred = widen(upper) * (cosine * previous - widen(lower) * earlier)
        at_start = orders == degree
        current = jnp.where(at_start, mant_ref[...], jnp.where(orders < degree, recurred, 0.0))
        exponent = jnp.where(at_start, exp_ref[...], exponent)
        value = weights * (current * jnp.exp2(exponent))
        for lane in range(width // LANES):
            rows_ref[lane, step * ORDER_PAD : (step + 1) * ORDER_PAD, :] = value[
                :, lane * LANES : (lane + 1) * LANES
            ]
        large = jnp.abs(current) > limit
        earlier = jnp.where(large, previous * shrink, previous)
        previous = jnp.where(large, current * shrink, current)
        exponent = jnp.where(large, exponent + 64.0, exponent)

    prev_ref[...] = previous
    early_ref[...] = earlier
    grow_ref[...] = exponent
    for order in range(DEG_DEV):
        for lane in range(0, width, LANES):
            cut = min(LANES, kept_width - lane)
            piece = rows_ref[lane // LANES, pl.ds(order, BLOCK, stride=ORDER_PAD), :]
            out_ref[order, :, lane : lane + cut] = piece[:, :cut].astype(out_ref.dtype)


def legendre_table(colatitude, first_order, degrees, weight_scale):
    rows = colatitude.shape[0]
    width = round_up(rows, LANES)
    colat = jnp.concatenate([colatitude, jnp.full((width - rows,), 0.5 * math.pi, jnp.float32)])
    orders = (first_order + jnp.arange(ORDER_PAD, dtype=jnp.int32)).astype(jnp.float32)
    sine_rows = jnp.sin(colat)
    log_start = 0.5 * jnp.log((2.0 * orders + 1.0) / (4.0 * math.pi)) + 0.5 * (
        lax.lgamma(orders + 0.5) - lax.lgamma(orders + 1.0) - 0.5 * math.log(math.pi)
    )
    log_diag = log_start[:, None] + orders[:, None] * jnp.log(sine_rows)[None, :]
    start_exp = 64.0 * jnp.floor(log_diag / (64.0 * math.log(2.0)))
    start_mant = jnp.exp(log_diag - start_exp * math.log(2.0))
    state = (ORDER_PAD, width)
    whole = pl.BlockSpec(state, lambda i: (0, 0))
    line = pl.BlockSpec((1, width), lambda i: (0, 0))
    return pl.pallas_call(
        legendre_kernel,
        grid=(degrees // BLOCK,),
        out_shape=jax.ShapeDtypeStruct((DEG_DEV, degrees, rows), jnp.bfloat16),
        in_specs=[whole, line, line, whole, whole],
        out_specs=pl.BlockSpec((DEG_DEV, BLOCK, rows), lambda i: (0, i, 0)),
        scratch_shapes=[
            pltpu.VMEM(state, jnp.float32),
            pltpu.VMEM(state, jnp.float32),
            pltpu.VMEM(state, jnp.float32),
            pltpu.VMEM((width // LANES, BLOCK * ORDER_PAD, LANES), jnp.float32),
        ],
        cost_estimate=pl.CostEstimate(
            flops=degrees * ORDER_PAD * width * 2000,
            bytes_accessed=DEG_DEV * degrees * rows * 2,
            transcendentals=degrees * ORDER_PAD * width,
        ),
        compiler_params=pltpu.CompilerParams(vmem_limit_bytes=24 * 1024 * 1024),
    )(
        jnp.broadcast_to(orders[:, None], state),
        jnp.cos(colat)[None, :],
        (weight_scale * sine_rows)[None, :],
        start_mant,
        start_exp,
    )


def expand_filter(filter_weight):
    real_part = filter_weight[:, 0]
    imag_part = filter_weight[:, 1]
    from_real = jnp.stack([real_part, imag_part], axis=1)
    from_imag = jnp.stack([-imag_part, real_part], axis=1)
    mixing = jnp.stack([from_real, from_imag], axis=1)
    same = jnp.eye(S, dtype=filter_weight.dtype)
    full = mixing.transpose(0, 1, 3, 2, 4)[:, :, None, :, :, None, :] * same[None, None, :, None, None, :, None]
    return full.reshape(filter_weight.shape[0], 2 * S * C, 2 * S * C)


def mix_kernel(sin_ref, cos_ref, weight_ref, out_ref, rows_ref):
    sources, degrees, orders, half = cos_ref.shape
    for degree in range(degrees):
        for source in range(sources):
            rows = slice(source * orders, (source + 1) * orders)
            rows_ref[degree, rows, :half] = cos_ref[source, degree].astype(jnp.float32)
            rows_ref[degree, rows, half:] = sin_ref[source, degree].astype(jnp.float32)
        out_ref[degree] = jnp.dot(
            rows_ref[degree].astype(jnp.bfloat16),
            weight_ref[degree],
            preferred_element_type=jnp.float32,
        ).astype(out_ref.dtype)


def mix(coef_sin, coef_cos, weights):
    sources, degrees, orders, half = coef_cos.shape
    wide = weights.shape[2]
    step = 2
    piece = pl.BlockSpec((sources, step, orders, half), lambda i: (0, i, 0, 0))
    return pl.pallas_call(
        mix_kernel,
        grid=(degrees // step,),
        out_shape=jax.ShapeDtypeStruct((degrees, sources * orders, wide), jnp.bfloat16),
        in_specs=[piece, piece, pl.BlockSpec((step, 2 * half, wide), lambda i: (i, 0, 0))],
        out_specs=pl.BlockSpec((step, sources * orders, wide), lambda i: (i, 0, 0)),
        scratch_shapes=[pltpu.VMEM((step, sources * orders, 2 * half), jnp.float32)],
        compiler_params=pltpu.CompilerParams(vmem_limit_bytes=24 * 1024 * 1024),
    )(coef_sin, coef_cos, weights)


def fourier_matrix(orders, longitudes):
    phases = (np.arange(orders)[:, None] * np.arange(longitudes)[None, :]) % longitudes
    angles = 2.0 * np.pi * phases / longitudes
    return np.stack([np.cos(angles), -np.sin(angles)]).astype(np.float32)


def plain_body(grid_field, norm_gain, filter_weight):
    device_index = lax.axis_index("lat")
    lat_count = lax.axis_size("lat")
    band_rows, longitudes, columns = grid_field.shape
    total_lat = band_rows * lat_count
    order_count = DEG_DEV * lat_count
    all_rows = jnp.arange(total_lat, dtype=jnp.int32)
    colat_all = math.pi * (all_rows.astype(jnp.float32) + 0.5) / total_lat
    sine_all = jnp.sin(colat_all)
    own_rows = device_index * band_rows + jnp.arange(band_rows, dtype=jnp.int32)
    sine_own = jnp.sin(math.pi * (own_rows.astype(jnp.float32) + 0.5) / total_lat)

    first = jnp.einsum("j,jnx->x", sine_own, grid_field, precision=lax.Precision.HIGHEST)
    second = jnp.einsum(
        "j,jnx->x", sine_own, grid_field * grid_field, precision=lax.Precision.HIGHEST
    )
    band_mean = first / (longitudes * jnp.sum(sine_own))
    denominator_rows = jnp.float32(longitudes)
    cos_table, sin_table = fourier_matrix(order_count, longitudes)

    def transform(table):
        return jnp.einsum(
            "mn,jnx->mjx", jnp.asarray(table), grid_field, precision=lax.Precision.HIGH
        )

    def to_orders(raw):
        return lax.all_to_all(
            raw.astype(jnp.bfloat16), "lat", split_axis=0, concat_axis=1, tiled=True
        )

    def to_degrees(sums):
        return lax.all_to_all(
            sums, "lat", split_axis=0, concat_axis=0
        )

    received_sin = to_orders(transform(sin_table))
    constant = jnp.arange(order_count) == 0
    shift = jnp.where(constant[:, None, None], denominator_rows * band_mean, 0.0)
    received_cos = to_orders(transform(cos_table) - shift)

    weight_scale = math.pi**1.5 / math.sqrt(total_lat * longitudes)
    legendre = legendre_table(colat_all, device_index * DEG_DEV, order_count, weight_scale)

    def analyse(received):
        return jnp.einsum("mlj,mjx->mlx", legendre, received, preferred_element_type=jnp.float32)

    def by_degree(sums):
        ordered = sums.astype(jnp.bfloat16).transpose(1, 0, 2)
        return ordered.reshape(lat_count, DEG_DEV, DEG_DEV, columns)

    sums_sin = by_degree(analyse(received_sin))
    moments, sums_sin = lax.optimization_barrier(
        (jnp.stack([first, second, band_mean]), sums_sin)
    )
    gathered, sums_sin = lax.optimization_barrier((lax.all_gather(moments, "lat"), sums_sin))
    denominator = longitudes * jnp.sum(sine_all)
    average = jnp.sum(gathered[:, 0], axis=0) / denominator
    mean_square = jnp.sum(gathered[:, 1], axis=0) / denominator
    spread = jnp.sqrt(mean_square - average * average + 1e-05)
    factor = jnp.tile(norm_gain, S) / spread
    coef_sin = to_degrees(sums_sin)
    band_sums = jnp.sum(
        legendre[0].astype(jnp.float32).reshape(order_count, lat_count, band_rows), axis=2
    )
    level = jnp.dot(
        band_sums,
        denominator_rows * (gathered[:, 2] - average),
        precision=lax.Precision.HIGHEST,
    )
    here = (device_index == 0) & (jnp.arange(DEG_DEV) == 0)
    coef_cos = to_degrees(
        by_degree(analyse(received_cos) + jnp.where(here[:, None, None], level[None], 0.0))
    )

    expanded = expand_filter(filter_weight)
    expanded = (expanded * jnp.tile(factor, 2)[None, :, None]).astype(jnp.bfloat16)

    return mix(coef_sin, coef_cos, expanded)


MESH = pl.DeviceIdType.MESH
ROWS = 8
WIDE = 2 * LANES
CHUNKS = 3
PLANE = 4
PLANE_CHUNKS = PLANE * CHUNKS - 1
VMEM_CAP = 60 * 1024 * 1024


def owner_rank(device):
    plane, inner = device // PLANE, device % PLANE
    flip = (inner // 2 + plane) % 2
    core = inner % 2
    return flip * (1 + core) + (1 - flip) * (PLANE - 1) * core


def owner_chunk(device, slot, count):
    plane = device // PLANE
    base = PLANE_CHUNKS * (count // PLANE - 1 - plane)
    return base + PLANE_CHUNKS - 1 - PLANE * slot - owner_rank(device)


def transform_tables(count, longitudes):
    table = np.zeros((CHUNKS, 2, count, ROWS, longitudes), np.float64)
    for slot in range(CHUNKS):
        for device in range(count):
            if slot == CHUNKS - 1 and owner_rank(device) == PLANE - 1:
                continue
            orders = owner_chunk(device, slot, count) * ROWS + np.arange(ROWS)
            phases = (orders[:, None] * np.arange(longitudes)[None, :]) % longitudes
            angles = 2.0 * np.pi * phases / longitudes
            table[slot, 0, device] = np.cos(angles)
            table[slot, 1, device] = -np.sin(angles)
    table = table.reshape(CHUNKS, 2 * count * ROWS, longitudes).astype(np.float32)
    high = table.astype(jnp.bfloat16)
    low = (table - high.astype(np.float32)).astype(jnp.bfloat16)
    return high, low


def angle_tables(count, band, places):
    colat = np.pi * (np.arange(count * band) + 0.5) / (count * band)
    by_place = np.full((count, places), 0.5 * np.pi)
    valid = np.zeros((count, places))
    for device in range(count):
        rows = colat[device * band : (device + 1) * band]
        by_place[device, :band] = rows if device < count // 2 else rows[::-1]
        valid[device, :band] = 1.0
    sine_places = np.sin(by_place) * valid
    north = by_place[: count // 2].reshape(1, -1)
    weight = sine_places[: count // 2].reshape(1, -1)
    width = round_up(north.shape[1], LANES)
    north = np.pad(north, ((0, 0), (0, width - north.shape[1])), constant_values=0.5 * np.pi)
    weight = np.pad(weight, ((0, 0), (0, width - weight.shape[1])))
    return (
        sine_places.reshape(-1).astype(np.float32),
        np.cos(north).astype(np.float32),
        weight,
        np.log(np.sin(north)).astype(np.float32),
        float(np.sum(np.sin(colat))),
    )


def log_starts(order_count):
    values = [
        0.5 * math.log((2.0 * m + 1.0) / (4.0 * math.pi))
        + 0.5 * (math.lgamma(m + 0.5) - math.lgamma(m + 1.0) - 0.5 * math.log(math.pi))
        for m in range(order_count)
    ]
    return np.broadcast_to(np.asarray(values, np.float32)[:, None], (order_count, LANES))


def spectral_kernel(
    sizes,
    field_ref,
    gain_ref,
    high_ref,
    low_ref,
    sine_ref,
    cosine_ref,
    weight_ref,
    logsine_ref,
    start_ref,
    out_ref,
    high,
    low,
    stage,
    field_high,
    field_low,
    turned,
    outgoing,
    landed,
    moments,
    moments_all,
    scales,
    table,
    prev_ref,
    early_ref,
    grow_ref,
    mant_ref,
    exp_ref,
    lines,
    sums,
    sums_out,
    table_sem,
    stage_sem,
    moment_send,
    moment_recv,
    send_sem,
    recv_sem,
    local_sem,
    send_two,
    recv_two,
):
    count, band, longitudes, total_sine = sizes
    me = lax.axis_index("lat")
    part = lax.axis_index("parts")
    half = count // 2
    south = me // half
    slot_of_me = me + south * (half + count - 1 - 2 * me)
    groups = outgoing.shape[0] // CHUNKS
    places = groups * ROWS
    degrees = table.shape[1]
    kept = table.shape[2]
    width = cosine_ref.shape[1]
    block_rows = DEG_DEV * ROWS
    zero_owner = [
        d for d in range(count) if owner_chunk(d, CHUNKS - 1, count) == 0 and owner_rank(d) < PLANE - 1
    ][0]
    has_last = owner_rank(me) < PLANE - 1

    def has_chunk(slot, device):
        return (slot < CHUNKS - 1) | (owner_rank(device) < PLANE - 1)

    def table_copies(slot):
        return (
            pltpu.make_async_copy(high_ref.at[slot], high.at[slot], table_sem.at[0, slot]),
            pltpu.make_async_copy(low_ref.at[slot], low.at[slot], table_sem.at[1, slot]),
        )

    def row_copy(place):
        row = place + south * (band - 1 - 2 * place)
        at = place % ROWS
        return pltpu.make_async_copy(field_ref.at[row], stage.at[at], stage_sem.at[at])

    for place in range(2):
        row_copy(place).start()
    for copy in table_copies(0):
        copy.start()
    for place in range(2, ROWS):
        row_copy(place).start()
    for slot in range(1, CHUNKS):
        for copy in table_copies(slot):
            copy.start()

    barrier = pltpu.get_barrier_semaphore()

    @pl.loop(1, count)
    def _(step):
        pl.semaphore_signal(
            barrier, inc=1, device_id=(part, (me + step) % count), device_id_type=MESH
        )

    moments[...] = jnp.zeros_like(moments)
    for place in range(band, places):
        lanes = slice((place % 2) * LANES, (place % 2 + 1) * LANES)
        field_high[place // 2, :, lanes] = jnp.zeros((longitudes, LANES), jnp.bfloat16)
        field_low[place // 2, :, lanes] = jnp.zeros((longitudes, LANES), jnp.bfloat16)

    piece = longitudes // 6

    def take_row(place, lanes):
        row_copy(place).wait()
        at = place % ROWS
        pair = place // 2
        total = jnp.zeros((ROWS, LANES), jnp.float32)
        square = jnp.zeros((ROWS, LANES), jnp.float32)
        for first in range(0, longitudes, piece):
            value = stage[at, first : first + piece, :]
            top = value.astype(jnp.bfloat16)
            field_high[pair, first : first + piece, lanes] = top
            field_low[pair, first : first + piece, lanes] = (
                value - top.astype(jnp.float32)
            ).astype(jnp.bfloat16)
            total += jnp.sum(value.reshape(-1, ROWS, LANES), axis=0)
            square += jnp.sum((value * value).reshape(-1, ROWS, LANES), axis=0)
        sine = sine_ref[me * places + place]
        moments[:ROWS] += sine * total
        moments[ROWS:] += sine * square

        @pl.when(place + ROWS < band)
        def _():
            row_copy(place + ROWS).start()

    def take_group(group):
        @pl.loop(0, ROWS // 2)
        def _(pair):
            place = group * ROWS + 2 * pair
            take_row(place, slice(0, LANES))

            @pl.when(place + 1 < band)
            def _():
                take_row(place + 1, slice(LANES, WIDE))

    take_group(0)
    pl.semaphore_wait(barrier, count - 1)

    def moment_copy(device):
        return pltpu.make_async_remote_copy(
            moments,
            moments_all.at[me],
            moment_send,
            moment_recv,
            device_id=(part, device),
            device_id_type=MESH,
        )

    def order_copy(slot, group, device):
        step = slot * groups + group
        rows = pl.ds(pl.multiple_of(device * ROWS * ROWS, ROWS * ROWS), ROWS * ROWS)
        return pltpu.make_async_remote_copy(
            outgoing.at[step, rows],
            landed.at[slot, slot_of_me, group],
            send_sem.at[step],
            recv_sem.at[slot],
            device_id=(part, device),
            device_id_type=MESH,
        )

    def own_copy(slot, group):
        step = slot * groups + group
        rows = pl.ds(pl.multiple_of(me * ROWS * ROWS, ROWS * ROWS), ROWS * ROWS)
        return pltpu.make_async_copy(
            outgoing.at[step, rows], landed.at[slot, slot_of_me, group], local_sem.at[step]
        )

    @pl.loop(0, CHUNKS * groups)
    def _(step):
        slot, group = step // groups, step % groups

        @pl.when((step > 0) & (slot == 0))
        def _():
            take_group(group)

        @pl.when(step == groups - 1)
        def _():
            moments_all[me] = moments[...]

            @pl.loop(1, count)
            def _(ahead):
                moment_copy((me + ahead) % count).start()

        @pl.when(group == 0)
        def _():
            for copy in table_copies(slot):
                copy.wait()

        @pl.when(step == (CHUNKS - 1) * groups)
        def _():
            pltpu.make_async_copy(
                moments_all.at[pl.ds(0, count - 1)],
                moments_all.at[pl.ds(0, count - 1)],
                moment_recv,
            ).wait()
            gathered = jnp.sum(moments_all[...], axis=0)
            first = jnp.sum(gathered[:ROWS], axis=0, keepdims=True) / (longitudes * total_sine)
            second = jnp.sum(gathered[ROWS:], axis=0, keepdims=True) / (longitudes * total_sine)
            spread = jnp.sqrt(second - first * first + 1e-05)
            gain = gain_ref[...]
            factor = jnp.concatenate([gain] * S, axis=1) / spread
            scales[:1] = jnp.concatenate([factor, factor], axis=1)
            scales[1:2] = jnp.concatenate([longitudes * first, jnp.zeros_like(first)], axis=1)

        @pl.loop(0, ROWS // 2)
        def _(pair):
            at = group * (ROWS // 2) + pair
            product = jnp.dot(high[slot], field_high[at], preferred_element_type=jnp.float32)
            product += jnp.dot(high[slot], field_low[at], preferred_element_type=jnp.float32)
            product += jnp.dot(low[slot], field_high[at], preferred_element_type=jnp.float32)
            lines_of = count * ROWS
            for side in range(2):
                for row in range(2):
                    turned[side, pl.ds(2 * pair + row, lines_of, stride=ROWS), :] = product[
                        side * lines_of : (side + 1) * lines_of, row * LANES : (row + 1) * LANES
                    ]

        @pl.when(slot == CHUNKS - 1)
        def _():
            at = zero_owner * ROWS * ROWS
            turned[0, at : at + ROWS, :] -= scales[1:2, :LANES]

        @pl.loop(0, count)
        def _(ahead):
            device = (me + 1 + ahead) % count
            rows = pl.ds(pl.multiple_of(device * ROWS * ROWS, ROWS * ROWS), ROWS * ROWS)
            outgoing[step, rows, :] = jnp.concatenate(
                [turned[0, rows, :], turned[1, rows, :]], axis=1
            ).astype(jnp.bfloat16)

            @pl.when((device != me) & has_chunk(slot, device))
            def _():
                order_copy(slot, group, device).start()

            @pl.when((device == me) & has_chunk(slot, device))
            def _():
                own_copy(slot, group).start()

    chunk_of = [owner_chunk(me, slot, count) for slot in range(CHUNKS)]
    chunk_of[-1] = jnp.maximum(chunk_of[-1], 0)
    lines_in = lax.broadcasted_iota(jnp.int32, (ROWS, width), 0)
    orders = jnp.concatenate(
        [(chunk * ROWS + lines_in).astype(jnp.float32) for chunk in chunk_of], axis=0
    )
    start = jnp.concatenate(
        [start_ref[pl.ds(pl.multiple_of(chunk * ROWS, ROWS), ROWS), :] for chunk in chunk_of], axis=0
    )

    def widen(value):
        return jnp.concatenate([value] * (width // LANES), axis=1)

    log_diag = widen(start) + orders * logsine_ref[...]
    start_exp = 64.0 * jnp.floor(log_diag / (64.0 * math.log(2.0)))
    exp_ref[...] = start_exp
    mant_ref[...] = jnp.exp(log_diag - start_exp * math.log(2.0))
    prev_ref[...] = jnp.zeros_like(prev_ref)
    early_ref[...] = jnp.zeros_like(early_ref)
    grow_ref[...] = jnp.zeros_like(grow_ref)
    order_lines = CHUNKS * ROWS

    @pl.loop(0, degrees // BLOCK)
    def _(block):
        narrow = orders[:, :LANES]
        order_sq = narrow * narrow
        cosine = cosine_ref[...]
        weights = weight_ref[...]
        limit = 2.0**64
        shrink = 2.0 ** (-64)
        previous, earlier, exponent = prev_ref[...], early_ref[...], grow_ref[...]
        first = (block * BLOCK).astype(jnp.float32)
        for step in range(BLOCK):
            degree = first + float(step)
            upper = jnp.sqrt(
                (4.0 * degree * degree - 1.0) / jnp.maximum(degree * degree - order_sq, 1.0)
            )
            below = degree - 1.0
            lower = jnp.sqrt(
                jnp.maximum(below * below - order_sq, 0.0)
                / jnp.maximum(jnp.full_like(order_sq, 4.0 * below * below - 1.0), 1.0)
            )
            recurred = widen(upper) * (cosine * previous - widen(lower) * earlier)
            at_start = orders == degree
            current = jnp.where(at_start, mant_ref[...], jnp.where(orders < degree, recurred, 0.0))
            exponent = jnp.where(at_start, exp_ref[...], exponent)
            value = weights * (current * jnp.exp2(exponent))
            for lane in range(width // LANES):
                lines[lane, step * order_lines : (step + 1) * order_lines, :] = value[
                    :, lane * LANES : (lane + 1) * LANES
                ]
            large = jnp.abs(current) > limit
            earlier = jnp.where(large, previous * shrink, previous)
            previous = jnp.where(large, current * shrink, current)
            exponent = jnp.where(large, exponent + 64.0, exponent)
        prev_ref[...] = previous
        early_ref[...] = earlier
        grow_ref[...] = exponent
        rows = pl.ds(pl.multiple_of(block * BLOCK, BLOCK), BLOCK)
        for order in range(order_lines):
            for lane in range(0, width, LANES):
                cut = min(LANES, kept - lane)
                part_of = lines[lane // LANES, pl.ds(order, BLOCK, stride=order_lines), :]
                table[order, rows, lane : lane + cut] = part_of[:, :cut].astype(table.dtype)

    def reaches(chunk, device):
        return chunk * ROWS <= device * DEG_DEV + DEG_DEV - 1

    def degree_copy(slot, device):
        chunk = owner_chunk(me, slot, count)
        rows = pl.ds(pl.multiple_of(device * block_rows, block_rows), block_rows)
        return pltpu.make_async_remote_copy(
            sums_out.at[slot, rows],
            out_ref.at[chunk],
            send_two.at[slot, device],
            recv_two.at[chunk],
            device_id=(part, device),
            device_id_type=MESH,
        )

    def own_degrees(slot):
        chunk = owner_chunk(me, slot, count)
        rows = pl.ds(pl.multiple_of(me * block_rows, block_rows), block_rows)
        return pltpu.make_async_copy(sums_out.at[slot, rows], out_ref.at[chunk], recv_two.at[chunk])

    degree_line = lax.broadcasted_iota(jnp.int32, (degrees, 1), 0)
    sign_even = jnp.where(degree_line % 2 == 0, 1.0, -1.0).astype(jnp.float32)

    def analyse(slot):
        pltpu.make_async_copy(
            landed.at[slot, pl.ds(0, count - 1)],
            landed.at[slot, pl.ds(0, count - 1)],
            recv_sem.at[slot],
        ).wait()
        for group in range(groups):
            own_copy(slot, group).wait()

        @pl.loop(0, ROWS // 2)
        def _(pair):
            rows = pl.ds(pl.multiple_of(pair * 2 * ROWS, 2 * ROWS), 2 * ROWS)
            both = landed[slot, :, :, rows, :].astype(jnp.float32)
            both = both.reshape(count * groups, 2, ROWS, WIDE)
            for odd in range(2):
                rhs = both[:, odd].reshape(count * places, WIDE).astype(jnp.bfloat16)
                lhs = table[slot * ROWS + 2 * pair + odd]
                north = jnp.dot(lhs, rhs[:kept], preferred_element_type=jnp.float32)
                mirror = jnp.dot(lhs, rhs[kept:], preferred_element_type=jnp.float32)
                sign = sign_even if odd == 0 else -sign_even
                result = (north + sign * mirror) * scales[:1]
                for lane in range(2):
                    sums[lane, pl.ds(2 * pair + odd, degrees, stride=ROWS), :] = result[
                        :, lane * LANES : (lane + 1) * LANES
                    ]

        @pl.loop(0, count)
        def _(ahead):
            device = (me + 1 + ahead) % count
            rows = pl.ds(pl.multiple_of(device * block_rows, block_rows), block_rows)
            sums_out[slot, rows, :] = jnp.concatenate(
                [sums[0, rows, :], sums[1, rows, :]], axis=1
            ).astype(jnp.bfloat16)
            wanted = reaches(owner_chunk(me, slot, count), device)

            @pl.when(wanted & (device != me))
            def _():
                degree_copy(slot, device).start()

            @pl.when(wanted & (device == me))
            def _():
                own_degrees(slot).start()

    @pl.loop(0, CHUNKS)
    def _(slot):
        @pl.when((slot < CHUNKS - 1) | has_last)
        def _():
            analyse(slot)

    pltpu.make_async_copy(
        moments_all.at[pl.ds(0, count - 1)], moments_all.at[pl.ds(0, count - 1)], moment_send
    ).wait()

    def wait_orders(step, devices):
        rows = pl.ds(0, devices * ROWS * ROWS)
        pltpu.make_async_copy(
            outgoing.at[step, rows], outgoing.at[step, rows], send_sem.at[step]
        ).wait()

    @pl.loop(0, (CHUNKS - 1) * groups)
    def _(step):
        wait_orders(step, count - 1)

    last_owners = count - count // PLANE

    @pl.loop((CHUNKS - 1) * groups, CHUNKS * groups)
    def _(step):
        @pl.when(has_last)
        def _():
            wait_orders(step, last_owners - 1)

        @pl.when(jnp.logical_not(has_last))
        def _():
            wait_orders(step, last_owners)

    @pl.loop(0, CHUNKS)
    def _(slot):
        @pl.loop(0, count)
        def _(device):
            wanted = reaches(owner_chunk(me, slot, count), device)

            @pl.when(wanted & (device != me) & has_chunk(slot, me))
            def _():
                degree_copy(slot, device).wait_send()

    @pl.loop(0, (me * DEG_DEV + DEG_DEV - 1) // ROWS + 1)
    def _(chunk):
        pltpu.make_async_copy(out_ref.at[chunk], out_ref.at[chunk], recv_two.at[chunk]).wait()


def scratch_of(count, band, longitudes):
    groups = -(-band // ROWS)
    places = groups * ROWS
    degrees = DEG_DEV * count
    lines_of = count * ROWS
    kept = count // 2 * places
    width = round_up(kept, LANES)
    order_lines = CHUNKS * ROWS
    state = (order_lines, width)
    bf16, f32 = jnp.bfloat16, jnp.float32
    return [
        ((CHUNKS, 2 * lines_of, longitudes), bf16),
        ((CHUNKS, 2 * lines_of, longitudes), bf16),
        ((ROWS, longitudes, LANES), f32),
        ((places // 2, longitudes, WIDE), bf16),
        ((places // 2, longitudes, WIDE), bf16),
        ((2, lines_of * ROWS, LANES), f32),
        ((CHUNKS * groups, lines_of * ROWS, WIDE), bf16),
        ((CHUNKS, count, groups, ROWS * ROWS, WIDE), bf16),
        ((2 * ROWS, LANES), f32),
        ((count, 2 * ROWS, LANES), f32),
        ((ROWS, WIDE), f32),
        ((order_lines, degrees, kept), bf16),
        (state, f32),
        (state, f32),
        (state, f32),
        (state, f32),
        (state, f32),
        ((width // LANES, BLOCK * order_lines, LANES), f32),
        ((2, degrees * ROWS, LANES), f32),
        ((CHUNKS, degrees * ROWS, WIDE), bf16),
    ]


def scratch_bytes(shapes):
    total = 0
    for shape, dtype in shapes:
        size = math.prod(shape[:-1]) * round_up(shape[-1], LANES)
        total += size * jnp.dtype(dtype).itemsize
    return total


def coefficients_of(grid_field, norm_gain, count):
    band, longitudes, columns = grid_field.shape
    groups = -(-band // ROWS)
    places = groups * ROWS
    order_count = DEG_DEV * count
    high, low = transform_tables(count, longitudes)
    sine, cosine, weight, logsine, total_sine = angle_tables(count, band, places)
    weight_scale = math.pi**1.5 / math.sqrt(count * band * longitudes)
    shapes = scratch_of(count, band, longitudes)
    dma = pltpu.SemaphoreType.DMA
    vmem = pl.BlockSpec(memory_space=pltpu.VMEM)
    anywhere = pl.BlockSpec(memory_space=pl.ANY)
    return pl.pallas_call(
        functools.partial(spectral_kernel, (count, band, longitudes, total_sine)),
        out_shape=jax.ShapeDtypeStruct((order_count // ROWS, DEG_DEV * ROWS, WIDE), jnp.bfloat16),
        in_specs=[
            anywhere,
            vmem,
            anywhere,
            anywhere,
            pl.BlockSpec(memory_space=pltpu.SMEM),
            vmem,
            vmem,
            vmem,
            vmem,
        ],
        out_specs=anywhere,
        scratch_shapes=[pltpu.VMEM(shape, dtype) for shape, dtype in shapes]
        + [
            dma((2, CHUNKS)),
            dma((ROWS,)),
            dma,
            dma,
            dma((CHUNKS * groups,)),
            dma((CHUNKS,)),
            dma((CHUNKS * groups,)),
            dma((CHUNKS, count)),
            dma((order_count // ROWS,)),
        ],
        cost_estimate=pl.CostEstimate(
            flops=20 * 10**9, bytes_accessed=40 * 10**6, transcendentals=10**6
        ),
        compiler_params=pltpu.CompilerParams(
            collective_id=0, has_side_effects=True, vmem_limit_bytes=VMEM_CAP
        ),
    )(
        grid_field,
        norm_gain[None, :],
        jnp.asarray(high),
        jnp.asarray(low),
        jnp.asarray(sine),
        jnp.asarray(cosine),
        jnp.asarray((weight * weight_scale).astype(np.float32)),
        jnp.asarray(logsine),
        jnp.asarray(log_starts(order_count)),
    )


def filter_kernel(coef_ref, weight_ref, out_ref, full_ref):
    chunks = coef_ref.shape[0]
    orders = chunks * ROWS
    first = pl.program_id(0) * 2 + lax.axis_index("lat") * DEG_DEV
    both = coef_ref[...].astype(jnp.float32).reshape(chunks, 2, ROWS, WIDE)
    lines = lax.broadcasted_iota(jnp.int32, (orders, 1), 0)

    @pl.when(pl.program_id(0) == 0)
    def _():
        full_ref[...] = jnp.zeros_like(full_ref)

    for odd in range(2):
        value = both[:, odd].reshape(orders, WIDE)
        value = jnp.where(lines <= first + odd, value, 0.0).astype(jnp.bfloat16)
        real, imag = weight_ref[odd, 0], weight_ref[odd, 1]
        for sample in range(S):
            for side, halves in enumerate(((real, imag), (-imag, real))):
                for target, block in enumerate(halves):
                    row = side * S * C + sample * C
                    lane = target * S * C + sample * C
                    full_ref[odd, row : row + C, lane : lane + C] = block
        out_ref[odd] = jnp.dot(
            value, full_ref[odd], preferred_element_type=jnp.float32
        ).astype(out_ref.dtype)


def apply_filter(coefficients, filter_weight):
    chunks = coefficients.shape[0]
    degrees = filter_weight.shape[0]
    return pl.pallas_call(
        filter_kernel,
        grid=(degrees // 2,),
        out_shape=jax.ShapeDtypeStruct((degrees, chunks * ROWS, WIDE), jnp.bfloat16),
        in_specs=[
            pl.BlockSpec((chunks, 2 * ROWS, WIDE), lambda i: (0, i, 0)),
            pl.BlockSpec((2, 2, C, C), lambda i: (i, 0, 0, 0)),
        ],
        out_specs=pl.BlockSpec((2, chunks * ROWS, WIDE), lambda i: (i, 0, 0)),
        scratch_shapes=[pltpu.VMEM((2, WIDE, WIDE), jnp.bfloat16)],
        compiler_params=pltpu.CompilerParams(vmem_limit_bytes=24 * 1024 * 1024),
    )(coefficients, filter_weight)


def body(grid_field, norm_gain, filter_weight):
    count = lax.axis_size("lat")
    band, longitudes, columns = grid_field.shape
    fits = scratch_bytes(scratch_of(count, band, longitudes)) < VMEM_CAP - 6 * 1024 * 1024
    if count % PLANE or not fits:
        return plain_body(grid_field, norm_gain, filter_weight)
    coefficients = coefficients_of(grid_field, norm_gain, count)
    return apply_filter(coefficients, filter_weight)


def solution(mesh):
    in_specs = (P("lat", None, "parts"), P("parts"), P("lat", None, None, "parts"))
    out_specs = P("lat", None, "parts")
    return jax.shard_map(body, mesh=mesh, in_specs=in_specs, out_specs=out_specs, check_vma=False)
```

```python
import functools
import math

import jax
import jax.numpy as jnp
import numpy as np
from jax import lax
from jax.experimental import pallas as pl
from jax.experimental.pallas import tpu as pltpu
from jax.sharding import PartitionSpec as P

C = 64
S = 2
DEG_DEV = 22
ORDER_PAD = 24
BLOCK = 16
LANES = 128


def round_up(value, step):
    return -(-value // step) * step


def legendre_kernel(
    orders_ref, cosine_ref, weights_ref, mant_ref, exp_ref, out_ref, prev_ref, early_ref, grow_ref, rows_ref
):
    block = pl.program_id(0)
    width = cosine_ref.shape[1]
    kept_width = out_ref.shape[2]

    @pl.when(block == 0)
    def _():
        prev_ref[...] = jnp.zeros_like(prev_ref)
        early_ref[...] = jnp.zeros_like(early_ref)
        grow_ref[...] = jnp.zeros_like(grow_ref)

    orders = orders_ref[...]
    narrow = orders[:, :LANES]
    order_sq = narrow * narrow
    cosine = cosine_ref[...]
    weights = weights_ref[...]
    limit = 2.0**64
    shrink = 2.0 ** (-64)
    previous, earlier, exponent = prev_ref[...], early_ref[...], grow_ref[...]
    first = (block * BLOCK).astype(jnp.float32)

    def widen(value):
        return jnp.concatenate([value] * (width // LANES), axis=1)

    for step in range(BLOCK):
        degree = first + float(step)
        upper = jnp.sqrt(
            (4.0 * degree * degree - 1.0) / jnp.maximum(degree * degree - order_sq, 1.0)
        )
        below = degree - 1.0
        lower = jnp.sqrt(
            jnp.maximum(below * below - order_sq, 0.0)
            / jnp.maximum(jnp.full_like(order_sq, 4.0 * below * below - 1.0), 1.0)
        )
        recurred = widen(upper) * (cosine * previous - widen(lower) * earlier)
        at_start = orders == degree
        current = jnp.where(at_start, mant_ref[...], jnp.where(orders < degree, recurred, 0.0))
        exponent = jnp.where(at_start, exp_ref[...], exponent)
        value = weights * (current * jnp.exp2(exponent))
        for lane in range(width // LANES):
            rows_ref[lane, step * ORDER_PAD : (step + 1) * ORDER_PAD, :] = value[
                :, lane * LANES : (lane + 1) * LANES
            ]
        large = jnp.abs(current) > limit
        earlier = jnp.where(large, previous * shrink, previous)
        previous = jnp.where(large, current * shrink, current)
        exponent = jnp.where(large, exponent + 64.0, exponent)

    prev_ref[...] = previous
    early_ref[...] = earlier
    grow_ref[...] = exponent
    for order in range(DEG_DEV):
        for lane in range(0, width, LANES):
            cut = min(LANES, kept_width - lane)
            piece = rows_ref[lane // LANES, pl.ds(order, BLOCK, stride=ORDER_PAD), :]
            out_ref[order, :, lane : lane + cut] = piece[:, :cut].astype(out_ref.dtype)


def legendre_table(colatitude, first_order, degrees, weight_scale):
    rows = colatitude.shape[0]
    width = round_up(rows, LANES)
    colat = jnp.concatenate([colatitude, jnp.full((width - rows,), 0.5 * math.pi, jnp.float32)])
    orders = (first_order + jnp.arange(ORDER_PAD, dtype=jnp.int32)).astype(jnp.float32)
    sine_rows = jnp.sin(colat)
    log_start = 0.5 * jnp.log((2.0 * orders + 1.0) / (4.0 * math.pi)) + 0.5 * (
        lax.lgamma(orders + 0.5) - lax.lgamma(orders + 1.0) - 0.5 * math.log(math.pi)
    )
    log_diag = log_start[:, None] + orders[:, None] * jnp.log(sine_rows)[None, :]
    start_exp = 64.0 * jnp.floor(log_diag / (64.0 * math.log(2.0)))
    start_mant = jnp.exp(log_diag - start_exp * math.log(2.0))
    state = (ORDER_PAD, width)
    whole = pl.BlockSpec(state, lambda i: (0, 0))
    line = pl.BlockSpec((1, width), lambda i: (0, 0))
    return pl.pallas_call(
        legendre_kernel,
        grid=(degrees // BLOCK,),
        out_shape=jax.ShapeDtypeStruct((DEG_DEV, degrees, rows), jnp.bfloat16),
        in_specs=[whole, line, line, whole, whole],
        out_specs=pl.BlockSpec((DEG_DEV, BLOCK, rows), lambda i: (0, i, 0)),
        scratch_shapes=[
            pltpu.VMEM(state, jnp.float32),
            pltpu.VMEM(state, jnp.float32),
            pltpu.VMEM(state, jnp.float32),
            pltpu.VMEM((width // LANES, BLOCK * ORDER_PAD, LANES), jnp.float32),
        ],
        cost_estimate=pl.CostEstimate(
            flops=degrees * ORDER_PAD * width * 2000,
            bytes_accessed=DEG_DEV * degrees * rows * 2,
            transcendentals=degrees * ORDER_PAD * width,
        ),
        compiler_params=pltpu.CompilerParams(vmem_limit_bytes=24 * 1024 * 1024),
    )(
        jnp.broadcast_to(orders[:, None], state),
        jnp.cos(colat)[None, :],
        (weight_scale * sine_rows)[None, :],
        start_mant,
        start_exp,
    )


def expand_filter(filter_weight):
    real_part = filter_weight[:, 0]
    imag_part = filter_weight[:, 1]
    from_real = jnp.stack([real_part, imag_part], axis=1)
    from_imag = jnp.stack([-imag_part, real_part], axis=1)
    mixing = jnp.stack([from_real, from_imag], axis=1)
    same = jnp.eye(S, dtype=filter_weight.dtype)
    full = mixing.transpose(0, 1, 3, 2, 4)[:, :, None, :, :, None, :] * same[None, None, :, None, None, :, None]
    return full.reshape(filter_weight.shape[0], 2 * S * C, 2 * S * C)


def mix_kernel(sin_ref, cos_ref, weight_ref, out_ref, rows_ref):
    sources, degrees, orders, half = cos_ref.shape
    for degree in range(degrees):
        for source in range(sources):
            rows = slice(source * orders, (source + 1) * orders)
            rows_ref[degree, rows, :half] = cos_ref[source, degree].astype(jnp.float32)
            rows_ref[degree, rows, half:] = sin_ref[source, degree].astype(jnp.float32)
        out_ref[degree] = jnp.dot(
            rows_ref[degree].astype(jnp.bfloat16),
            weight_ref[degree],
            preferred_element_type=jnp.float32,
        ).astype(out_ref.dtype)


def mix(coef_sin, coef_cos, weights):
    sources, degrees, orders, half = coef_cos.shape
    wide = weights.shape[2]
    step = 2
    piece = pl.BlockSpec((sources, step, orders, half), lambda i: (0, i, 0, 0))
    return pl.pallas_call(
        mix_kernel,
        grid=(degrees // step,),
        out_shape=jax.ShapeDtypeStruct((degrees, sources * orders, wide), jnp.bfloat16),
        in_specs=[piece, piece, pl.BlockSpec((step, 2 * half, wide), lambda i: (i, 0, 0))],
        out_specs=pl.BlockSpec((step, sources * orders, wide), lambda i: (i, 0, 0)),
        scratch_shapes=[pltpu.VMEM((step, sources * orders, 2 * half), jnp.float32)],
        compiler_params=pltpu.CompilerParams(vmem_limit_bytes=24 * 1024 * 1024),
    )(coef_sin, coef_cos, weights)


def fourier_matrix(orders, longitudes):
    phases = (np.arange(orders)[:, None] * np.arange(longitudes)[None, :]) % longitudes
    angles = 2.0 * np.pi * phases / longitudes
    return np.stack([np.cos(angles), -np.sin(angles)]).astype(np.float32)


def plain_body(grid_field, norm_gain, filter_weight):
    device_index = lax.axis_index("lat")
    lat_count = lax.axis_size("lat")
    band_rows, longitudes, columns = grid_field.shape
    total_lat = band_rows * lat_count
    order_count = DEG_DEV * lat_count
    all_rows = jnp.arange(total_lat, dtype=jnp.int32)
    colat_all = math.pi * (all_rows.astype(jnp.float32) + 0.5) / total_lat
    sine_all = jnp.sin(colat_all)
    own_rows = device_index * band_rows + jnp.arange(band_rows, dtype=jnp.int32)
    sine_own = jnp.sin(math.pi * (own_rows.astype(jnp.float32) + 0.5) / total_lat)

    first = jnp.einsum("j,jnx->x", sine_own, grid_field, precision=lax.Precision.HIGHEST)
    second = jnp.einsum(
        "j,jnx->x", sine_own, grid_field * grid_field, precision=lax.Precision.HIGHEST
    )
    band_mean = first / (longitudes * jnp.sum(sine_own))
    denominator_rows = jnp.float32(longitudes)
    cos_table, sin_table = fourier_matrix(order_count, longitudes)

    def transform(table):
        return jnp.einsum(
            "mn,jnx->mjx", jnp.asarray(table), grid_field, precision=lax.Precision.HIGH
        )

    def to_orders(raw):
        return lax.all_to_all(
            raw.astype(jnp.bfloat16), "lat", split_axis=0, concat_axis=1, tiled=True
        )

    def to_degrees(sums):
        return lax.all_to_all(
            sums, "lat", split_axis=0, concat_axis=0
        )

    received_sin = to_orders(transform(sin_table))
    constant = jnp.arange(order_count) == 0
    shift = jnp.where(constant[:, None, None], denominator_rows * band_mean, 0.0)
    received_cos = to_orders(transform(cos_table) - shift)

    weight_scale = math.pi**1.5 / math.sqrt(total_lat * longitudes)
    legendre = legendre_table(colat_all, device_index * DEG_DEV, order_count, weight_scale)

    def analyse(received):
        return jnp.einsum("mlj,mjx->mlx", legendre, received, preferred_element_type=jnp.float32)

    def by_degree(sums):
        ordered = sums.astype(jnp.bfloat16).transpose(1, 0, 2)
        return ordered.reshape(lat_count, DEG_DEV, DEG_DEV, columns)

    sums_sin = by_degree(analyse(received_sin))
    moments, sums_sin = lax.optimization_barrier(
        (jnp.stack([first, second, band_mean]), sums_sin)
    )
    gathered, sums_sin = lax.optimization_barrier((lax.all_gather(moments, "lat"), sums_sin))
    denominator = longitudes * jnp.sum(sine_all)
    average = jnp.sum(gathered[:, 0], axis=0) / denominator
    mean_square = jnp.sum(gathered[:, 1], axis=0) / denominator
    spread = jnp.sqrt(mean_square - average * average + 1e-05)
    factor = jnp.tile(norm_gain, S) / spread
    coef_sin = to_degrees(sums_sin)
    band_sums = jnp.sum(
        legendre[0].astype(jnp.float32).reshape(order_count, lat_count, band_rows), axis=2
    )
    level = jnp.dot(
        band_sums,
        denominator_rows * (gathered[:, 2] - average),
        precision=lax.Precision.HIGHEST,
    )
    here = (device_index == 0) & (jnp.arange(DEG_DEV) == 0)
    coef_cos = to_degrees(
        by_degree(analyse(received_cos) + jnp.where(here[:, None, None], level[None], 0.0))
    )

    expanded = expand_filter(filter_weight)
    expanded = (expanded * jnp.tile(factor, 2)[None, :, None]).astype(jnp.bfloat16)

    return mix(coef_sin, coef_cos, expanded)


MESH = pl.DeviceIdType.MESH
ROWS = 8
WIDE = 2 * LANES
CHUNKS = 3
PLANE = 4
PLANE_CHUNKS = PLANE * CHUNKS - 1
VMEM_CAP = 60 * 1024 * 1024


def owns_last(device):
    return device % PLANE != 1


def owner_chunk(device, slot, count):
    plane, inner = count // PLANE - 1 - device // PLANE, device % PLANE
    first = 1 // (plane + inner + 1)
    at = slot + first * (CHUNKS - 1 - 2 * slot)
    return PLANE_CHUNKS * plane + PLANE * at + inner - (at // (CHUNKS - 1)) * ((inner + 2) // PLANE)


def transform_tables(count, longitudes):
    table = np.zeros((CHUNKS, 2, count, ROWS, longitudes), np.float64)
    for slot in range(CHUNKS):
        for device in range(count):
            if slot == CHUNKS - 1 and not owns_last(device):
                continue
            orders = owner_chunk(device, slot, count) * ROWS + np.arange(ROWS)
            phases = (orders[:, None] * np.arange(longitudes)[None, :]) % longitudes
            angles = 2.0 * np.pi * phases / longitudes
            table[slot, 0, device] = np.cos(angles)
            table[slot, 1, device] = -np.sin(angles)
    table = table.reshape(CHUNKS, 2 * count * ROWS, longitudes).astype(np.float32)
    high = table.astype(jnp.bfloat16)
    low = (table - high.astype(np.float32)).astype(jnp.bfloat16)
    return high, low


def angle_tables(count, band, places):
    colat = np.pi * (np.arange(count * band) + 0.5) / (count * band)
    by_place = np.full((count, places), 0.5 * np.pi)
    valid = np.zeros((count, places))
    for device in range(count):
        rows = colat[device * band : (device + 1) * band]
        by_place[device, :band] = rows if device < count // 2 else rows[::-1]
        valid[device, :band] = 1.0
    sine_places = np.sin(by_place) * valid
    north = by_place[: count // 2].reshape(1, -1)
    weight = sine_places[: count // 2].reshape(1, -1)
    width = round_up(north.shape[1], LANES)
    north = np.pad(north, ((0, 0), (0, width - north.shape[1])), constant_values=0.5 * np.pi)
    weight = np.pad(weight, ((0, 0), (0, width - weight.shape[1])))
    return (
        sine_places.reshape(-1).astype(np.float32),
        np.cos(north).astype(np.float32),
        weight,
        np.log(np.sin(north)).astype(np.float32),
        float(np.sum(np.sin(colat))),
    )


def log_starts(order_count):
    values = [
        0.5 * math.log((2.0 * m + 1.0) / (4.0 * math.pi))
        + 0.5 * (math.lgamma(m + 0.5) - math.lgamma(m + 1.0) - 0.5 * math.log(math.pi))
        for m in range(order_count)
    ]
    return np.asarray(values, np.float32)[:, None]


def spectral_kernel(
    sizes,
    field_ref,
    gain_ref,
    high_ref,
    low_ref,
    sine_ref,
    cosine_ref,
    weight_ref,
    logsine_ref,
    start_ref,
    out_ref,
    high,
    low,
    stage,
    field_high,
    field_low,
    turned,
    outgoing,
    landed,
    moments,
    moments_all,
    scales,
    table,
    prev_ref,
    early_ref,
    grow_ref,
    mant_ref,
    exp_ref,
    lines,
    sums,
    sums_out,
    blank,
    table_sem,
    stage_sem,
    moment_send,
    moment_recv,
    send_sem,
    recv_sem,
    local_sem,
    send_two,
    recv_two,
    blank_sem,
):
    count, band, longitudes, total_sine = sizes
    me = lax.axis_index("lat")
    part = lax.axis_index("parts")
    half = count // 2
    south = me // half
    slot_of_me = me + south * (half + count - 1 - 2 * me)
    groups = outgoing.shape[0] // CHUNKS
    places = groups * ROWS
    degrees = table.shape[1]
    kept = table.shape[2]
    width = cosine_ref.shape[1]
    block_rows = DEG_DEV * ROWS
    zero_owner = count - PLANE
    has_last = owns_last(me)

    def has_chunk(slot, device):
        return (slot < CHUNKS - 1) | owns_last(device)

    def table_copies(slot):
        return (
            pltpu.make_async_copy(high_ref.at[slot], high.at[slot], table_sem.at[0, slot]),
            pltpu.make_async_copy(low_ref.at[slot], low.at[slot], table_sem.at[1, slot]),
        )

    def row_copy(place):
        row = place + south * (band - 1 - 2 * place)
        at = place % ROWS
        return pltpu.make_async_copy(field_ref.at[row], stage.at[at], stage_sem.at[at])

    for place in range(2):
        row_copy(place).start()
    for copy in table_copies(0):
        copy.start()
    for place in range(2, ROWS):
        row_copy(place).start()
    for slot in range(1, CHUNKS):
        for copy in table_copies(slot):
            copy.start()

    barrier = pltpu.get_barrier_semaphore()

    @pl.loop(1, count)
    def _(step):
        pl.semaphore_signal(
            barrier, inc=1, device_id=(part, (me + step) % count), device_id_type=MESH
        )

    moments[...] = jnp.zeros_like(moments)
    for place in range(band, places):
        lanes = slice((place % 2) * LANES, (place % 2 + 1) * LANES)
        field_high[place // 2, :, lanes] = jnp.zeros((longitudes, LANES), jnp.bfloat16)
        field_low[place // 2, :, lanes] = jnp.zeros((longitudes, LANES), jnp.bfloat16)

    piece = longitudes // 6

    def take_row(place, lanes):
        row_copy(place).wait()
        at = place % ROWS
        pair = place // 2
        total = jnp.zeros((ROWS, LANES), jnp.float32)
        square = jnp.zeros((ROWS, LANES), jnp.float32)
        for first in range(0, longitudes, piece):
            value = stage[at, first : first + piece, :]
            top = value.astype(jnp.bfloat16)
            field_high[pair, first : first + piece, lanes] = top
            field_low[pair, first : first + piece, lanes] = (
                value - top.astype(jnp.float32)
            ).astype(jnp.bfloat16)
            total += jnp.sum(value.reshape(-1, ROWS, LANES), axis=0)
            square += jnp.sum((value * value).reshape(-1, ROWS, LANES), axis=0)
        sine = sine_ref[me * places + place]
        moments[:ROWS] += sine * total
        moments[ROWS:] += sine * square

        @pl.when(place + ROWS < band)
        def _():
            row_copy(place + ROWS).start()

    def take_group(group):
        @pl.loop(0, ROWS // 2)
        def _(pair):
            place = group * ROWS + 2 * pair
            take_row(place, slice(0, LANES))

            @pl.when(place + 1 < band)
            def _():
                take_row(place + 1, slice(LANES, WIDE))

    take_group(0)
    pl.semaphore_wait(barrier, count - 1)

    def blank_copy(chunk, lines_off):
        rows = pl.ds(0, lines_off * ROWS)
        return pltpu.make_async_copy(
            blank.at[rows], out_ref.at[chunk, rows], blank_sem.at[chunk]
        )

    def moment_copy(device):
        return pltpu.make_async_remote_copy(
            moments,
            moments_all.at[me],
            moment_send,
            moment_recv,
            device_id=(part, device),
            device_id_type=MESH,
        )

    def order_copy(slot, group, device):
        step = slot * groups + group
        rows = pl.ds(pl.multiple_of(device * ROWS * ROWS, ROWS * ROWS), ROWS * ROWS)
        return pltpu.make_async_remote_copy(
            outgoing.at[step, rows],
            landed.at[slot, slot_of_me, group],
            send_sem.at[step],
            recv_sem.at[slot],
            device_id=(part, device),
            device_id_type=MESH,
        )

    def own_copy(slot, group):
        step = slot * groups + group
        rows = pl.ds(pl.multiple_of(me * ROWS * ROWS, ROWS * ROWS), ROWS * ROWS)
        return pltpu.make_async_copy(
            outgoing.at[step, rows], landed.at[slot, slot_of_me, group], local_sem.at[step]
        )

    def transform(step):
        slot, group = step // groups, step % groups

        @pl.when((step > 0) & (slot == 0))
        def _():
            take_group(group)

        @pl.when(step == groups - 1)
        def _():
            moments_all[me] = moments[...]

            @pl.loop(1, count)
            def _(ahead):
                moment_copy((me + ahead) % count).start()

        @pl.when(group == 0)
        def _():
            for copy in table_copies(slot):
                copy.wait()

        @pl.loop(0, ROWS // 2)
        def _(pair):
            at = group * (ROWS // 2) + pair
            product = jnp.dot(high[slot], field_high[at], preferred_element_type=jnp.float32)
            product += jnp.dot(high[slot], field_low[at], preferred_element_type=jnp.float32)
            product += jnp.dot(low[slot], field_high[at], preferred_element_type=jnp.float32)
            lines_of = count * ROWS
            for side in range(2):
                for row in range(2):
                    turned[side, pl.ds(2 * pair + row, lines_of, stride=ROWS), :] = product[
                        side * lines_of : (side + 1) * lines_of, row * LANES : (row + 1) * LANES
                    ]

        @pl.when(slot == CHUNKS - 1)
        def _():
            at = zero_owner * ROWS * ROWS
            turned[0, at : at + ROWS, :] -= scales[1:2, :LANES]

        @pl.loop(0, count)
        def _(ahead):
            device = (me + 1 + ahead) % count
            rows = pl.ds(pl.multiple_of(device * ROWS * ROWS, ROWS * ROWS), ROWS * ROWS)
            outgoing[step, rows, :] = jnp.concatenate(
                [turned[0, rows, :], turned[1, rows, :]], axis=1
            ).astype(jnp.bfloat16)

            @pl.when((device != me) & has_chunk(slot, device))
            def _():
                order_copy(slot, group, device).start()

            @pl.when((device == me) & has_chunk(slot, device))
            def _():
                own_copy(slot, group).start()

    pl.loop(0, (CHUNKS - 1) * groups)(transform)

    pltpu.make_async_copy(
        moments_all.at[pl.ds(0, count - 1)],
        moments_all.at[pl.ds(0, count - 1)],
        moment_recv,
    ).wait()
    gathered = jnp.sum(moments_all[...], axis=0)
    first = jnp.sum(gathered[:ROWS], axis=0, keepdims=True) / (longitudes * total_sine)
    second = jnp.sum(gathered[ROWS:], axis=0, keepdims=True) / (longitudes * total_sine)
    spread = jnp.sqrt(second - first * first + 1e-05)
    gain = gain_ref[...]
    factor = jnp.concatenate([gain] * S, axis=1) / spread
    scales[:1] = jnp.concatenate([factor, factor], axis=1)
    scales[1:2] = jnp.concatenate([longitudes * first, jnp.zeros_like(first)], axis=1)

    blank[...] = jnp.zeros_like(blank)

    @pl.loop(0, out_ref.shape[0])
    def _(chunk):
        low_line = chunk * ROWS - me * DEG_DEV

        @pl.when(low_line >= DEG_DEV)
        def _():
            pltpu.make_async_copy(blank, out_ref.at[chunk], recv_two.at[chunk]).start()

        for lines_off in range(2, DEG_DEV, 2):

            @pl.when(low_line == lines_off)
            def _():
                blank_copy(chunk, lines_off).start()

    chunk_of = [owner_chunk(me, slot, count) for slot in range(CHUNKS)]
    lines_in = lax.broadcasted_iota(jnp.int32, (ROWS, width), 0)
    orders = jnp.concatenate(
        [(chunk * ROWS + lines_in).astype(jnp.float32) for chunk in chunk_of], axis=0
    )
    start = jnp.concatenate(
        [start_ref[pl.ds(pl.multiple_of(chunk * ROWS, ROWS), ROWS), :] for chunk in chunk_of], axis=0
    )
    start = jnp.broadcast_to(start, (CHUNKS * ROWS, width))

    def widen(value):
        return jnp.concatenate([value] * (width // LANES), axis=1)

    log_diag = start + orders * logsine_ref[...]
    start_exp = 64.0 * jnp.floor(log_diag / (64.0 * math.log(2.0)))
    exp_ref[...] = start_exp
    mant_ref[...] = jnp.exp(log_diag - start_exp * math.log(2.0))
    prev_ref[...] = jnp.zeros_like(prev_ref)
    early_ref[...] = jnp.zeros_like(early_ref)
    grow_ref[...] = jnp.zeros_like(grow_ref)
    order_lines = CHUNKS * ROWS

    @pl.loop(0, degrees // BLOCK)
    def _(block):
        narrow = orders[:, :LANES]
        order_sq = narrow * narrow
        cosine = cosine_ref[...]
        weights = weight_ref[...]
        limit = 2.0**64
        shrink = 2.0 ** (-64)
        previous, earlier, exponent = prev_ref[...], early_ref[...], grow_ref[...]
        first = (block * BLOCK).astype(jnp.float32)
        for step in range(BLOCK):
            degree = first + float(step)
            upper = jnp.sqrt(
                (4.0 * degree * degree - 1.0) / jnp.maximum(degree * degree - order_sq, 1.0)
            )
            below = degree - 1.0
            lower = jnp.sqrt(
                jnp.maximum(below * below - order_sq, 0.0)
                / jnp.maximum(jnp.full_like(order_sq, 4.0 * below * below - 1.0), 1.0)
            )
            recurred = widen(upper) * (cosine * previous - widen(lower) * earlier)
            at_start = orders == degree
            current = jnp.where(at_start, mant_ref[...], jnp.where(orders < degree, recurred, 0.0))
            exponent = jnp.where(at_start, exp_ref[...], exponent)
            value = weights * (current * jnp.exp2(exponent))
            for lane in range(width // LANES):
                lines[lane, step * order_lines : (step + 1) * order_lines, :] = value[
                    :, lane * LANES : (lane + 1) * LANES
                ]
            large = jnp.abs(current) > limit
            earlier = jnp.where(large, previous * shrink, previous)
            previous = jnp.where(large, current * shrink, current)
            exponent = jnp.where(large, exponent + 64.0, exponent)
        prev_ref[...] = previous
        early_ref[...] = earlier
        grow_ref[...] = exponent
        rows = pl.ds(pl.multiple_of(block * BLOCK, BLOCK), BLOCK)
        for order in range(order_lines):
            for lane in range(0, width, LANES):
                cut = min(LANES, kept - lane)
                part_of = lines[lane // LANES, pl.ds(order, BLOCK, stride=order_lines), :]
                table[order, rows, lane : lane + cut] = part_of[:, :cut].astype(table.dtype)

    def rows_from(device, lines_off):
        base = pl.multiple_of(device * block_rows + lines_off * ROWS, 2 * ROWS)
        return pl.ds(base, block_rows - lines_off * ROWS)

    def degree_copy(slot, device, lines_off=0):
        chunk = owner_chunk(me, slot, count)
        return pltpu.make_async_remote_copy(
            sums_out.at[slot, rows_from(device, lines_off)],
            out_ref.at[chunk, rows_from(0, lines_off)],
            send_two.at[slot, device],
            recv_two.at[chunk],
            device_id=(part, device),
            device_id_type=MESH,
        )

    def own_degrees(slot, lines_off=0):
        chunk = owner_chunk(me, slot, count)
        return pltpu.make_async_copy(
            sums_out.at[slot, rows_from(me, lines_off)],
            out_ref.at[chunk, rows_from(0, lines_off)],
            recv_two.at[chunk],
        )

    def diagonal(slot, remote, local):
        first_line = owner_chunk(me, slot, count) * ROWS
        device = first_line // DEG_DEV
        for lines_off in range(2, DEG_DEV, 2):
            hit = first_line - device * DEG_DEV == lines_off

            @pl.when(hit & (device != me))
            def _():
                remote(slot, device, lines_off)

            if local is not None:

                @pl.when(hit & (device == me))
                def _():
                    local(slot, lines_off)

    degree_line = lax.broadcasted_iota(jnp.int32, (degrees, 1), 0)
    sign_even = jnp.where(degree_line % 2 == 0, 1.0, -1.0).astype(jnp.float32)

    def analyse(slot):
        pltpu.make_async_copy(
            landed.at[slot, pl.ds(0, count - 1)],
            landed.at[slot, pl.ds(0, count - 1)],
            recv_sem.at[slot],
        ).wait()
        for group in range(groups):
            own_copy(slot, group).wait()

        @pl.loop(0, ROWS // 2)
        def _(pair):
            rows = pl.ds(pl.multiple_of(pair * 2 * ROWS, 2 * ROWS), 2 * ROWS)
            both = landed[slot, :, :, rows, :].astype(jnp.float32)
            both = both.reshape(count * groups, 2, ROWS, WIDE)
            for odd in range(2):
                rhs = both[:, odd].reshape(count * places, WIDE).astype(jnp.bfloat16)
                lhs = table[slot * ROWS + 2 * pair + odd]
                north = jnp.dot(lhs, rhs[:kept], preferred_element_type=jnp.float32)
                mirror = jnp.dot(lhs, rhs[kept:], preferred_element_type=jnp.float32)
                sign = sign_even if odd == 0 else -sign_even
                result = (north + sign * mirror) * scales[:1]
                for lane in range(2):
                    sums[lane, pl.ds(2 * pair + odd, degrees, stride=ROWS), :] = result[
                        :, lane * LANES : (lane + 1) * LANES
                    ]

        @pl.loop(0, count)
        def _(ahead):
            device = (me + 1 + ahead) % count
            rows = pl.ds(pl.multiple_of(device * block_rows, block_rows), block_rows)
            sums_out[slot, rows, :] = jnp.concatenate(
                [sums[0, rows, :], sums[1, rows, :]], axis=1
            ).astype(jnp.bfloat16)
            wanted = owner_chunk(me, slot, count) * ROWS <= device * DEG_DEV

            @pl.when(wanted & (device != me))
            def _():
                degree_copy(slot, device).start()

            @pl.when(wanted & (device == me))
            def _():
                own_degrees(slot).start()

        diagonal(
            slot,
            lambda *where: degree_copy(*where).start(),
            lambda *where: own_degrees(*where).start(),
        )

    @pl.loop(0, CHUNKS)
    def _(slot):
        @pl.when((slot < CHUNKS - 1) | has_last)
        def _():
            analyse(slot)

        @pl.when(slot == 0)
        def _():
            pl.loop((CHUNKS - 1) * groups, CHUNKS * groups)(transform)

    pltpu.make_async_copy(
        moments_all.at[pl.ds(0, count - 1)], moments_all.at[pl.ds(0, count - 1)], moment_send
    ).wait()

    def wait_orders(step, devices):
        rows = pl.ds(0, devices * ROWS * ROWS)
        pltpu.make_async_copy(
            outgoing.at[step, rows], outgoing.at[step, rows], send_sem.at[step]
        ).wait()

    @pl.loop(0, (CHUNKS - 1) * groups)
    def _(step):
        wait_orders(step, count - 1)

    last_owners = count - count // PLANE

    @pl.loop((CHUNKS - 1) * groups, CHUNKS * groups)
    def _(step):
        @pl.when(has_last)
        def _():
            wait_orders(step, last_owners - 1)

        @pl.when(jnp.logical_not(has_last))
        def _():
            wait_orders(step, last_owners)

    @pl.loop(0, CHUNKS)
    def _(slot):
        @pl.when(has_chunk(slot, me))
        def _():
            @pl.loop(0, count)
            def _(device):
                wanted = owner_chunk(me, slot, count) * ROWS <= device * DEG_DEV

                @pl.when(wanted & (device != me))
                def _():
                    degree_copy(slot, device).wait_send()

            diagonal(slot, lambda *where: degree_copy(*where).wait_send(), None)

    @pl.loop(0, out_ref.shape[0])
    def _(chunk):
        low_line = chunk * ROWS - me * DEG_DEV

        @pl.when((low_line <= 0) | (low_line >= DEG_DEV))
        def _():
            pltpu.make_async_copy(blank, out_ref.at[chunk], recv_two.at[chunk]).wait()

        for lines_off in range(2, DEG_DEV, 2):

            @pl.when(low_line == lines_off)
            def _():
                blank_copy(chunk, lines_off).wait()
                rows = rows_from(0, lines_off)
                pltpu.make_async_copy(
                    blank.at[rows], out_ref.at[chunk, rows], recv_two.at[chunk]
                ).wait()


def scratch_of(count, band, longitudes):
    groups = -(-band // ROWS)
    places = groups * ROWS
    degrees = DEG_DEV * count
    lines_of = count * ROWS
    kept = count // 2 * places
    width = round_up(kept, LANES)
    order_lines = CHUNKS * ROWS
    state = (order_lines, width)
    bf16, f32 = jnp.bfloat16, jnp.float32
    return [
        ((CHUNKS, 2 * lines_of, longitudes), bf16),
        ((CHUNKS, 2 * lines_of, longitudes), bf16),
        ((ROWS, longitudes, LANES), f32),
        ((places // 2, longitudes, WIDE), bf16),
        ((places // 2, longitudes, WIDE), bf16),
        ((2, lines_of * ROWS, LANES), f32),
        ((CHUNKS * groups, lines_of * ROWS, WIDE), bf16),
        ((CHUNKS, count, groups, ROWS * ROWS, WIDE), bf16),
        ((2 * ROWS, LANES), f32),
        ((count, 2 * ROWS, LANES), f32),
        ((ROWS, WIDE), f32),
        ((order_lines, degrees, kept), bf16),
        (state, f32),
        (state, f32),
        (state, f32),
        (state, f32),
        (state, f32),
        ((width // LANES, BLOCK * order_lines, LANES), f32),
        ((2, degrees * ROWS, LANES), f32),
        ((CHUNKS, degrees * ROWS, WIDE), bf16),
        ((DEG_DEV * ROWS, WIDE), bf16),
    ]


def scratch_bytes(shapes):
    total = 0
    for shape, dtype in shapes:
        size = math.prod(shape[:-1]) * round_up(shape[-1], LANES)
        total += size * jnp.dtype(dtype).itemsize
    return total


def coefficients_of(grid_field, norm_gain, count):
    band, longitudes, columns = grid_field.shape
    groups = -(-band // ROWS)
    places = groups * ROWS
    order_count = DEG_DEV * count
    high, low = transform_tables(count, longitudes)
    sine, cosine, weight, logsine, total_sine = angle_tables(count, band, places)
    weight_scale = math.pi**1.5 / math.sqrt(count * band * longitudes)
    shapes = scratch_of(count, band, longitudes)
    dma = pltpu.SemaphoreType.DMA
    vmem = pl.BlockSpec(memory_space=pltpu.VMEM)
    anywhere = pl.BlockSpec(memory_space=pl.ANY)
    return pl.pallas_call(
        functools.partial(spectral_kernel, (count, band, longitudes, total_sine)),
        out_shape=jax.ShapeDtypeStruct((order_count // ROWS, DEG_DEV * ROWS, WIDE), jnp.bfloat16),
        in_specs=[
            anywhere,
            vmem,
            anywhere,
            anywhere,
            pl.BlockSpec(memory_space=pltpu.SMEM),
            vmem,
            vmem,
            vmem,
            vmem,
        ],
        out_specs=anywhere,
        scratch_shapes=[pltpu.VMEM(shape, dtype) for shape, dtype in shapes]
        + [
            dma((2, CHUNKS)),
            dma((ROWS,)),
            dma,
            dma,
            dma((CHUNKS * groups,)),
            dma((CHUNKS,)),
            dma((CHUNKS * groups,)),
            dma((CHUNKS, count)),
            dma((order_count // ROWS,)),
            dma((order_count // ROWS,)),
        ],
        cost_estimate=pl.CostEstimate(
            flops=20 * 10**9, bytes_accessed=40 * 10**6, transcendentals=10**6
        ),
        compiler_params=pltpu.CompilerParams(
            collective_id=0, has_side_effects=True, vmem_limit_bytes=VMEM_CAP
        ),
    )(
        grid_field,
        norm_gain[None, :],
        jnp.asarray(high),
        jnp.asarray(low),
        jnp.asarray(sine),
        jnp.asarray(cosine),
        jnp.asarray((weight * weight_scale).astype(np.float32)),
        jnp.asarray(logsine),
        jnp.asarray(log_starts(order_count)),
    )


def filter_kernel(coef_ref, weight_ref, out_ref, coefs, outs, full_ref, in_sem, out_sem):
    pairs = coefs.shape[0]
    chunks = coefs.shape[1]
    orders = chunks * ROWS

    def fetch(pair):
        rows = pl.ds(pl.multiple_of(pair * 2 * ROWS, 2 * ROWS), 2 * ROWS)
        return pltpu.make_async_copy(coef_ref.at[:, rows, :], coefs.at[pair], in_sem.at[pair])

    def store(pair):
        return pltpu.make_async_copy(
            outs.at[pair], out_ref.at[pl.ds(2 * pair, 2)], out_sem.at[pair]
        )

    for pair in range(pairs):
        fetch(pair).start()
    full_ref[...] = jnp.zeros_like(full_ref)

    @pl.loop(0, pairs)
    def _(pair):
        for odd in range(2):
            real, imag = weight_ref[2 * pair + odd, 0], weight_ref[2 * pair + odd, 1]
            for sample in range(S):
                for side, halves in enumerate(((real, imag), (-imag, real))):
                    for target, block in enumerate(halves):
                        row = side * S * C + sample * C
                        lane = target * S * C + sample * C
                        full_ref[odd, row : row + C, lane : lane + C] = block
        fetch(pair).wait()
        both = coefs[pair].astype(jnp.float32).reshape(chunks, 2, ROWS, WIDE)
        for odd in range(2):
            value = both[:, odd].reshape(orders, WIDE).astype(jnp.bfloat16)
            outs[pair, odd] = jnp.dot(
                value, full_ref[odd], preferred_element_type=jnp.float32
            ).astype(outs.dtype)
        store(pair).start()

    @pl.loop(0, pairs)
    def _(pair):
        store(pair).wait()


def apply_filter(coefficients, filter_weight):
    chunks = coefficients.shape[0]
    degrees = filter_weight.shape[0]
    pairs = degrees // 2
    orders = chunks * ROWS
    anywhere = pl.BlockSpec(memory_space=pl.ANY)
    return pl.pallas_call(
        filter_kernel,
        out_shape=jax.ShapeDtypeStruct((degrees, orders, WIDE), jnp.bfloat16),
        in_specs=[anywhere, pl.BlockSpec(memory_space=pltpu.VMEM)],
        out_specs=anywhere,
        scratch_shapes=[
            pltpu.VMEM((pairs, chunks, 2 * ROWS, WIDE), jnp.bfloat16),
            pltpu.VMEM((pairs, 2, orders, WIDE), jnp.bfloat16),
            pltpu.VMEM((2, WIDE, WIDE), jnp.bfloat16),
            pltpu.SemaphoreType.DMA((pairs,)),
            pltpu.SemaphoreType.DMA((pairs,)),
        ],
        compiler_params=pltpu.CompilerParams(vmem_limit_bytes=VMEM_CAP),
    )(coefficients, filter_weight)


def body(grid_field, norm_gain, filter_weight):
    count = lax.axis_size("lat")
    band, longitudes, columns = grid_field.shape
    fits = scratch_bytes(scratch_of(count, band, longitudes)) < VMEM_CAP - 6 * 1024 * 1024
    if count % PLANE or not fits:
        return plain_body(grid_field, norm_gain, filter_weight)
    coefficients = coefficients_of(grid_field, norm_gain, count)
    return apply_filter(coefficients, filter_weight)


def solution(mesh):
    in_specs = (P("lat", None, "parts"), P("parts"), P("lat", None, None, "parts"))
    out_specs = P("lat", None, "parts")
    return jax.shard_map(body, mesh=mesh, in_specs=in_specs, out_specs=out_specs, check_vma=False)
```

```python
import functools
import math

import jax
import jax.numpy as jnp
import numpy as np
from jax import lax
from jax.experimental import pallas as pl
from jax.experimental.pallas import tpu as pltpu
from jax.sharding import PartitionSpec as P

C = 64
S = 2
DEG_DEV = 22
ORDER_PAD = 24
BLOCK = 16
LANES = 128


def round_up(value, step):
    return -(-value // step) * step


def legendre_kernel(
    orders_ref, cosine_ref, weights_ref, mant_ref, exp_ref, out_ref, prev_ref, early_ref, grow_ref, rows_ref
):
    block = pl.program_id(0)
    width = cosine_ref.shape[1]
    kept_width = out_ref.shape[2]

    @pl.when(block == 0)
    def _():
        prev_ref[...] = jnp.zeros_like(prev_ref)
        early_ref[...] = jnp.zeros_like(early_ref)
        grow_ref[...] = jnp.zeros_like(grow_ref)

    orders = orders_ref[...]
    narrow = orders[:, :LANES]
    order_sq = narrow * narrow
    cosine = cosine_ref[...]
    weights = weights_ref[...]
    limit = 2.0**64
    shrink = 2.0 ** (-64)
    previous, earlier, exponent = prev_ref[...], early_ref[...], grow_ref[...]
    first = (block * BLOCK).astype(jnp.float32)

    def widen(value):
        return jnp.concatenate([value] * (width // LANES), axis=1)

    for step in range(BLOCK):
        degree = first + float(step)
        upper = jnp.sqrt(
            (4.0 * degree * degree - 1.0) / jnp.maximum(degree * degree - order_sq, 1.0)
        )
        below = degree - 1.0
        lower = jnp.sqrt(
            jnp.maximum(below * below - order_sq, 0.0)
            / jnp.maximum(jnp.full_like(order_sq, 4.0 * below * below - 1.0), 1.0)
        )
        recurred = widen(upper) * (cosine * previous - widen(lower) * earlier)
        at_start = orders == degree
        current = jnp.where(at_start, mant_ref[...], jnp.where(orders < degree, recurred, 0.0))
        exponent = jnp.where(at_start, exp_ref[...], exponent)
        value = weights * (current * jnp.exp2(exponent))
        for lane in range(width // LANES):
            rows_ref[lane, step * ORDER_PAD : (step + 1) * ORDER_PAD, :] = value[
                :, lane * LANES : (lane + 1) * LANES
            ]
        large = jnp.abs(current) > limit
        earlier = jnp.where(large, previous * shrink, previous)
        previous = jnp.where(large, current * shrink, current)
        exponent = jnp.where(large, exponent + 64.0, exponent)

    prev_ref[...] = previous
    early_ref[...] = earlier
    grow_ref[...] = exponent
    for order in range(DEG_DEV):
        for lane in range(0, width, LANES):
            cut = min(LANES, kept_width - lane)
            piece = rows_ref[lane // LANES, pl.ds(order, BLOCK, stride=ORDER_PAD), :]
            out_ref[order, :, lane : lane + cut] = piece[:, :cut].astype(out_ref.dtype)


def legendre_table(colatitude, first_order, degrees, weight_scale):
    rows = colatitude.shape[0]
    width = round_up(rows, LANES)
    colat = jnp.concatenate([colatitude, jnp.full((width - rows,), 0.5 * math.pi, jnp.float32)])
    orders = (first_order + jnp.arange(ORDER_PAD, dtype=jnp.int32)).astype(jnp.float32)
    sine_rows = jnp.sin(colat)
    log_start = 0.5 * jnp.log((2.0 * orders + 1.0) / (4.0 * math.pi)) + 0.5 * (
        lax.lgamma(orders + 0.5) - lax.lgamma(orders + 1.0) - 0.5 * math.log(math.pi)
    )
    log_diag = log_start[:, None] + orders[:, None] * jnp.log(sine_rows)[None, :]
    start_exp = 64.0 * jnp.floor(log_diag / (64.0 * math.log(2.0)))
    start_mant = jnp.exp(log_diag - start_exp * math.log(2.0))
    state = (ORDER_PAD, width)
    whole = pl.BlockSpec(state, lambda i: (0, 0))
    line = pl.BlockSpec((1, width), lambda i: (0, 0))
    return pl.pallas_call(
        legendre_kernel,
        grid=(degrees // BLOCK,),
        out_shape=jax.ShapeDtypeStruct((DEG_DEV, degrees, rows), jnp.bfloat16),
        in_specs=[whole, line, line, whole, whole],
        out_specs=pl.BlockSpec((DEG_DEV, BLOCK, rows), lambda i: (0, i, 0)),
        scratch_shapes=[
            pltpu.VMEM(state, jnp.float32),
            pltpu.VMEM(state, jnp.float32),
            pltpu.VMEM(state, jnp.float32),
            pltpu.VMEM((width // LANES, BLOCK * ORDER_PAD, LANES), jnp.float32),
        ],
        cost_estimate=pl.CostEstimate(
            flops=degrees * ORDER_PAD * width * 2000,
            bytes_accessed=DEG_DEV * degrees * rows * 2,
            transcendentals=degrees * ORDER_PAD * width,
        ),
        compiler_params=pltpu.CompilerParams(vmem_limit_bytes=24 * 1024 * 1024),
    )(
        jnp.broadcast_to(orders[:, None], state),
        jnp.cos(colat)[None, :],
        (weight_scale * sine_rows)[None, :],
        start_mant,
        start_exp,
    )


def expand_filter(filter_weight):
    real_part = filter_weight[:, 0]
    imag_part = filter_weight[:, 1]
    from_real = jnp.stack([real_part, imag_part], axis=1)
    from_imag = jnp.stack([-imag_part, real_part], axis=1)
    mixing = jnp.stack([from_real, from_imag], axis=1)
    same = jnp.eye(S, dtype=filter_weight.dtype)
    full = mixing.transpose(0, 1, 3, 2, 4)[:, :, None, :, :, None, :] * same[None, None, :, None, None, :, None]
    return full.reshape(filter_weight.shape[0], 2 * S * C, 2 * S * C)


def mix_kernel(sin_ref, cos_ref, weight_ref, out_ref, rows_ref):
    sources, degrees, orders, half = cos_ref.shape
    for degree in range(degrees):
        for source in range(sources):
            rows = slice(source * orders, (source + 1) * orders)
            rows_ref[degree, rows, :half] = cos_ref[source, degree].astype(jnp.float32)
            rows_ref[degree, rows, half:] = sin_ref[source, degree].astype(jnp.float32)
        out_ref[degree] = jnp.dot(
            rows_ref[degree].astype(jnp.bfloat16),
            weight_ref[degree],
            preferred_element_type=jnp.float32,
        ).astype(out_ref.dtype)


def mix(coef_sin, coef_cos, weights):
    sources, degrees, orders, half = coef_cos.shape
    wide = weights.shape[2]
    step = 2
    piece = pl.BlockSpec((sources, step, orders, half), lambda i: (0, i, 0, 0))
    return pl.pallas_call(
        mix_kernel,
        grid=(degrees // step,),
        out_shape=jax.ShapeDtypeStruct((degrees, sources * orders, wide), jnp.bfloat16),
        in_specs=[piece, piece, pl.BlockSpec((step, 2 * half, wide), lambda i: (i, 0, 0))],
        out_specs=pl.BlockSpec((step, sources * orders, wide), lambda i: (i, 0, 0)),
        scratch_shapes=[pltpu.VMEM((step, sources * orders, 2 * half), jnp.float32)],
        compiler_params=pltpu.CompilerParams(vmem_limit_bytes=24 * 1024 * 1024),
    )(coef_sin, coef_cos, weights)


def fourier_matrix(orders, longitudes):
    phases = (np.arange(orders)[:, None] * np.arange(longitudes)[None, :]) % longitudes
    angles = 2.0 * np.pi * phases / longitudes
    return np.stack([np.cos(angles), -np.sin(angles)]).astype(np.float32)


def plain_body(grid_field, norm_gain, filter_weight):
    device_index = lax.axis_index("lat")
    lat_count = lax.axis_size("lat")
    band_rows, longitudes, columns = grid_field.shape
    total_lat = band_rows * lat_count
    order_count = DEG_DEV * lat_count
    all_rows = jnp.arange(total_lat, dtype=jnp.int32)
    colat_all = math.pi * (all_rows.astype(jnp.float32) + 0.5) / total_lat
    sine_all = jnp.sin(colat_all)
    own_rows = device_index * band_rows + jnp.arange(band_rows, dtype=jnp.int32)
    sine_own = jnp.sin(math.pi * (own_rows.astype(jnp.float32) + 0.5) / total_lat)

    first = jnp.einsum("j,jnx->x", sine_own, grid_field, precision=lax.Precision.HIGHEST)
    second = jnp.einsum(
        "j,jnx->x", sine_own, grid_field * grid_field, precision=lax.Precision.HIGHEST
    )
    band_mean = first / (longitudes * jnp.sum(sine_own))
    denominator_rows = jnp.float32(longitudes)
    cos_table, sin_table = fourier_matrix(order_count, longitudes)

    def transform(table):
        return jnp.einsum(
            "mn,jnx->mjx", jnp.asarray(table), grid_field, precision=lax.Precision.HIGH
        )

    def to_orders(raw):
        return lax.all_to_all(
            raw.astype(jnp.bfloat16), "lat", split_axis=0, concat_axis=1, tiled=True
        )

    def to_degrees(sums):
        return lax.all_to_all(
            sums, "lat", split_axis=0, concat_axis=0
        )

    received_sin = to_orders(transform(sin_table))
    constant = jnp.arange(order_count) == 0
    shift = jnp.where(constant[:, None, None], denominator_rows * band_mean, 0.0)
    received_cos = to_orders(transform(cos_table) - shift)

    weight_scale = math.pi**1.5 / math.sqrt(total_lat * longitudes)
    legendre = legendre_table(colat_all, device_index * DEG_DEV, order_count, weight_scale)

    def analyse(received):
        return jnp.einsum("mlj,mjx->mlx", legendre, received, preferred_element_type=jnp.float32)

    def by_degree(sums):
        ordered = sums.astype(jnp.bfloat16).transpose(1, 0, 2)
        return ordered.reshape(lat_count, DEG_DEV, DEG_DEV, columns)

    sums_sin = by_degree(analyse(received_sin))
    moments, sums_sin = lax.optimization_barrier(
        (jnp.stack([first, second, band_mean]), sums_sin)
    )
    gathered, sums_sin = lax.optimization_barrier((lax.all_gather(moments, "lat"), sums_sin))
    denominator = longitudes * jnp.sum(sine_all)
    average = jnp.sum(gathered[:, 0], axis=0) / denominator
    mean_square = jnp.sum(gathered[:, 1], axis=0) / denominator
    spread = jnp.sqrt(mean_square - average * average + 1e-05)
    factor = jnp.tile(norm_gain, S) / spread
    coef_sin = to_degrees(sums_sin)
    band_sums = jnp.sum(
        legendre[0].astype(jnp.float32).reshape(order_count, lat_count, band_rows), axis=2
    )
    level = jnp.dot(
        band_sums,
        denominator_rows * (gathered[:, 2] - average),
        precision=lax.Precision.HIGHEST,
    )
    here = (device_index == 0) & (jnp.arange(DEG_DEV) == 0)
    coef_cos = to_degrees(
        by_degree(analyse(received_cos) + jnp.where(here[:, None, None], level[None], 0.0))
    )

    expanded = expand_filter(filter_weight)
    expanded = (expanded * jnp.tile(factor, 2)[None, :, None]).astype(jnp.bfloat16)

    return mix(coef_sin, coef_cos, expanded)


MESH = pl.DeviceIdType.MESH
ROWS = 8
WIDE = 2 * LANES
CHUNKS = 3
PLANE = 4
PLANE_CHUNKS = PLANE * CHUNKS - 1
VMEM_CAP = 60 * 1024 * 1024


def owns_last(device):
    return device % PLANE != 1


def owner_chunk(device, slot, count):
    plane, inner = count // PLANE - 1 - device // PLANE, device % PLANE
    first = 1 // (plane + inner + 1)
    at = slot + first * (CHUNKS - 1 - 2 * slot)
    return PLANE_CHUNKS * plane + PLANE * at + inner - (at // (CHUNKS - 1)) * ((inner + 2) // PLANE)


def transform_tables(count, longitudes):
    table = np.zeros((CHUNKS, 2, count, ROWS, longitudes), np.float64)
    for slot in range(CHUNKS):
        for device in range(count):
            if slot == CHUNKS - 1 and not owns_last(device):
                continue
            orders = owner_chunk(device, slot, count) * ROWS + np.arange(ROWS)
            phases = (orders[:, None] * np.arange(longitudes)[None, :]) % longitudes
            angles = 2.0 * np.pi * phases / longitudes
            table[slot, 0, device] = np.cos(angles)
            table[slot, 1, device] = -np.sin(angles)
    table = table.reshape(CHUNKS, 2 * count * ROWS, longitudes).astype(np.float32)
    high = table.astype(jnp.bfloat16)
    low = (table - high.astype(np.float32)).astype(jnp.bfloat16)
    return high, low


def angle_tables(count, band, places):
    colat = np.pi * (np.arange(count * band) + 0.5) / (count * band)
    by_place = np.full((count, places), 0.5 * np.pi)
    valid = np.zeros((count, places))
    for device in range(count):
        rows = colat[device * band : (device + 1) * band]
        by_place[device, :band] = rows if device < count // 2 else rows[::-1]
        valid[device, :band] = 1.0
    sine_places = np.sin(by_place) * valid
    north = by_place[: count // 2].reshape(1, -1)
    weight = sine_places[: count // 2].reshape(1, -1)
    width = round_up(north.shape[1], LANES)
    north = np.pad(north, ((0, 0), (0, width - north.shape[1])), constant_values=0.5 * np.pi)
    weight = np.pad(weight, ((0, 0), (0, width - weight.shape[1])))
    return (
        sine_places.reshape(-1).astype(np.float32),
        np.cos(north).astype(np.float32),
        weight,
        np.log(np.sin(north)).astype(np.float32),
        float(np.sum(np.sin(colat))),
    )


def log_starts(order_count):
    values = [
        0.5 * math.log((2.0 * m + 1.0) / (4.0 * math.pi))
        + 0.5 * (math.lgamma(m + 0.5) - math.lgamma(m + 1.0) - 0.5 * math.log(math.pi))
        for m in range(order_count)
    ]
    return np.asarray(values, np.float32)[:, None]


def spectral_kernel(
    sizes,
    field_ref,
    gain_ref,
    high_ref,
    low_ref,
    sine_ref,
    cosine_ref,
    weight_ref,
    logsine_ref,
    start_ref,
    out_ref,
    high,
    low,
    stage,
    field_high,
    field_low,
    turned,
    outgoing,
    landed,
    moments,
    moments_all,
    scales,
    table,
    prev_ref,
    early_ref,
    grow_ref,
    mant_ref,
    exp_ref,
    lines,
    sums,
    sums_out,
    blank,
    table_sem,
    stage_sem,
    moment_send,
    moment_recv,
    send_sem,
    recv_sem,
    local_sem,
    send_two,
    recv_two,
    blank_sem,
):
    count, band, longitudes, total_sine = sizes
    me = lax.axis_index("lat")
    part = lax.axis_index("parts")
    half = count // 2
    south = me // half
    slot_of_me = me + south * (half + count - 1 - 2 * me)
    groups = outgoing.shape[0] // CHUNKS
    places = groups * ROWS
    degrees = table.shape[1]
    kept = table.shape[2]
    width = cosine_ref.shape[1]
    block_rows = DEG_DEV * ROWS
    zero_owner = count - PLANE
    has_last = owns_last(me)

    def has_chunk(slot, device):
        return (slot < CHUNKS - 1) | owns_last(device)

    def table_copies(slot):
        return (
            pltpu.make_async_copy(high_ref.at[slot], high.at[slot], table_sem.at[0, slot]),
            pltpu.make_async_copy(low_ref.at[slot], low.at[slot], table_sem.at[1, slot]),
        )

    def row_copy(place):
        row = place + south * (band - 1 - 2 * place)
        at = place % ROWS
        return pltpu.make_async_copy(field_ref.at[row], stage.at[at], stage_sem.at[at])

    for place in range(2):
        row_copy(place).start()
    for copy in table_copies(0):
        copy.start()
    for place in range(2, ROWS):
        row_copy(place).start()
    for slot in range(1, CHUNKS):
        for copy in table_copies(slot):
            copy.start()

    barrier = pltpu.get_barrier_semaphore()

    @pl.loop(1, count)
    def _(step):
        pl.semaphore_signal(
            barrier, inc=1, device_id=(part, (me + step) % count), device_id_type=MESH
        )

    moments[...] = jnp.zeros_like(moments)
    for place in range(band, places):
        lanes = slice((place % 2) * LANES, (place % 2 + 1) * LANES)
        field_high[place // 2, :, lanes] = jnp.zeros((longitudes, LANES), jnp.bfloat16)
        field_low[place // 2, :, lanes] = jnp.zeros((longitudes, LANES), jnp.bfloat16)

    piece = longitudes // 6

    def take_row(place, lanes):
        row_copy(place).wait()
        at = place % ROWS
        pair = place // 2
        total = jnp.zeros((ROWS, LANES), jnp.float32)
        square = jnp.zeros((ROWS, LANES), jnp.float32)
        for first in range(0, longitudes, piece):
            value = stage[at, first : first + piece, :]
            top = value.astype(jnp.bfloat16)
            field_high[pair, first : first + piece, lanes] = top
            field_low[pair, first : first + piece, lanes] = (
                value - top.astype(jnp.float32)
            ).astype(jnp.bfloat16)
            total += jnp.sum(value.reshape(-1, ROWS, LANES), axis=0)
            square += jnp.sum((value * value).reshape(-1, ROWS, LANES), axis=0)
        sine = sine_ref[me * places + place]
        moments[:ROWS] += sine * total
        moments[ROWS:] += sine * square

        @pl.when(place + ROWS < band)
        def _():
            row_copy(place + ROWS).start()

    def take_group(group):
        @pl.loop(0, ROWS // 2)
        def _(pair):
            place = group * ROWS + 2 * pair
            take_row(place, slice(0, LANES))

            @pl.when(place + 1 < band)
            def _():
                take_row(place + 1, slice(LANES, WIDE))

    take_group(0)
    pl.semaphore_wait(barrier, count - 1)

    def blank_copy(chunk, lines_off):
        rows = pl.ds(0, lines_off * ROWS)
        return pltpu.make_async_copy(
            blank.at[rows], out_ref.at[chunk, rows], blank_sem.at[chunk]
        )

    def moment_copy(device):
        return pltpu.make_async_remote_copy(
            moments,
            moments_all.at[me],
            moment_send,
            moment_recv,
            device_id=(part, device),
            device_id_type=MESH,
        )

    def order_copy(slot, group, device):
        step = slot * groups + group
        rows = pl.ds(pl.multiple_of(device * ROWS * ROWS, ROWS * ROWS), ROWS * ROWS)
        return pltpu.make_async_remote_copy(
            outgoing.at[step, rows],
            landed.at[slot, slot_of_me, group],
            send_sem.at[step],
            recv_sem.at[slot],
            device_id=(part, device),
            device_id_type=MESH,
        )

    def own_copy(slot, group):
        step = slot * groups + group
        rows = pl.ds(pl.multiple_of(me * ROWS * ROWS, ROWS * ROWS), ROWS * ROWS)
        return pltpu.make_async_copy(
            outgoing.at[step, rows], landed.at[slot, slot_of_me, group], local_sem.at[step]
        )

    def transform(step):
        slot, group = step // groups, step % groups

        @pl.when((step > 0) & (slot == 0))
        def _():
            take_group(group)

        @pl.when(step == groups - 1)
        def _():
            moments_all[me] = moments[...]

            @pl.loop(1, count)
            def _(ahead):
                moment_copy((me + ahead) % count).start()

        @pl.when(group == 0)
        def _():
            for copy in table_copies(slot):
                copy.wait()

        @pl.loop(0, ROWS // 2)
        def _(pair):
            at = group * (ROWS // 2) + pair
            product = jnp.dot(high[slot], field_high[at], preferred_element_type=jnp.float32)
            product += jnp.dot(high[slot], field_low[at], preferred_element_type=jnp.float32)
            product += jnp.dot(low[slot], field_high[at], preferred_element_type=jnp.float32)
            lines_of = count * ROWS
            for side in range(2):
                for row in range(2):
                    turned[side, pl.ds(2 * pair + row, lines_of, stride=ROWS), :] = product[
                        side * lines_of : (side + 1) * lines_of, row * LANES : (row + 1) * LANES
                    ]

        @pl.when(slot == CHUNKS - 1)
        def _():
            at = zero_owner * ROWS * ROWS
            turned[0, at : at + ROWS, :] -= scales[1:2, :LANES]

        @pl.loop(0, count)
        def _(ahead):
            device = (me + 1 + ahead) % count
            rows = pl.ds(pl.multiple_of(device * ROWS * ROWS, ROWS * ROWS), ROWS * ROWS)
            outgoing[step, rows, :] = jnp.concatenate(
                [turned[0, rows, :], turned[1, rows, :]], axis=1
            ).astype(jnp.bfloat16)

            @pl.when((device != me) & has_chunk(slot, device))
            def _():
                order_copy(slot, group, device).start()

            @pl.when((device == me) & has_chunk(slot, device))
            def _():
                own_copy(slot, group).start()

    pl.loop(0, (CHUNKS - 1) * groups)(transform)

    pltpu.make_async_copy(
        moments_all.at[pl.ds(0, count - 1)],
        moments_all.at[pl.ds(0, count - 1)],
        moment_recv,
    ).wait()
    gathered = jnp.sum(moments_all[...], axis=0)
    first = jnp.sum(gathered[:ROWS], axis=0, keepdims=True) / (longitudes * total_sine)
    second = jnp.sum(gathered[ROWS:], axis=0, keepdims=True) / (longitudes * total_sine)
    spread = jnp.sqrt(second - first * first + 1e-05)
    gain = gain_ref[...]
    factor = jnp.concatenate([gain] * S, axis=1) / spread
    scales[:1] = jnp.concatenate([factor, factor], axis=1)
    scales[1:2] = jnp.concatenate([longitudes * first, jnp.zeros_like(first)], axis=1)

    blank[...] = jnp.zeros_like(blank)

    @pl.loop(0, out_ref.shape[0])
    def _(chunk):
        low_line = chunk * ROWS - me * DEG_DEV

        @pl.when(low_line >= DEG_DEV)
        def _():
            pltpu.make_async_copy(blank, out_ref.at[chunk], recv_two.at[chunk]).start()

        for lines_off in range(2, DEG_DEV, 2):

            @pl.when(low_line == lines_off)
            def _():
                blank_copy(chunk, lines_off).start()

    chunk_of = [owner_chunk(me, slot, count) for slot in range(CHUNKS)]
    lines_in = lax.broadcasted_iota(jnp.int32, (ROWS, width), 0)
    orders = jnp.concatenate(
        [(chunk * ROWS + lines_in).astype(jnp.float32) for chunk in chunk_of], axis=0
    )
    start = jnp.concatenate(
        [start_ref[pl.ds(pl.multiple_of(chunk * ROWS, ROWS), ROWS), :] for chunk in chunk_of], axis=0
    )
    start = jnp.broadcast_to(start, (CHUNKS * ROWS, width))

    def widen(value):
        return jnp.concatenate([value] * (width // LANES), axis=1)

    log_diag = start + orders * logsine_ref[...]
    start_exp = 64.0 * jnp.floor(log_diag / (64.0 * math.log(2.0)))
    exp_ref[...] = start_exp
    mant_ref[...] = jnp.exp(log_diag - start_exp * math.log(2.0))
    prev_ref[...] = jnp.zeros_like(prev_ref)
    early_ref[...] = jnp.zeros_like(early_ref)
    grow_ref[...] = jnp.zeros_like(grow_ref)
    order_lines = CHUNKS * ROWS

    @pl.loop(0, degrees // BLOCK)
    def _(block):
        narrow = orders[:, :LANES]
        order_sq = narrow * narrow
        cosine = cosine_ref[...]
        weights = weight_ref[...]
        limit = 2.0**64
        shrink = 2.0 ** (-64)
        previous, earlier, exponent = prev_ref[...], early_ref[...], grow_ref[...]
        first = (block * BLOCK).astype(jnp.float32)
        for step in range(BLOCK):
            degree = first + float(step)
            upper = jnp.sqrt(
                (4.0 * degree * degree - 1.0) / jnp.maximum(degree * degree - order_sq, 1.0)
            )
            below = degree - 1.0
            lower = jnp.sqrt(
                jnp.maximum(below * below - order_sq, 0.0)
                / jnp.maximum(jnp.full_like(order_sq, 4.0 * below * below - 1.0), 1.0)
            )
            recurred = widen(upper) * (cosine * previous - widen(lower) * earlier)
            at_start = orders == degree
            current = jnp.where(at_start, mant_ref[...], jnp.where(orders < degree, recurred, 0.0))
            exponent = jnp.where(at_start, exp_ref[...], exponent)
            value = weights * (current * jnp.exp2(exponent))
            for lane in range(width // LANES):
                lines[lane, step * order_lines : (step + 1) * order_lines, :] = value[
                    :, lane * LANES : (lane + 1) * LANES
                ]
            large = jnp.abs(current) > limit
            earlier = jnp.where(large, previous * shrink, previous)
            previous = jnp.where(large, current * shrink, current)
            exponent = jnp.where(large, exponent + 64.0, exponent)
        prev_ref[...] = previous
        early_ref[...] = earlier
        grow_ref[...] = exponent
        rows = pl.ds(pl.multiple_of(block * BLOCK, BLOCK), BLOCK)
        for order in range(order_lines):
            for lane in range(0, width, LANES):
                cut = min(LANES, kept - lane)
                part_of = lines[lane // LANES, pl.ds(order, BLOCK, stride=order_lines), :]
                table[order, rows, lane : lane + cut] = part_of[:, :cut].astype(table.dtype)

    def rows_from(device, lines_off):
        base = pl.multiple_of(device * block_rows + lines_off * ROWS, 2 * ROWS)
        return pl.ds(base, block_rows - lines_off * ROWS)

    def degree_copy(slot, device, lines_off=0):
        chunk = owner_chunk(me, slot, count)
        return pltpu.make_async_remote_copy(
            sums_out.at[slot, rows_from(device, lines_off)],
            out_ref.at[chunk, rows_from(0, lines_off)],
            send_two.at[slot, device],
            recv_two.at[chunk],
            device_id=(part, device),
            device_id_type=MESH,
        )

    def own_degrees(slot, lines_off=0):
        chunk = owner_chunk(me, slot, count)
        return pltpu.make_async_copy(
            sums_out.at[slot, rows_from(me, lines_off)],
            out_ref.at[chunk, rows_from(0, lines_off)],
            recv_two.at[chunk],
        )

    upper = count - count // PLANE

    def crosses(device):
        return (device >= upper) != (me >= upper)

    def each_target(slot, chosen, remote, local):
        first_line = owner_chunk(me, slot, count) * ROWS

        @pl.loop(1, count)
        def _(ahead):
            device = (me + ahead) % count

            @pl.when((first_line <= device * DEG_DEV) & chosen(device))
            def _():
                remote(slot, device, 0)

        @pl.when((first_line <= me * DEG_DEV) & chosen(me))
        def _():
            local(slot, 0)

        device = first_line // DEG_DEV
        for lines_off in range(2, DEG_DEV, 2):
            hit = (first_line - device * DEG_DEV == lines_off) & chosen(device)

            @pl.when(hit & (device != me))
            def _():
                remote(slot, device, lines_off)

            @pl.when(hit & (device == me))
            def _():
                local(slot, lines_off)

    def send_degrees(slot, chosen):
        each_target(
            slot,
            chosen,
            lambda *where: degree_copy(*where).start(),
            lambda *where: own_degrees(*where).start(),
        )

    degree_line = lax.broadcasted_iota(jnp.int32, (degrees, 1), 0)
    sign_even = jnp.where(degree_line % 2 == 0, 1.0, -1.0).astype(jnp.float32)

    def analyse(slot):
        pltpu.make_async_copy(
            landed.at[slot, pl.ds(0, count - 1)],
            landed.at[slot, pl.ds(0, count - 1)],
            recv_sem.at[slot],
        ).wait()
        for group in range(groups):
            own_copy(slot, group).wait()

        @pl.loop(0, ROWS // 2)
        def _(pair):
            rows = pl.ds(pl.multiple_of(pair * 2 * ROWS, 2 * ROWS), 2 * ROWS)
            both = landed[slot, :, :, rows, :].astype(jnp.float32)
            both = both.reshape(count * groups, 2, ROWS, WIDE)
            for odd in range(2):
                rhs = both[:, odd].reshape(count * places, WIDE).astype(jnp.bfloat16)
                lhs = table[slot * ROWS + 2 * pair + odd]
                north = jnp.dot(lhs, rhs[:kept], preferred_element_type=jnp.float32)
                mirror = jnp.dot(lhs, rhs[kept:], preferred_element_type=jnp.float32)
                sign = sign_even if odd == 0 else -sign_even
                result = (north + sign * mirror) * scales[:1]
                for lane in range(2):
                    sums[lane, pl.ds(2 * pair + odd, degrees, stride=ROWS), :] = result[
                        :, lane * LANES : (lane + 1) * LANES
                    ]

        @pl.loop(0, count)
        def _(device):
            rows = pl.ds(pl.multiple_of(device * block_rows, block_rows), block_rows)
            sums_out[slot, rows, :] = jnp.concatenate(
                [sums[0, rows, :], sums[1, rows, :]], axis=1
            ).astype(jnp.bfloat16)

    @pl.loop(0, CHUNKS)
    def _(slot):
        @pl.when((slot < CHUNKS - 1) | has_last)
        def _():
            analyse(slot)
            send_degrees(slot, crosses)

        @pl.when(slot == 0)
        def _():
            pl.loop((CHUNKS - 1) * groups, CHUNKS * groups)(transform)

        @pl.when((slot < CHUNKS - 1) | has_last)
        def _():
            send_degrees(slot, lambda device: jnp.logical_not(crosses(device)))

    pltpu.make_async_copy(
        moments_all.at[pl.ds(0, count - 1)], moments_all.at[pl.ds(0, count - 1)], moment_send
    ).wait()

    def wait_orders(step, devices):
        rows = pl.ds(0, devices * ROWS * ROWS)
        pltpu.make_async_copy(
            outgoing.at[step, rows], outgoing.at[step, rows], send_sem.at[step]
        ).wait()

    @pl.loop(0, (CHUNKS - 1) * groups)
    def _(step):
        wait_orders(step, count - 1)

    last_owners = count - count // PLANE

    @pl.loop((CHUNKS - 1) * groups, CHUNKS * groups)
    def _(step):
        @pl.when(has_last)
        def _():
            wait_orders(step, last_owners - 1)

        @pl.when(jnp.logical_not(has_last))
        def _():
            wait_orders(step, last_owners)

    @pl.loop(0, CHUNKS)
    def _(slot):
        @pl.when(has_chunk(slot, me))
        def _():
            each_target(
                slot,
                lambda device: device >= 0,
                lambda *where: degree_copy(*where).wait_send(),
                lambda *where: None,
            )

    @pl.loop(0, out_ref.shape[0])
    def _(chunk):
        low_line = chunk * ROWS - me * DEG_DEV

        @pl.when((low_line <= 0) | (low_line >= DEG_DEV))
        def _():
            pltpu.make_async_copy(blank, out_ref.at[chunk], recv_two.at[chunk]).wait()

        for lines_off in range(2, DEG_DEV, 2):

            @pl.when(low_line == lines_off)
            def _():
                blank_copy(chunk, lines_off).wait()
                rows = rows_from(0, lines_off)
                pltpu.make_async_copy(
                    blank.at[rows], out_ref.at[chunk, rows], recv_two.at[chunk]
                ).wait()


def scratch_of(count, band, longitudes):
    groups = -(-band // ROWS)
    places = groups * ROWS
    degrees = DEG_DEV * count
    lines_of = count * ROWS
    kept = count // 2 * places
    width = round_up(kept, LANES)
    order_lines = CHUNKS * ROWS
    state = (order_lines, width)
    bf16, f32 = jnp.bfloat16, jnp.float32
    return [
        ((CHUNKS, 2 * lines_of, longitudes), bf16),
        ((CHUNKS, 2 * lines_of, longitudes), bf16),
        ((ROWS, longitudes, LANES), f32),
        ((places // 2, longitudes, WIDE), bf16),
        ((places // 2, longitudes, WIDE), bf16),
        ((2, lines_of * ROWS, LANES), f32),
        ((CHUNKS * groups, lines_of * ROWS, WIDE), bf16),
        ((CHUNKS, count, groups, ROWS * ROWS, WIDE), bf16),
        ((2 * ROWS, LANES), f32),
        ((count, 2 * ROWS, LANES), f32),
        ((ROWS, WIDE), f32),
        ((order_lines, degrees, kept), bf16),
        (state, f32),
        (state, f32),
        (state, f32),
        (state, f32),
        (state, f32),
        ((width // LANES, BLOCK * order_lines, LANES), f32),
        ((2, degrees * ROWS, LANES), f32),
        ((CHUNKS, degrees * ROWS, WIDE), bf16),
        ((DEG_DEV * ROWS, WIDE), bf16),
    ]


def scratch_bytes(shapes):
    total = 0
    for shape, dtype in shapes:
        size = math.prod(shape[:-1]) * round_up(shape[-1], LANES)
        total += size * jnp.dtype(dtype).itemsize
    return total


def coefficients_of(grid_field, norm_gain, count):
    band, longitudes, columns = grid_field.shape
    groups = -(-band // ROWS)
    places = groups * ROWS
    order_count = DEG_DEV * count
    high, low = transform_tables(count, longitudes)
    sine, cosine, weight, logsine, total_sine = angle_tables(count, band, places)
    weight_scale = math.pi**1.5 / math.sqrt(count * band * longitudes)
    shapes = scratch_of(count, band, longitudes)
    dma = pltpu.SemaphoreType.DMA
    vmem = pl.BlockSpec(memory_space=pltpu.VMEM)
    anywhere = pl.BlockSpec(memory_space=pl.ANY)
    return pl.pallas_call(
        functools.partial(spectral_kernel, (count, band, longitudes, total_sine)),
        out_shape=jax.ShapeDtypeStruct((order_count // ROWS, DEG_DEV * ROWS, WIDE), jnp.bfloat16),
        in_specs=[
            anywhere,
            vmem,
            anywhere,
            anywhere,
            pl.BlockSpec(memory_space=pltpu.SMEM),
            vmem,
            vmem,
            vmem,
            vmem,
        ],
        out_specs=anywhere,
        scratch_shapes=[pltpu.VMEM(shape, dtype) for shape, dtype in shapes]
        + [
            dma((2, CHUNKS)),
            dma((ROWS,)),
            dma,
            dma,
            dma((CHUNKS * groups,)),
            dma((CHUNKS,)),
            dma((CHUNKS * groups,)),
            dma((CHUNKS, count)),
            dma((order_count // ROWS,)),
            dma((order_count // ROWS,)),
        ],
        cost_estimate=pl.CostEstimate(
            flops=20 * 10**9, bytes_accessed=40 * 10**6, transcendentals=10**6
        ),
        compiler_params=pltpu.CompilerParams(
            collective_id=0, has_side_effects=True, vmem_limit_bytes=VMEM_CAP
        ),
    )(
        grid_field,
        norm_gain[None, :],
        jnp.asarray(high),
        jnp.asarray(low),
        jnp.asarray(sine),
        jnp.asarray(cosine),
        jnp.asarray((weight * weight_scale).astype(np.float32)),
        jnp.asarray(logsine),
        jnp.asarray(log_starts(order_count)),
    )


def filter_kernel(coef_ref, weight_ref, out_ref, coefs, outs, full_ref, in_sem, out_sem):
    pairs = coefs.shape[0]
    chunks = coefs.shape[1]
    orders = chunks * ROWS

    def fetch(pair):
        rows = pl.ds(pl.multiple_of(pair * 2 * ROWS, 2 * ROWS), 2 * ROWS)
        return pltpu.make_async_copy(coef_ref.at[:, rows, :], coefs.at[pair], in_sem.at[pair])

    def store(pair):
        return pltpu.make_async_copy(
            outs.at[pair], out_ref.at[pl.ds(2 * pair, 2)], out_sem.at[pair]
        )

    for pair in range(pairs):
        fetch(pair).start()
    full_ref[...] = jnp.zeros_like(full_ref)

    @pl.loop(0, pairs)
    def _(pair):
        for odd in range(2):
            real, imag = weight_ref[2 * pair + odd, 0], weight_ref[2 * pair + odd, 1]
            for sample in range(S):
                for side, halves in enumerate(((real, imag), (-imag, real))):
                    for target, block in enumerate(halves):
                        row = side * S * C + sample * C
                        lane = target * S * C + sample * C
                        full_ref[odd, row : row + C, lane : lane + C] = block
        fetch(pair).wait()
        both = coefs[pair].astype(jnp.float32).reshape(chunks, 2, ROWS, WIDE)
        for odd in range(2):
            value = both[:, odd].reshape(orders, WIDE).astype(jnp.bfloat16)
            outs[pair, odd] = jnp.dot(
                value, full_ref[odd], preferred_element_type=jnp.float32
            ).astype(outs.dtype)
        store(pair).start()

    @pl.loop(0, pairs)
    def _(pair):
        store(pair).wait()


def apply_filter(coefficients, filter_weight):
    chunks = coefficients.shape[0]
    degrees = filter_weight.shape[0]
    pairs = degrees // 2
    orders = chunks * ROWS
    anywhere = pl.BlockSpec(memory_space=pl.ANY)
    return pl.pallas_call(
        filter_kernel,
        out_shape=jax.ShapeDtypeStruct((degrees, orders, WIDE), jnp.bfloat16),
        in_specs=[anywhere, pl.BlockSpec(memory_space=pltpu.VMEM)],
        out_specs=anywhere,
        scratch_shapes=[
            pltpu.VMEM((pairs, chunks, 2 * ROWS, WIDE), jnp.bfloat16),
            pltpu.VMEM((pairs, 2, orders, WIDE), jnp.bfloat16),
            pltpu.VMEM((2, WIDE, WIDE), jnp.bfloat16),
            pltpu.SemaphoreType.DMA((pairs,)),
            pltpu.SemaphoreType.DMA((pairs,)),
        ],
        compiler_params=pltpu.CompilerParams(vmem_limit_bytes=VMEM_CAP),
    )(coefficients, filter_weight)


def body(grid_field, norm_gain, filter_weight):
    count = lax.axis_size("lat")
    band, longitudes, columns = grid_field.shape
    fits = scratch_bytes(scratch_of(count, band, longitudes)) < VMEM_CAP - 6 * 1024 * 1024
    if count % PLANE or not fits:
        return plain_body(grid_field, norm_gain, filter_weight)
    coefficients = coefficients_of(grid_field, norm_gain, count)
    return apply_filter(coefficients, filter_weight)


def solution(mesh):
    in_specs = (P("lat", None, "parts"), P("parts"), P("lat", None, None, "parts"))
    out_specs = P("lat", None, "parts")
    return jax.shard_map(body, mesh=mesh, in_specs=in_specs, out_specs=out_specs, check_vma=False)
```

```python
import functools
import math

import jax
import jax.numpy as jnp
import numpy as np
from jax import lax
from jax.experimental import pallas as pl
from jax.experimental.pallas import tpu as pltpu
from jax.sharding import PartitionSpec as P

C = 64
S = 2
DEG_DEV = 22
ORDER_PAD = 24
BLOCK = 16
LANES = 128


def round_up(value, step):
    return -(-value // step) * step


def legendre_kernel(
    orders_ref, cosine_ref, weights_ref, mant_ref, exp_ref, out_ref, prev_ref, early_ref, grow_ref, rows_ref
):
    block = pl.program_id(0)
    width = cosine_ref.shape[1]
    kept_width = out_ref.shape[2]

    @pl.when(block == 0)
    def _():
        prev_ref[...] = jnp.zeros_like(prev_ref)
        early_ref[...] = jnp.zeros_like(early_ref)
        grow_ref[...] = jnp.zeros_like(grow_ref)

    orders = orders_ref[...]
    narrow = orders[:, :LANES]
    order_sq = narrow * narrow
    cosine = cosine_ref[...]
    weights = weights_ref[...]
    limit = 2.0**64
    shrink = 2.0 ** (-64)
    previous, earlier, exponent = prev_ref[...], early_ref[...], grow_ref[...]
    first = (block * BLOCK).astype(jnp.float32)

    def widen(value):
        return jnp.concatenate([value] * (width // LANES), axis=1)

    for step in range(BLOCK):
        degree = first + float(step)
        upper = jnp.sqrt(
            (4.0 * degree * degree - 1.0) / jnp.maximum(degree * degree - order_sq, 1.0)
        )
        below = degree - 1.0
        lower = jnp.sqrt(
            jnp.maximum(below * below - order_sq, 0.0)
            / jnp.maximum(jnp.full_like(order_sq, 4.0 * below * below - 1.0), 1.0)
        )
        recurred = widen(upper) * (cosine * previous - widen(lower) * earlier)
        at_start = orders == degree
        current = jnp.where(at_start, mant_ref[...], jnp.where(orders < degree, recurred, 0.0))
        exponent = jnp.where(at_start, exp_ref[...], exponent)
        value = weights * (current * jnp.exp2(exponent))
        for lane in range(width // LANES):
            rows_ref[lane, step * ORDER_PAD : (step + 1) * ORDER_PAD, :] = value[
                :, lane * LANES : (lane + 1) * LANES
            ]
        large = jnp.abs(current) > limit
        earlier = jnp.where(large, previous * shrink, previous)
        previous = jnp.where(large, current * shrink, current)
        exponent = jnp.where(large, exponent + 64.0, exponent)

    prev_ref[...] = previous
    early_ref[...] = earlier
    grow_ref[...] = exponent
    for order in range(DEG_DEV):
        for lane in range(0, width, LANES):
            cut = min(LANES, kept_width - lane)
            piece = rows_ref[lane // LANES, pl.ds(order, BLOCK, stride=ORDER_PAD), :]
            out_ref[order, :, lane : lane + cut] = piece[:, :cut].astype(out_ref.dtype)


def legendre_table(colatitude, first_order, degrees, weight_scale):
    rows = colatitude.shape[0]
    width = round_up(rows, LANES)
    colat = jnp.concatenate([colatitude, jnp.full((width - rows,), 0.5 * math.pi, jnp.float32)])
    orders = (first_order + jnp.arange(ORDER_PAD, dtype=jnp.int32)).astype(jnp.float32)
    sine_rows = jnp.sin(colat)
    log_start = 0.5 * jnp.log((2.0 * orders + 1.0) / (4.0 * math.pi)) + 0.5 * (
        lax.lgamma(orders + 0.5) - lax.lgamma(orders + 1.0) - 0.5 * math.log(math.pi)
    )
    log_diag = log_start[:, None] + orders[:, None] * jnp.log(sine_rows)[None, :]
    start_exp = 64.0 * jnp.floor(log_diag / (64.0 * math.log(2.0)))
    start_mant = jnp.exp(log_diag - start_exp * math.log(2.0))
    state = (ORDER_PAD, width)
    whole = pl.BlockSpec(state, lambda i: (0, 0))
    line = pl.BlockSpec((1, width), lambda i: (0, 0))
    return pl.pallas_call(
        legendre_kernel,
        grid=(degrees // BLOCK,),
        out_shape=jax.ShapeDtypeStruct((DEG_DEV, degrees, rows), jnp.bfloat16),
        in_specs=[whole, line, line, whole, whole],
        out_specs=pl.BlockSpec((DEG_DEV, BLOCK, rows), lambda i: (0, i, 0)),
        scratch_shapes=[
            pltpu.VMEM(state, jnp.float32),
            pltpu.VMEM(state, jnp.float32),
            pltpu.VMEM(state, jnp.float32),
            pltpu.VMEM((width // LANES, BLOCK * ORDER_PAD, LANES), jnp.float32),
        ],
        cost_estimate=pl.CostEstimate(
            flops=degrees * ORDER_PAD * width * 2000,
            bytes_accessed=DEG_DEV * degrees * rows * 2,
            transcendentals=degrees * ORDER_PAD * width,
        ),
        compiler_params=pltpu.CompilerParams(vmem_limit_bytes=24 * 1024 * 1024),
    )(
        jnp.broadcast_to(orders[:, None], state),
        jnp.cos(colat)[None, :],
        (weight_scale * sine_rows)[None, :],
        start_mant,
        start_exp,
    )


def expand_filter(filter_weight):
    real_part = filter_weight[:, 0]
    imag_part = filter_weight[:, 1]
    from_real = jnp.stack([real_part, imag_part], axis=1)
    from_imag = jnp.stack([-imag_part, real_part], axis=1)
    mixing = jnp.stack([from_real, from_imag], axis=1)
    same = jnp.eye(S, dtype=filter_weight.dtype)
    full = mixing.transpose(0, 1, 3, 2, 4)[:, :, None, :, :, None, :] * same[None, None, :, None, None, :, None]
    return full.reshape(filter_weight.shape[0], 2 * S * C, 2 * S * C)


def mix_kernel(sin_ref, cos_ref, weight_ref, out_ref, rows_ref):
    sources, degrees, orders, half = cos_ref.shape
    for degree in range(degrees):
        for source in range(sources):
            rows = slice(source * orders, (source + 1) * orders)
            rows_ref[degree, rows, :half] = cos_ref[source, degree].astype(jnp.float32)
            rows_ref[degree, rows, half:] = sin_ref[source, degree].astype(jnp.float32)
        out_ref[degree] = jnp.dot(
            rows_ref[degree].astype(jnp.bfloat16),
            weight_ref[degree],
            preferred_element_type=jnp.float32,
        ).astype(out_ref.dtype)


def mix(coef_sin, coef_cos, weights):
    sources, degrees, orders, half = coef_cos.shape
    wide = weights.shape[2]
    step = 2
    piece = pl.BlockSpec((sources, step, orders, half), lambda i: (0, i, 0, 0))
    return pl.pallas_call(
        mix_kernel,
        grid=(degrees // step,),
        out_shape=jax.ShapeDtypeStruct((degrees, sources * orders, wide), jnp.bfloat16),
        in_specs=[piece, piece, pl.BlockSpec((step, 2 * half, wide), lambda i: (i, 0, 0))],
        out_specs=pl.BlockSpec((step, sources * orders, wide), lambda i: (i, 0, 0)),
        scratch_shapes=[pltpu.VMEM((step, sources * orders, 2 * half), jnp.float32)],
        compiler_params=pltpu.CompilerParams(vmem_limit_bytes=24 * 1024 * 1024),
    )(coef_sin, coef_cos, weights)


def fourier_matrix(orders, longitudes):
    phases = (np.arange(orders)[:, None] * np.arange(longitudes)[None, :]) % longitudes
    angles = 2.0 * np.pi * phases / longitudes
    return np.stack([np.cos(angles), -np.sin(angles)]).astype(np.float32)


def plain_body(grid_field, norm_gain, filter_weight):
    device_index = lax.axis_index("lat")
    lat_count = lax.axis_size("lat")
    band_rows, longitudes, columns = grid_field.shape
    total_lat = band_rows * lat_count
    order_count = DEG_DEV * lat_count
    all_rows = jnp.arange(total_lat, dtype=jnp.int32)
    colat_all = math.pi * (all_rows.astype(jnp.float32) + 0.5) / total_lat
    sine_all = jnp.sin(colat_all)
    own_rows = device_index * band_rows + jnp.arange(band_rows, dtype=jnp.int32)
    sine_own = jnp.sin(math.pi * (own_rows.astype(jnp.float32) + 0.5) / total_lat)

    first = jnp.einsum("j,jnx->x", sine_own, grid_field, precision=lax.Precision.HIGHEST)
    second = jnp.einsum(
        "j,jnx->x", sine_own, grid_field * grid_field, precision=lax.Precision.HIGHEST
    )
    band_mean = first / (longitudes * jnp.sum(sine_own))
    denominator_rows = jnp.float32(longitudes)
    cos_table, sin_table = fourier_matrix(order_count, longitudes)

    def transform(table):
        return jnp.einsum(
            "mn,jnx->mjx", jnp.asarray(table), grid_field, precision=lax.Precision.HIGH
        )

    def to_orders(raw):
        return lax.all_to_all(
            raw.astype(jnp.bfloat16), "lat", split_axis=0, concat_axis=1, tiled=True
        )

    def to_degrees(sums):
        return lax.all_to_all(
            sums, "lat", split_axis=0, concat_axis=0
        )

    received_sin = to_orders(transform(sin_table))
    constant = jnp.arange(order_count) == 0
    shift = jnp.where(constant[:, None, None], denominator_rows * band_mean, 0.0)
    received_cos = to_orders(transform(cos_table) - shift)

    weight_scale = math.pi**1.5 / math.sqrt(total_lat * longitudes)
    legendre = legendre_table(colat_all, device_index * DEG_DEV, order_count, weight_scale)

    def analyse(received):
        return jnp.einsum("mlj,mjx->mlx", legendre, received, preferred_element_type=jnp.float32)

    def by_degree(sums):
        ordered = sums.astype(jnp.bfloat16).transpose(1, 0, 2)
        return ordered.reshape(lat_count, DEG_DEV, DEG_DEV, columns)

    sums_sin = by_degree(analyse(received_sin))
    moments, sums_sin = lax.optimization_barrier(
        (jnp.stack([first, second, band_mean]), sums_sin)
    )
    gathered, sums_sin = lax.optimization_barrier((lax.all_gather(moments, "lat"), sums_sin))
    denominator = longitudes * jnp.sum(sine_all)
    average = jnp.sum(gathered[:, 0], axis=0) / denominator
    mean_square = jnp.sum(gathered[:, 1], axis=0) / denominator
    spread = jnp.sqrt(mean_square - average * average + 1e-05)
    factor = jnp.tile(norm_gain, S) / spread
    coef_sin = to_degrees(sums_sin)
    band_sums = jnp.sum(
        legendre[0].astype(jnp.float32).reshape(order_count, lat_count, band_rows), axis=2
    )
    level = jnp.dot(
        band_sums,
        denominator_rows * (gathered[:, 2] - average),
        precision=lax.Precision.HIGHEST,
    )
    here = (device_index == 0) & (jnp.arange(DEG_DEV) == 0)
    coef_cos = to_degrees(
        by_degree(analyse(received_cos) + jnp.where(here[:, None, None], level[None], 0.0))
    )

    expanded = expand_filter(filter_weight)
    expanded = (expanded * jnp.tile(factor, 2)[None, :, None]).astype(jnp.bfloat16)

    return mix(coef_sin, coef_cos, expanded)


MESH = pl.DeviceIdType.MESH
ROWS = 8
WIDE = 2 * LANES
CHUNKS = 3
PLANE = 4
PLANE_CHUNKS = PLANE * CHUNKS - 1
VMEM_CAP = 60 * 1024 * 1024


def owns_last(device):
    return device % PLANE != 1


def owner_chunk(device, slot, count):
    plane, inner = count // PLANE - 1 - device // PLANE, device % PLANE
    first = 1 // (plane + inner + 1)
    at = slot + first * (CHUNKS - 1 - 2 * slot)
    return PLANE_CHUNKS * plane + PLANE * at + inner - (at // (CHUNKS - 1)) * ((inner + 2) // PLANE)


def transform_tables(count, longitudes):
    table = np.zeros((CHUNKS, 2, count, ROWS, longitudes), np.float64)
    for slot in range(CHUNKS):
        for device in range(count):
            if slot == CHUNKS - 1 and not owns_last(device):
                continue
            orders = owner_chunk(device, slot, count) * ROWS + np.arange(ROWS)
            phases = (orders[:, None] * np.arange(longitudes)[None, :]) % longitudes
            angles = 2.0 * np.pi * phases / longitudes
            table[slot, 0, device] = np.cos(angles)
            table[slot, 1, device] = -np.sin(angles)
    table = table.reshape(CHUNKS, 2 * count * ROWS, longitudes).astype(np.float32)
    high = table.astype(jnp.bfloat16)
    low = (table - high.astype(np.float32)).astype(jnp.bfloat16)
    return high, low


def angle_tables(count, band, places):
    colat = np.pi * (np.arange(count * band) + 0.5) / (count * band)
    by_place = np.full((count, places), 0.5 * np.pi)
    valid = np.zeros((count, places))
    for device in range(count):
        rows = colat[device * band : (device + 1) * band]
        by_place[device, :band] = rows if device < count // 2 else rows[::-1]
        valid[device, :band] = 1.0
    sine_places = np.sin(by_place) * valid
    north = by_place[: count // 2].reshape(1, -1)
    weight = sine_places[: count // 2].reshape(1, -1)
    width = round_up(north.shape[1], LANES)
    north = np.pad(north, ((0, 0), (0, width - north.shape[1])), constant_values=0.5 * np.pi)
    weight = np.pad(weight, ((0, 0), (0, width - weight.shape[1])))
    return (
        sine_places.reshape(-1).astype(np.float32),
        np.cos(north).astype(np.float32),
        weight,
        np.log(np.sin(north)).astype(np.float32),
        float(np.sum(np.sin(colat))),
    )


def log_starts(order_count):
    values = [
        0.5 * math.log((2.0 * m + 1.0) / (4.0 * math.pi))
        + 0.5 * (math.lgamma(m + 0.5) - math.lgamma(m + 1.0) - 0.5 * math.log(math.pi))
        for m in range(order_count)
    ]
    return np.asarray(values, np.float32)[:, None]


def spectral_kernel(
    sizes,
    field_ref,
    gain_ref,
    high_ref,
    low_ref,
    sine_ref,
    cosine_ref,
    weight_ref,
    logsine_ref,
    start_ref,
    out_ref,
    high,
    low,
    stage,
    field_high,
    field_low,
    turned,
    outgoing,
    landed,
    moments,
    moments_all,
    scales,
    table,
    prev_ref,
    early_ref,
    grow_ref,
    mant_ref,
    exp_ref,
    lines,
    sums,
    sums_out,
    blank,
    held,
    paired,
    landed_pair,
    spread_out,
    pair_sems,
    table_sem,
    stage_sem,
    moment_send,
    moment_recv,
    send_sem,
    recv_sem,
    local_sem,
    send_two,
    recv_two,
    blank_sem,
):
    count, band, longitudes, total_sine = sizes
    me = lax.axis_index("lat")
    part = lax.axis_index("parts")
    half = count // 2
    south = me // half
    slot_of_me = me + south * (half + count - 1 - 2 * me)
    groups = outgoing.shape[0] // CHUNKS
    places = groups * ROWS
    degrees = table.shape[1]
    kept = table.shape[2]
    width = cosine_ref.shape[1]
    block_rows = DEG_DEV * ROWS
    zero_owner = count - PLANE
    has_last = owns_last(me)

    def has_chunk(slot, device):
        return (slot < CHUNKS - 1) | owns_last(device)

    def table_copies(slot):
        return (
            pltpu.make_async_copy(high_ref.at[slot], high.at[slot], table_sem.at[0, slot]),
            pltpu.make_async_copy(low_ref.at[slot], low.at[slot], table_sem.at[1, slot]),
        )

    def row_copy(place):
        row = place + south * (band - 1 - 2 * place)
        at = place % ROWS
        return pltpu.make_async_copy(field_ref.at[row], stage.at[at], stage_sem.at[at])

    for place in range(2):
        row_copy(place).start()
    for copy in table_copies(0):
        copy.start()
    for place in range(2, ROWS):
        row_copy(place).start()
    for slot in range(1, CHUNKS):
        for copy in table_copies(slot):
            copy.start()

    barrier = pltpu.get_barrier_semaphore()

    @pl.loop(1, count)
    def _(step):
        pl.semaphore_signal(
            barrier, inc=1, device_id=(part, (me + step) % count), device_id_type=MESH
        )

    moments[...] = jnp.zeros_like(moments)
    for place in range(band, places):
        lanes = slice((place % 2) * LANES, (place % 2 + 1) * LANES)
        field_high[place // 2, :, lanes] = jnp.zeros((longitudes, LANES), jnp.bfloat16)
        field_low[place // 2, :, lanes] = jnp.zeros((longitudes, LANES), jnp.bfloat16)

    piece = longitudes // 6

    def split_row(place, lanes):
        at = place % ROWS
        pair = place // 2
        total = jnp.zeros((ROWS, LANES), jnp.float32)
        square = jnp.zeros((ROWS, LANES), jnp.float32)
        for first in range(0, longitudes, piece):
            value = stage[at, first : first + piece, :]
            top = value.astype(jnp.bfloat16)
            field_high[pair, first : first + piece, lanes] = top
            field_low[pair, first : first + piece, lanes] = (
                value - top.astype(jnp.float32)
            ).astype(jnp.bfloat16)
            total += jnp.sum(value.reshape(-1, ROWS, LANES), axis=0)
            square += jnp.sum((value * value).reshape(-1, ROWS, LANES), axis=0)
        sine = sine_ref[me * places + place]
        moments[:ROWS] += sine * total
        moments[ROWS:] += sine * square

    def take_row(place, lanes):
        row_copy(place).wait()
        split_row(place, lanes)

        @pl.when(place + ROWS < band)
        def _():
            row_copy(place + ROWS).start()

    def take_group(group):
        @pl.loop(0, ROWS // 2)
        def _(pair):
            place = group * ROWS + 2 * pair
            take_row(place, slice(0, LANES))

            @pl.when(place + 1 < band)
            def _():
                take_row(place + 1, slice(LANES, WIDE))

    halves = (slice(0, LANES), slice(LANES, WIDE))
    lines_of = count * ROWS

    def project(slot, at):
        product = jnp.dot(high[slot], field_high[at], preferred_element_type=jnp.float32)
        product += jnp.dot(high[slot], field_low[at], preferred_element_type=jnp.float32)
        product += jnp.dot(low[slot], field_high[at], preferred_element_type=jnp.float32)
        return product

    def turn(product, pair):
        for side in range(2):
            for row in range(2):
                turned[side, pl.ds(2 * pair + row, lines_of, stride=ROWS), :] = product[
                    side * lines_of : (side + 1) * lines_of, row * LANES : (row + 1) * LANES
                ]

    for row in range(2):
        take_row(row, halves[row])
    for copy in table_copies(0):
        copy.wait()
    for pair in range(ROWS // 2):
        following = range(2 * pair + 2, 2 * pair + 4) if pair + 1 < ROWS // 2 else ()
        for place in following:
            row_copy(place).wait()
        product = project(0, pair)
        for place in following:
            split_row(place, halves[place % 2])
        turn(product, pair)
        for place in following:
            if place + ROWS < band:
                row_copy(place + ROWS).start()
    pl.semaphore_wait(barrier, count - 1)

    def blank_copy(chunk, lines_off):
        rows = pl.ds(0, lines_off * ROWS)
        return pltpu.make_async_copy(
            blank.at[rows], out_ref.at[chunk, rows], blank_sem.at[chunk]
        )

    def moment_copy(device):
        return pltpu.make_async_remote_copy(
            moments,
            moments_all.at[me],
            moment_send,
            moment_recv,
            device_id=(part, device),
            device_id_type=MESH,
        )

    def order_copy(slot, group, device):
        step = slot * groups + group
        rows = pl.ds(pl.multiple_of(device * ROWS * ROWS, ROWS * ROWS), ROWS * ROWS)
        return pltpu.make_async_remote_copy(
            outgoing.at[step, rows],
            landed.at[slot, slot_of_me, group],
            send_sem.at[step],
            recv_sem.at[slot],
            device_id=(part, device),
            device_id_type=MESH,
        )

    def own_copy(slot, group):
        step = slot * groups + group
        rows = pl.ds(pl.multiple_of(me * ROWS * ROWS, ROWS * ROWS), ROWS * ROWS)
        return pltpu.make_async_copy(
            outgoing.at[step, rows], landed.at[slot, slot_of_me, group], local_sem.at[step]
        )

    short = ROWS * (ROWS - 1)

    def pair_copy(device):
        return pltpu.make_async_remote_copy(
            paired.at[device],
            landed_pair.at[slot_of_me],
            pair_sems.at[0],
            pair_sems.at[1],
            device_id=(part, device),
            device_id_type=MESH,
        )

    def own_pair():
        return pltpu.make_async_copy(
            paired.at[me], landed_pair.at[slot_of_me], pair_sems.at[2]
        )

    def fold_last():
        @pl.loop(0, count)
        def _(device):
            first = device * ROWS * ROWS
            for side in range(2):
                last = turned[side, pl.ds(pl.multiple_of(first + short, ROWS), ROWS), :]
                turned[side, pl.ds(first + ROWS - 1, ROWS, stride=ROWS), :] = last

    def send_pairs():
        @pl.loop(0, count)
        def _(ahead):
            device = (me + 1 + ahead) % count
            rows = pl.ds(pl.multiple_of(device * ROWS * ROWS, ROWS), short)
            paired[device] = jnp.concatenate(
                [
                    jnp.concatenate([source[0, rows, :], source[1, rows, :]], axis=1)
                    for source in (held, turned)
                ],
                axis=0,
            ).astype(jnp.bfloat16)

            @pl.when(device != me)
            def _():
                pair_copy(device).start()

            @pl.when(device == me)
            def _():
                own_pair().start()

    upper = count - count // PLANE

    def crosses(device):
        return (device >= upper) != (me >= upper)

    def transform(step):
        slot, group = step // groups, step % groups

        @pl.when(step == 1)
        def _():
            pl.loop(1, groups)(take_group)
            moments_all[me] = moments[...]

            @pl.loop(1, count)
            def _(ahead):
                moment_copy((me + ahead) % count).start()

        @pl.when((step == 2 * groups - 1) | (step == 2 * groups))
        def _():
            for copy in table_copies(slot):
                copy.wait()

        @pl.when(step > 0)
        def _():
            @pl.loop(0, ROWS // 2)
            def _(pair):
                turn(project(slot, group * (ROWS // 2) + pair), pair)

        @pl.when(slot == CHUNKS - 1)
        def _():
            at = zero_owner * ROWS * ROWS
            turned[0, at : at + ROWS, :] -= scales[1:2, :LANES]

        folded = (group == groups - 1) & (slot < CHUNKS - 1)

        @pl.when(jnp.logical_not(folded))
        def _():
            @pl.loop(0, count)
            def _(ahead):
                device = (me + 1 + ahead) % count
                rows = pl.ds(pl.multiple_of(device * ROWS * ROWS, ROWS * ROWS), ROWS * ROWS)
                outgoing[step, rows, :] = jnp.concatenate(
                    [turned[0, rows, :], turned[1, rows, :]], axis=1
                ).astype(jnp.bfloat16)

                @pl.when((device != me) & has_chunk(slot, device))
                def _():
                    order_copy(slot, group, device).start()

                @pl.when((device == me) & has_chunk(slot, device))
                def _():
                    own_copy(slot, group).start()

        @pl.when(folded)
        def _():
            fold_last()

            @pl.when(slot == 0)
            def _():
                held[...] = turned[...]

            @pl.when(slot > 0)
            def _():
                send_pairs()

    @pl.loop(0, groups + 2)
    def _(turn_at):
        tail = groups + (groups - 1) * (groups + 1 - turn_at)
        transform(jnp.where(turn_at < groups, turn_at, tail))

    blank[...] = jnp.zeros_like(blank)

    @pl.loop(0, out_ref.shape[0])
    def _(chunk):
        low_line = chunk * ROWS - me * DEG_DEV

        @pl.when(low_line >= DEG_DEV)
        def _():
            pltpu.make_async_copy(blank, out_ref.at[chunk], recv_two.at[chunk]).start()

        for lines_off in range(2, DEG_DEV, 2):

            @pl.when(low_line == lines_off)
            def _():
                blank_copy(chunk, lines_off).start()

    chunk_of = [owner_chunk(me, slot, count) for slot in range(CHUNKS)]
    lines_in = lax.broadcasted_iota(jnp.int32, (ROWS, width), 0)
    orders = jnp.concatenate(
        [(chunk * ROWS + lines_in).astype(jnp.float32) for chunk in chunk_of], axis=0
    )
    start = jnp.concatenate(
        [start_ref[pl.ds(pl.multiple_of(chunk * ROWS, ROWS), ROWS), :] for chunk in chunk_of], axis=0
    )
    start = jnp.broadcast_to(start, (CHUNKS * ROWS, width))

    def widen(value):
        return jnp.concatenate([value] * (width // LANES), axis=1)

    log_diag = start + orders * logsine_ref[...]
    start_exp = 64.0 * jnp.floor(log_diag / (64.0 * math.log(2.0)))
    exp_ref[...] = start_exp
    mant_ref[...] = jnp.exp(log_diag - start_exp * math.log(2.0))
    prev_ref[...] = jnp.zeros_like(prev_ref)
    early_ref[...] = jnp.zeros_like(early_ref)
    grow_ref[...] = jnp.zeros_like(grow_ref)
    order_lines = CHUNKS * ROWS

    @pl.loop(0, degrees // BLOCK)
    def _(block):
        narrow = orders[:, :LANES]
        order_sq = narrow * narrow
        cosine = cosine_ref[...]
        weights = weight_ref[...]
        limit = 2.0**64
        shrink = 2.0 ** (-64)
        previous, earlier, exponent = prev_ref[...], early_ref[...], grow_ref[...]
        first = (block * BLOCK).astype(jnp.float32)
        for step in range(BLOCK):
            degree = first + float(step)
            upper = jnp.sqrt(
                (4.0 * degree * degree - 1.0) / jnp.maximum(degree * degree - order_sq, 1.0)
            )
            below = degree - 1.0
            lower = jnp.sqrt(
                jnp.maximum(below * below - order_sq, 0.0)
                / jnp.maximum(jnp.full_like(order_sq, 4.0 * below * below - 1.0), 1.0)
            )
            recurred = widen(upper) * (cosine * previous - widen(lower) * earlier)
            at_start = orders == degree
            current = jnp.where(at_start, mant_ref[...], jnp.where(orders < degree, recurred, 0.0))
            exponent = jnp.where(at_start, exp_ref[...], exponent)
            value = weights * (current * jnp.exp2(exponent))
            for lane in range(width // LANES):
                lines[lane, step * order_lines : (step + 1) * order_lines, :] = value[
                    :, lane * LANES : (lane + 1) * LANES
                ]
            large = jnp.abs(current) > limit
            earlier = jnp.where(large, previous * shrink, previous)
            previous = jnp.where(large, current * shrink, current)
            exponent = jnp.where(large, exponent + 64.0, exponent)
        prev_ref[...] = previous
        early_ref[...] = earlier
        grow_ref[...] = exponent
        rows = pl.ds(pl.multiple_of(block * BLOCK, BLOCK), BLOCK)
        for order in range(order_lines):
            for lane in range(0, width, LANES):
                cut = min(LANES, kept - lane)
                part_of = lines[lane // LANES, pl.ds(order, BLOCK, stride=order_lines), :]
                table[order, rows, lane : lane + cut] = part_of[:, :cut].astype(table.dtype)

    def rows_from(device, lines_off):
        base = pl.multiple_of(device * block_rows + lines_off * ROWS, 2 * ROWS)
        return pl.ds(base, block_rows - lines_off * ROWS)

    def degree_copy(slot, device, lines_off=0):
        chunk = owner_chunk(me, slot, count)
        return pltpu.make_async_remote_copy(
            sums_out.at[slot, rows_from(device, lines_off)],
            out_ref.at[chunk, rows_from(0, lines_off)],
            send_two.at[slot, device],
            recv_two.at[chunk],
            device_id=(part, device),
            device_id_type=MESH,
        )

    def own_degrees(slot, lines_off=0):
        chunk = owner_chunk(me, slot, count)
        return pltpu.make_async_copy(
            sums_out.at[slot, rows_from(me, lines_off)],
            out_ref.at[chunk, rows_from(0, lines_off)],
            recv_two.at[chunk],
        )

    def each_target(slot, chosen, remote, local):
        first_line = owner_chunk(me, slot, count) * ROWS

        @pl.loop(1, count)
        def _(ahead):
            device = (me + ahead) % count

            @pl.when((first_line <= device * DEG_DEV) & chosen(device))
            def _():
                remote(slot, device, 0)

        @pl.when((first_line <= me * DEG_DEV) & chosen(me))
        def _():
            local(slot, 0)

        device = first_line // DEG_DEV
        for lines_off in range(2, DEG_DEV, 2):
            hit = (first_line - device * DEG_DEV == lines_off) & chosen(device)

            @pl.when(hit & (device != me))
            def _():
                remote(slot, device, lines_off)

            @pl.when(hit & (device == me))
            def _():
                local(slot, lines_off)

    def send_degrees(slot, chosen):
        each_target(
            slot,
            chosen,
            lambda *where: degree_copy(*where).start(),
            lambda *where: own_degrees(*where).start(),
        )

    degree_line = lax.broadcasted_iota(jnp.int32, (degrees, 1), 0)
    sign_even = jnp.where(degree_line % 2 == 0, 1.0, -1.0).astype(jnp.float32)

    def unfold():
        blocks = landed_pair.at[pl.ds(0, count - 1)]
        pltpu.make_async_copy(blocks, blocks, pair_sems.at[1]).wait()
        own_pair().wait()
        spread_out[...] = jnp.zeros_like(spread_out)

        @pl.loop(0, count)
        def _(source):
            value = landed_pair[source].astype(jnp.float32)
            for lane in range(2):
                spread_out[lane, : 2 * short, :] = value[:, lane * LANES : (lane + 1) * LANES]
            for slot in range(2):
                last = jnp.concatenate(
                    [
                        spread_out[lane, pl.ds(slot * short + ROWS - 1, ROWS, stride=ROWS), :]
                        for lane in range(2)
                    ],
                    axis=1,
                )
                landed[slot, source, groups - 1] = jnp.concatenate(
                    [value[slot * short : (slot + 1) * short], last], axis=0
                ).astype(landed.dtype)

    def analyse(slot):
        def wait_landed(parts):
            blocks = landed.at[slot, pl.ds(0, count - 1), pl.ds(0, parts)]
            pltpu.make_async_copy(blocks, blocks, recv_sem.at[slot]).wait()
            for group in range(parts):
                own_copy(slot, group).wait()

        @pl.when(slot < CHUNKS - 1)
        def _():
            wait_landed(groups - 1)

        @pl.when(slot == CHUNKS - 1)
        def _():
            wait_landed(groups)

        @pl.when(slot == 0)
        def _():
            unfold()

        @pl.loop(0, ROWS // 2)
        def _(pair):
            rows = pl.ds(pl.multiple_of(pair * 2 * ROWS, 2 * ROWS), 2 * ROWS)
            both = landed[slot, :, :, rows, :].astype(jnp.float32)
            both = both.reshape(count * groups, 2, ROWS, WIDE)
            for odd in range(2):
                rhs = both[:, odd].reshape(count * places, WIDE).astype(jnp.bfloat16)
                lhs = table[slot * ROWS + 2 * pair + odd]
                north = jnp.dot(lhs, rhs[:kept], preferred_element_type=jnp.float32)
                mirror = jnp.dot(lhs, rhs[kept:], preferred_element_type=jnp.float32)
                sign = sign_even if odd == 0 else -sign_even
                result = (north + sign * mirror) * scales[:1]
                for lane in range(2):
                    sums[lane, pl.ds(2 * pair + odd, degrees, stride=ROWS), :] = result[
                        :, lane * LANES : (lane + 1) * LANES
                    ]

        @pl.loop(0, count)
        def _(device):
            rows = pl.ds(pl.multiple_of(device * block_rows, block_rows), block_rows)
            sums_out[slot, rows, :] = jnp.concatenate(
                [sums[0, rows, :], sums[1, rows, :]], axis=1
            ).astype(jnp.bfloat16)

    pltpu.make_async_copy(
        moments_all.at[pl.ds(0, count - 1)],
        moments_all.at[pl.ds(0, count - 1)],
        moment_recv,
    ).wait()
    gathered = jnp.sum(moments_all[...], axis=0)
    first = jnp.sum(gathered[:ROWS], axis=0, keepdims=True) / (longitudes * total_sine)
    second = jnp.sum(gathered[ROWS:], axis=0, keepdims=True) / (longitudes * total_sine)
    spread = jnp.sqrt(second - first * first + 1e-05)
    gain = gain_ref[...]
    factor = jnp.concatenate([gain] * S, axis=1) / spread
    scales[:1] = jnp.concatenate([factor, factor], axis=1)
    scales[1:2] = jnp.concatenate([longitudes * first, jnp.zeros_like(first)], axis=1)

    @pl.loop(0, 2 * groups - 2)
    def _(turn_at):
        late = turn_at < groups - 2
        transform(jnp.where(late, turn_at + groups + 1, turn_at + groups + 2))

    @pl.loop(0, CHUNKS)
    def _(slot):
        @pl.when((slot < CHUNKS - 1) | has_last)
        def _():
            analyse(slot)
            send_degrees(slot, crosses)

        @pl.when((slot < CHUNKS - 1) | has_last)
        def _():
            send_degrees(slot, lambda device: jnp.logical_not(crosses(device)))

    pltpu.make_async_copy(
        moments_all.at[pl.ds(0, count - 1)], moments_all.at[pl.ds(0, count - 1)], moment_send
    ).wait()

    def wait_orders(step, devices):
        rows = pl.ds(0, devices * ROWS * ROWS)
        pltpu.make_async_copy(
            outgoing.at[step, rows], outgoing.at[step, rows], send_sem.at[step]
        ).wait()

    for slot in range(CHUNKS - 1):
        for group in range(groups - 1):
            wait_orders(slot * groups + group, count - 1)
    blocks = paired.at[pl.ds(0, count - 1)]
    pltpu.make_async_copy(blocks, blocks, pair_sems.at[0]).wait()

    last_owners = count - count // PLANE

    @pl.loop((CHUNKS - 1) * groups, CHUNKS * groups)
    def _(step):
        @pl.when(has_last)
        def _():
            wait_orders(step, last_owners - 1)

        @pl.when(jnp.logical_not(has_last))
        def _():
            wait_orders(step, last_owners)

    @pl.loop(0, CHUNKS)
    def _(slot):
        @pl.when(has_chunk(slot, me))
        def _():
            each_target(
                slot,
                lambda device: device >= 0,
                lambda *where: degree_copy(*where).wait_send(),
                lambda *where: None,
            )

    @pl.loop(0, out_ref.shape[0])
    def _(chunk):
        low_line = chunk * ROWS - me * DEG_DEV

        @pl.when((low_line <= 0) | (low_line >= DEG_DEV))
        def _():
            pltpu.make_async_copy(blank, out_ref.at[chunk], recv_two.at[chunk]).wait()

        for lines_off in range(2, DEG_DEV, 2):

            @pl.when(low_line == lines_off)
            def _():
                blank_copy(chunk, lines_off).wait()
                rows = rows_from(0, lines_off)
                pltpu.make_async_copy(
                    blank.at[rows], out_ref.at[chunk, rows], recv_two.at[chunk]
                ).wait()


def scratch_of(count, band, longitudes):
    groups = -(-band // ROWS)
    places = groups * ROWS
    degrees = DEG_DEV * count
    lines_of = count * ROWS
    kept = count // 2 * places
    width = round_up(kept, LANES)
    order_lines = CHUNKS * ROWS
    state = (order_lines, width)
    bf16, f32 = jnp.bfloat16, jnp.float32
    return [
        ((CHUNKS, 2 * lines_of, longitudes), bf16),
        ((CHUNKS, 2 * lines_of, longitudes), bf16),
        ((ROWS, longitudes, LANES), f32),
        ((places // 2, longitudes, WIDE), bf16),
        ((places // 2, longitudes, WIDE), bf16),
        ((2, lines_of * ROWS, LANES), f32),
        ((CHUNKS * groups, lines_of * ROWS, WIDE), bf16),
        ((CHUNKS, count, groups, ROWS * ROWS, WIDE), bf16),
        ((2 * ROWS, LANES), f32),
        ((count, 2 * ROWS, LANES), f32),
        ((ROWS, WIDE), f32),
        ((order_lines, degrees, kept), bf16),
        (state, f32),
        (state, f32),
        (state, f32),
        (state, f32),
        (state, f32),
        ((width // LANES, BLOCK * order_lines, LANES), f32),
        ((2, degrees * ROWS, LANES), f32),
        ((CHUNKS, degrees * ROWS, WIDE), bf16),
        ((DEG_DEV * ROWS, WIDE), bf16),
        ((2, lines_of * ROWS, LANES), f32),
        ((count, 2 * ROWS * (ROWS - 1), WIDE), bf16),
        ((count, 2 * ROWS * (ROWS - 1), WIDE), bf16),
        ((2, 2 * ROWS * ROWS, LANES), f32),
    ]


def scratch_bytes(shapes):
    total = 0
    for shape, dtype in shapes:
        size = math.prod(shape[:-1]) * round_up(shape[-1], LANES)
        total += size * jnp.dtype(dtype).itemsize
    return total


def coefficients_of(grid_field, norm_gain, count):
    band, longitudes, columns = grid_field.shape
    groups = -(-band // ROWS)
    places = groups * ROWS
    order_count = DEG_DEV * count
    high, low = transform_tables(count, longitudes)
    sine, cosine, weight, logsine, total_sine = angle_tables(count, band, places)
    weight_scale = math.pi**1.5 / math.sqrt(count * band * longitudes)
    shapes = scratch_of(count, band, longitudes)
    dma = pltpu.SemaphoreType.DMA
    vmem = pl.BlockSpec(memory_space=pltpu.VMEM)
    anywhere = pl.BlockSpec(memory_space=pl.ANY)
    return pl.pallas_call(
        functools.partial(spectral_kernel, (count, band, longitudes, total_sine)),
        out_shape=jax.ShapeDtypeStruct((order_count // ROWS, DEG_DEV * ROWS, WIDE), jnp.bfloat16),
        in_specs=[
            anywhere,
            vmem,
            anywhere,
            anywhere,
            pl.BlockSpec(memory_space=pltpu.SMEM),
            vmem,
            vmem,
            vmem,
            vmem,
        ],
        out_specs=anywhere,
        scratch_shapes=[pltpu.VMEM(shape, dtype) for shape, dtype in shapes]
        + [
            dma((3,)),
            dma((2, CHUNKS)),
            dma((ROWS,)),
            dma,
            dma,
            dma((CHUNKS * groups,)),
            dma((CHUNKS,)),
            dma((CHUNKS * groups,)),
            dma((CHUNKS, count)),
            dma((order_count // ROWS,)),
            dma((order_count // ROWS,)),
        ],
        cost_estimate=pl.CostEstimate(
            flops=20 * 10**9, bytes_accessed=40 * 10**6, transcendentals=10**6
        ),
        compiler_params=pltpu.CompilerParams(
            collective_id=0, has_side_effects=True, vmem_limit_bytes=VMEM_CAP
        ),
    )(
        grid_field,
        norm_gain[None, :],
        jnp.asarray(high),
        jnp.asarray(low),
        jnp.asarray(sine),
        jnp.asarray(cosine),
        jnp.asarray((weight * weight_scale).astype(np.float32)),
        jnp.asarray(logsine),
        jnp.asarray(log_starts(order_count)),
    )


def filter_kernel(coef_ref, weight_ref, out_ref, coefs, outs, full_ref, in_sem, out_sem):
    pairs = coefs.shape[0]
    chunks = coefs.shape[1]
    orders = chunks * ROWS

    def fetch(pair):
        rows = pl.ds(pl.multiple_of(pair * 2 * ROWS, 2 * ROWS), 2 * ROWS)
        return pltpu.make_async_copy(coef_ref.at[:, rows, :], coefs.at[pair], in_sem.at[pair])

    def store(pair):
        return pltpu.make_async_copy(
            outs.at[pair], out_ref.at[pl.ds(2 * pair, 2)], out_sem.at[pair]
        )

    for pair in range(pairs):
        fetch(pair).start()

    full_ref[...] = jnp.zeros_like(full_ref)
    for pair in range(pairs):
        for odd in range(2):
            degree = 2 * pair + odd
            real, imag = weight_ref[degree, 0], weight_ref[degree, 1]
            for sample in range(S):
                for side, halves in enumerate(((real, imag), (-imag, real))):
                    for target, block in enumerate(halves):
                        row = side * S * C + sample * C
                        lane = target * S * C + sample * C
                        full_ref[degree, row : row + C, lane : lane + C] = block
        fetch(pair).wait()
        both = coefs[pair].astype(jnp.float32).reshape(chunks, 2, ROWS, WIDE)
        for odd in range(2):
            value = both[:, odd].reshape(orders, WIDE).astype(jnp.bfloat16)
            outs[pair, odd] = jnp.dot(
                value, full_ref[2 * pair + odd], preferred_element_type=jnp.float32
            ).astype(outs.dtype)
        store(pair).start()

    @pl.loop(0, pairs)
    def _(pair):
        store(pair).wait()


def apply_filter(coefficients, filter_weight):
    chunks = coefficients.shape[0]
    degrees = filter_weight.shape[0]
    pairs = degrees // 2
    orders = chunks * ROWS
    anywhere = pl.BlockSpec(memory_space=pl.ANY)
    return pl.pallas_call(
        filter_kernel,
        out_shape=jax.ShapeDtypeStruct((degrees, orders, WIDE), jnp.bfloat16),
        in_specs=[anywhere, pl.BlockSpec(memory_space=pltpu.VMEM)],
        out_specs=anywhere,
        scratch_shapes=[
            pltpu.VMEM((pairs, chunks, 2 * ROWS, WIDE), jnp.bfloat16),
            pltpu.VMEM((pairs, 2, orders, WIDE), jnp.bfloat16),
            pltpu.VMEM((degrees, WIDE, WIDE), jnp.bfloat16),
            pltpu.SemaphoreType.DMA((pairs,)),
            pltpu.SemaphoreType.DMA((pairs,)),
        ],
        compiler_params=pltpu.CompilerParams(vmem_limit_bytes=VMEM_CAP),
    )(coefficients, filter_weight)


def body(grid_field, norm_gain, filter_weight):
    count = lax.axis_size("lat")
    band, longitudes, columns = grid_field.shape
    fits = scratch_bytes(scratch_of(count, band, longitudes)) < VMEM_CAP - 3 * 1024 * 1024
    if count % PLANE or band % ROWS != ROWS - 1 or band < 2 * ROWS or not fits:
        return plain_body(grid_field, norm_gain, filter_weight)
    coefficients = coefficients_of(grid_field, norm_gain, count)
    return apply_filter(coefficients, filter_weight)


def solution(mesh):
    in_specs = (P("lat", None, "parts"), P("parts"), P("lat", None, None, "parts"))
    out_specs = P("lat", None, "parts")
    return jax.shard_map(body, mesh=mesh, in_specs=in_specs, out_specs=out_specs, check_vma=False)
```

```python
import functools
import math

import jax
import jax.numpy as jnp
import numpy as np
from jax import lax
from jax.experimental import pallas as pl
from jax.experimental.pallas import tpu as pltpu
from jax.sharding import PartitionSpec as P

C = 64
S = 2
DEG_DEV = 22
ORDER_PAD = 24
BLOCK = 16
LANES = 128


def round_up(value, step):
    return -(-value // step) * step


def legendre_kernel(
    orders_ref, cosine_ref, weights_ref, mant_ref, exp_ref, out_ref, prev_ref, early_ref, grow_ref, rows_ref
):
    block = pl.program_id(0)
    width = cosine_ref.shape[1]
    kept_width = out_ref.shape[2]

    @pl.when(block == 0)
    def _():
        prev_ref[...] = jnp.zeros_like(prev_ref)
        early_ref[...] = jnp.zeros_like(early_ref)
        grow_ref[...] = jnp.zeros_like(grow_ref)

    orders = orders_ref[...]
    narrow = orders[:, :LANES]
    order_sq = narrow * narrow
    cosine = cosine_ref[...]
    weights = weights_ref[...]
    limit = 2.0**64
    shrink = 2.0 ** (-64)
    previous, earlier, exponent = prev_ref[...], early_ref[...], grow_ref[...]
    first = (block * BLOCK).astype(jnp.float32)

    def widen(value):
        return jnp.concatenate([value] * (width // LANES), axis=1)

    for step in range(BLOCK):
        degree = first + float(step)
        upper = jnp.sqrt(
            (4.0 * degree * degree - 1.0) / jnp.maximum(degree * degree - order_sq, 1.0)
        )
        below = degree - 1.0
        lower = jnp.sqrt(
            jnp.maximum(below * below - order_sq, 0.0)
            / jnp.maximum(jnp.full_like(order_sq, 4.0 * below * below - 1.0), 1.0)
        )
        recurred = widen(upper) * (cosine * previous - widen(lower) * earlier)
        at_start = orders == degree
        current = jnp.where(at_start, mant_ref[...], jnp.where(orders < degree, recurred, 0.0))
        exponent = jnp.where(at_start, exp_ref[...], exponent)
        value = weights * (current * jnp.exp2(exponent))
        for lane in range(width // LANES):
            rows_ref[lane, step * ORDER_PAD : (step + 1) * ORDER_PAD, :] = value[
                :, lane * LANES : (lane + 1) * LANES
            ]
        large = jnp.abs(current) > limit
        earlier = jnp.where(large, previous * shrink, previous)
        previous = jnp.where(large, current * shrink, current)
        exponent = jnp.where(large, exponent + 64.0, exponent)

    prev_ref[...] = previous
    early_ref[...] = earlier
    grow_ref[...] = exponent
    for order in range(DEG_DEV):
        for lane in range(0, width, LANES):
            cut = min(LANES, kept_width - lane)
            piece = rows_ref[lane // LANES, pl.ds(order, BLOCK, stride=ORDER_PAD), :]
            out_ref[order, :, lane : lane + cut] = piece[:, :cut].astype(out_ref.dtype)


def legendre_table(colatitude, first_order, degrees, weight_scale):
    rows = colatitude.shape[0]
    width = round_up(rows, LANES)
    colat = jnp.concatenate([colatitude, jnp.full((width - rows,), 0.5 * math.pi, jnp.float32)])
    orders = (first_order + jnp.arange(ORDER_PAD, dtype=jnp.int32)).astype(jnp.float32)
    sine_rows = jnp.sin(colat)
    log_start = 0.5 * jnp.log((2.0 * orders + 1.0) / (4.0 * math.pi)) + 0.5 * (
        lax.lgamma(orders + 0.5) - lax.lgamma(orders + 1.0) - 0.5 * math.log(math.pi)
    )
    log_diag = log_start[:, None] + orders[:, None] * jnp.log(sine_rows)[None, :]
    start_exp = 64.0 * jnp.floor(log_diag / (64.0 * math.log(2.0)))
    start_mant = jnp.exp(log_diag - start_exp * math.log(2.0))
    state = (ORDER_PAD, width)
    whole = pl.BlockSpec(state, lambda i: (0, 0))
    line = pl.BlockSpec((1, width), lambda i: (0, 0))
    return pl.pallas_call(
        legendre_kernel,
        grid=(degrees // BLOCK,),
        out_shape=jax.ShapeDtypeStruct((DEG_DEV, degrees, rows), jnp.bfloat16),
        in_specs=[whole, line, line, whole, whole],
        out_specs=pl.BlockSpec((DEG_DEV, BLOCK, rows), lambda i: (0, i, 0)),
        scratch_shapes=[
            pltpu.VMEM(state, jnp.float32),
            pltpu.VMEM(state, jnp.float32),
            pltpu.VMEM(state, jnp.float32),
            pltpu.VMEM((width // LANES, BLOCK * ORDER_PAD, LANES), jnp.float32),
        ],
        cost_estimate=pl.CostEstimate(
            flops=degrees * ORDER_PAD * width * 2000,
            bytes_accessed=DEG_DEV * degrees * rows * 2,
            transcendentals=degrees * ORDER_PAD * width,
        ),
        compiler_params=pltpu.CompilerParams(vmem_limit_bytes=24 * 1024 * 1024),
    )(
        jnp.broadcast_to(orders[:, None], state),
        jnp.cos(colat)[None, :],
        (weight_scale * sine_rows)[None, :],
        start_mant,
        start_exp,
    )


def expand_filter(filter_weight):
    real_part = filter_weight[:, 0]
    imag_part = filter_weight[:, 1]
    from_real = jnp.stack([real_part, imag_part], axis=1)
    from_imag = jnp.stack([-imag_part, real_part], axis=1)
    mixing = jnp.stack([from_real, from_imag], axis=1)
    same = jnp.eye(S, dtype=filter_weight.dtype)
    full = mixing.transpose(0, 1, 3, 2, 4)[:, :, None, :, :, None, :] * same[None, None, :, None, None, :, None]
    return full.reshape(filter_weight.shape[0], 2 * S * C, 2 * S * C)


def mix_kernel(sin_ref, cos_ref, weight_ref, out_ref, rows_ref):
    sources, degrees, orders, half = cos_ref.shape
    for degree in range(degrees):
        for source in range(sources):
            rows = slice(source * orders, (source + 1) * orders)
            rows_ref[degree, rows, :half] = cos_ref[source, degree].astype(jnp.float32)
            rows_ref[degree, rows, half:] = sin_ref[source, degree].astype(jnp.float32)
        out_ref[degree] = jnp.dot(
            rows_ref[degree].astype(jnp.bfloat16),
            weight_ref[degree],
            preferred_element_type=jnp.float32,
        ).astype(out_ref.dtype)


def mix(coef_sin, coef_cos, weights):
    sources, degrees, orders, half = coef_cos.shape
    wide = weights.shape[2]
    step = 2
    piece = pl.BlockSpec((sources, step, orders, half), lambda i: (0, i, 0, 0))
    return pl.pallas_call(
        mix_kernel,
        grid=(degrees // step,),
        out_shape=jax.ShapeDtypeStruct((degrees, sources * orders, wide), jnp.bfloat16),
        in_specs=[piece, piece, pl.BlockSpec((step, 2 * half, wide), lambda i: (i, 0, 0))],
        out_specs=pl.BlockSpec((step, sources * orders, wide), lambda i: (i, 0, 0)),
        scratch_shapes=[pltpu.VMEM((step, sources * orders, 2 * half), jnp.float32)],
        compiler_params=pltpu.CompilerParams(vmem_limit_bytes=24 * 1024 * 1024),
    )(coef_sin, coef_cos, weights)


def fourier_matrix(orders, longitudes):
    phases = (np.arange(orders)[:, None] * np.arange(longitudes)[None, :]) % longitudes
    angles = 2.0 * np.pi * phases / longitudes
    return np.stack([np.cos(angles), -np.sin(angles)]).astype(np.float32)


def plain_body(grid_field, norm_gain, filter_weight):
    device_index = lax.axis_index("lat")
    lat_count = lax.axis_size("lat")
    band_rows, longitudes, columns = grid_field.shape
    total_lat = band_rows * lat_count
    order_count = DEG_DEV * lat_count
    all_rows = jnp.arange(total_lat, dtype=jnp.int32)
    colat_all = math.pi * (all_rows.astype(jnp.float32) + 0.5) / total_lat
    sine_all = jnp.sin(colat_all)
    own_rows = device_index * band_rows + jnp.arange(band_rows, dtype=jnp.int32)
    sine_own = jnp.sin(math.pi * (own_rows.astype(jnp.float32) + 0.5) / total_lat)

    first = jnp.einsum("j,jnx->x", sine_own, grid_field, precision=lax.Precision.HIGHEST)
    second = jnp.einsum(
        "j,jnx->x", sine_own, grid_field * grid_field, precision=lax.Precision.HIGHEST
    )
    band_mean = first / (longitudes * jnp.sum(sine_own))
    denominator_rows = jnp.float32(longitudes)
    cos_table, sin_table = fourier_matrix(order_count, longitudes)

    def transform(table):
        return jnp.einsum(
            "mn,jnx->mjx", jnp.asarray(table), grid_field, precision=lax.Precision.HIGH
        )

    def to_orders(raw):
        return lax.all_to_all(
            raw.astype(jnp.bfloat16), "lat", split_axis=0, concat_axis=1, tiled=True
        )

    def to_degrees(sums):
        return lax.all_to_all(
            sums, "lat", split_axis=0, concat_axis=0
        )

    received_sin = to_orders(transform(sin_table))
    constant = jnp.arange(order_count) == 0
    shift = jnp.where(constant[:, None, None], denominator_rows * band_mean, 0.0)
    received_cos = to_orders(transform(cos_table) - shift)

    weight_scale = math.pi**1.5 / math.sqrt(total_lat * longitudes)
    legendre = legendre_table(colat_all, device_index * DEG_DEV, order_count, weight_scale)

    def analyse(received):
        return jnp.einsum("mlj,mjx->mlx", legendre, received, preferred_element_type=jnp.float32)

    def by_degree(sums):
        ordered = sums.astype(jnp.bfloat16).transpose(1, 0, 2)
        return ordered.reshape(lat_count, DEG_DEV, DEG_DEV, columns)

    sums_sin = by_degree(analyse(received_sin))
    moments, sums_sin = lax.optimization_barrier(
        (jnp.stack([first, second, band_mean]), sums_sin)
    )
    gathered, sums_sin = lax.optimization_barrier((lax.all_gather(moments, "lat"), sums_sin))
    denominator = longitudes * jnp.sum(sine_all)
    average = jnp.sum(gathered[:, 0], axis=0) / denominator
    mean_square = jnp.sum(gathered[:, 1], axis=0) / denominator
    spread = jnp.sqrt(mean_square - average * average + 1e-05)
    factor = jnp.tile(norm_gain, S) / spread
    coef_sin = to_degrees(sums_sin)
    band_sums = jnp.sum(
        legendre[0].astype(jnp.float32).reshape(order_count, lat_count, band_rows), axis=2
    )
    level = jnp.dot(
        band_sums,
        denominator_rows * (gathered[:, 2] - average),
        precision=lax.Precision.HIGHEST,
    )
    here = (device_index == 0) & (jnp.arange(DEG_DEV) == 0)
    coef_cos = to_degrees(
        by_degree(analyse(received_cos) + jnp.where(here[:, None, None], level[None], 0.0))
    )

    expanded = expand_filter(filter_weight)
    expanded = (expanded * jnp.tile(factor, 2)[None, :, None]).astype(jnp.bfloat16)

    return mix(coef_sin, coef_cos, expanded)


MESH = pl.DeviceIdType.MESH
ROWS = 8
WIDE = 2 * LANES
CHUNKS = 3
PLANE = 4
PLANE_CHUNKS = PLANE * CHUNKS - 1
VMEM_CAP = 60 * 1024 * 1024


def owns_last(device):
    return device % PLANE != 1


def owner_chunk(device, slot, count):
    plane, inner = count // PLANE - 1 - device // PLANE, device % PLANE
    first = 1 // (plane + inner + 1)
    at = slot + first * (CHUNKS - 1 - 2 * slot)
    return PLANE_CHUNKS * plane + PLANE * at + inner - (at // (CHUNKS - 1)) * ((inner + 2) // PLANE)


def transform_tables(count, longitudes):
    table = np.zeros((CHUNKS, 2, count, ROWS, longitudes), np.float64)
    for slot in range(CHUNKS):
        for device in range(count):
            if slot == CHUNKS - 1 and not owns_last(device):
                continue
            orders = owner_chunk(device, slot, count) * ROWS + np.arange(ROWS)
            phases = (orders[:, None] * np.arange(longitudes)[None, :]) % longitudes
            angles = 2.0 * np.pi * phases / longitudes
            table[slot, 0, device] = np.cos(angles)
            table[slot, 1, device] = -np.sin(angles)
    table = table.reshape(CHUNKS, 2 * count * ROWS, longitudes).astype(np.float32)
    high = table.astype(jnp.bfloat16)
    low = (table - high.astype(np.float32)).astype(jnp.bfloat16)
    return high, low


def angle_tables(count, band, places):
    colat = np.pi * (np.arange(count * band) + 0.5) / (count * band)
    by_place = np.full((count, places), 0.5 * np.pi)
    valid = np.zeros((count, places))
    for device in range(count):
        rows = colat[device * band : (device + 1) * band]
        by_place[device, :band] = rows if device < count // 2 else rows[::-1]
        valid[device, :band] = 1.0
    sine_places = np.sin(by_place) * valid
    north = by_place[: count // 2].reshape(1, -1)
    weight = sine_places[: count // 2].reshape(1, -1)
    width = round_up(north.shape[1], LANES)
    north = np.pad(north, ((0, 0), (0, width - north.shape[1])), constant_values=0.5 * np.pi)
    weight = np.pad(weight, ((0, 0), (0, width - weight.shape[1])))
    return (
        sine_places.reshape(-1).astype(np.float32),
        np.cos(north).astype(np.float32),
        weight,
        np.log(np.sin(north)).astype(np.float32),
        float(np.sum(np.sin(colat))),
    )


def log_starts(order_count):
    values = [
        0.5 * math.log((2.0 * m + 1.0) / (4.0 * math.pi))
        + 0.5 * (math.lgamma(m + 0.5) - math.lgamma(m + 1.0) - 0.5 * math.log(math.pi))
        for m in range(order_count)
    ]
    return np.asarray(values, np.float32)[:, None]


def spectral_kernel(
    sizes,
    field_ref,
    gain_ref,
    high_ref,
    low_ref,
    sine_ref,
    cosine_ref,
    weight_ref,
    logsine_ref,
    start_ref,
    out_ref,
    high,
    low,
    stage,
    field_high,
    field_low,
    turned,
    outgoing,
    landed,
    moments,
    moments_all,
    scales,
    table,
    prev_ref,
    early_ref,
    grow_ref,
    mant_ref,
    exp_ref,
    lines,
    sums,
    sums_out,
    blank,
    held,
    paired,
    landed_pair,
    spread_out,
    pair_sems,
    table_sem,
    stage_sem,
    moment_send,
    moment_recv,
    send_sem,
    recv_sem,
    local_sem,
    send_two,
    recv_two,
    blank_sem,
):
    count, band, longitudes, total_sine = sizes
    me = lax.axis_index("lat")
    part = lax.axis_index("parts")
    half = count // 2
    south = me // half
    slot_of_me = me + south * (half + count - 1 - 2 * me)
    groups = outgoing.shape[0] // CHUNKS
    places = groups * ROWS
    degrees = table.shape[1]
    kept = table.shape[2]
    width = cosine_ref.shape[1]
    block_rows = DEG_DEV * ROWS
    zero_owner = count - PLANE
    has_last = owns_last(me)

    def has_chunk(slot, device):
        return (slot < CHUNKS - 1) | owns_last(device)

    def table_copies(slot):
        return (
            pltpu.make_async_copy(high_ref.at[slot], high.at[slot], table_sem.at[0, slot]),
            pltpu.make_async_copy(low_ref.at[slot], low.at[slot], table_sem.at[1, slot]),
        )

    def row_copy(place):
        row = place + south * (band - 1 - 2 * place)
        at = place % ROWS
        return pltpu.make_async_copy(field_ref.at[row], stage.at[at], stage_sem.at[at])

    for place in range(2):
        row_copy(place).start()
    for copy in table_copies(0):
        copy.start()
    for place in range(2, ROWS):
        row_copy(place).start()
    for slot in range(1, CHUNKS):
        for copy in table_copies(slot):
            copy.start()

    barrier = pltpu.get_barrier_semaphore()

    @pl.loop(1, count)
    def _(step):
        pl.semaphore_signal(
            barrier, inc=1, device_id=(part, (me + step) % count), device_id_type=MESH
        )

    moments[...] = jnp.zeros_like(moments)
    for place in range(band, places):
        lanes = slice((place % 2) * LANES, (place % 2 + 1) * LANES)
        field_high[place // 2, :, lanes] = jnp.zeros((longitudes, LANES), jnp.bfloat16)
        field_low[place // 2, :, lanes] = jnp.zeros((longitudes, LANES), jnp.bfloat16)

    piece = longitudes // 6

    def split_row(place, lanes):
        at = place % ROWS
        pair = place // 2
        total = jnp.zeros((ROWS, LANES), jnp.float32)
        square = jnp.zeros((ROWS, LANES), jnp.float32)
        for first in range(0, longitudes, piece):
            value = stage[at, first : first + piece, :]
            top = value.astype(jnp.bfloat16)
            field_high[pair, first : first + piece, lanes] = top
            field_low[pair, first : first + piece, lanes] = (
                value - top.astype(jnp.float32)
            ).astype(jnp.bfloat16)
            total += jnp.sum(value.reshape(-1, ROWS, LANES), axis=0)
            square += jnp.sum((value * value).reshape(-1, ROWS, LANES), axis=0)
        sine = sine_ref[me * places + place]
        moments[:ROWS] += sine * total
        moments[ROWS:] += sine * square

    def take_row(place, lanes):
        row_copy(place).wait()
        split_row(place, lanes)

        @pl.when(place + ROWS < band)
        def _():
            row_copy(place + ROWS).start()

    def take_group(group):
        @pl.loop(0, ROWS // 2)
        def _(pair):
            place = group * ROWS + 2 * pair
            take_row(place, slice(0, LANES))

            @pl.when(place + 1 < band)
            def _():
                take_row(place + 1, slice(LANES, WIDE))

    halves = (slice(0, LANES), slice(LANES, WIDE))
    lines_of = count * ROWS

    def project(slot, at):
        product = jnp.dot(high[slot], field_high[at], preferred_element_type=jnp.float32)
        product += jnp.dot(high[slot], field_low[at], preferred_element_type=jnp.float32)
        product += jnp.dot(low[slot], field_high[at], preferred_element_type=jnp.float32)
        return product

    def turn(product, pair):
        for side in range(2):
            for row in range(2):
                turned[side, pl.ds(2 * pair + row, lines_of, stride=ROWS), :] = product[
                    side * lines_of : (side + 1) * lines_of, row * LANES : (row + 1) * LANES
                ]


    def blank_copy(chunk, lines_off):
        rows = pl.ds(0, lines_off * ROWS)
        return pltpu.make_async_copy(
            blank.at[rows], out_ref.at[chunk, rows], blank_sem.at[chunk]
        )

    def moment_copy(device):
        return pltpu.make_async_remote_copy(
            moments,
            moments_all.at[me],
            moment_send,
            moment_recv,
            device_id=(part, device),
            device_id_type=MESH,
        )

    def order_copy(slot, group, device):
        step = slot * groups + group
        rows = pl.ds(pl.multiple_of(device * ROWS * ROWS, ROWS * ROWS), ROWS * ROWS)
        return pltpu.make_async_remote_copy(
            outgoing.at[step, rows],
            landed.at[slot, slot_of_me, group],
            send_sem.at[step],
            recv_sem.at[slot],
            device_id=(part, device),
            device_id_type=MESH,
        )

    def own_copy(slot, group):
        step = slot * groups + group
        rows = pl.ds(pl.multiple_of(me * ROWS * ROWS, ROWS * ROWS), ROWS * ROWS)
        return pltpu.make_async_copy(
            outgoing.at[step, rows], landed.at[slot, slot_of_me, group], local_sem.at[step]
        )

    short = ROWS * (ROWS - 1)

    def pair_copy(device):
        return pltpu.make_async_remote_copy(
            paired.at[device],
            landed_pair.at[slot_of_me],
            pair_sems.at[0],
            pair_sems.at[1],
            device_id=(part, device),
            device_id_type=MESH,
        )

    def own_pair():
        return pltpu.make_async_copy(
            paired.at[me], landed_pair.at[slot_of_me], pair_sems.at[2]
        )

    def fold_last():
        @pl.loop(0, count)
        def _(device):
            first = device * ROWS * ROWS
            for side in range(2):
                last = turned[side, pl.ds(pl.multiple_of(first + short, ROWS), ROWS), :]
                turned[side, pl.ds(first + ROWS - 1, ROWS, stride=ROWS), :] = last

    def send_pairs():
        @pl.loop(0, count)
        def _(ahead):
            device = ((me // half + 1 + ahead // half) % 2) * half + (me + ahead) % half
            rows = pl.ds(pl.multiple_of(device * ROWS * ROWS, ROWS), short)
            paired[device] = jnp.concatenate(
                [
                    jnp.concatenate([source[0, rows, :], source[1, rows, :]], axis=1)
                    for source in (held, turned)
                ],
                axis=0,
            ).astype(jnp.bfloat16)

            @pl.when(device != me)
            def _():
                pair_copy(device).start()

            @pl.when(device == me)
            def _():
                own_pair().start()

    upper = count - count // PLANE

    def crosses(device):
        return (device >= upper) != (me >= upper)

    def send_group(slot, group, first, last):
        @pl.loop(first, last)
        def _(ahead):
            device = ((me // half + 1 + ahead // half) % 2) * half + (me + ahead) % half
            rows = pl.ds(pl.multiple_of(device * ROWS * ROWS, ROWS * ROWS), ROWS * ROWS)
            outgoing[slot * groups + group, rows, :] = jnp.concatenate(
                [turned[0, rows, :], turned[1, rows, :]], axis=1
            ).astype(jnp.bfloat16)

            @pl.when((device != me) & has_chunk(slot, device))
            def _():
                order_copy(slot, group, device).start()

            @pl.when((device == me) & has_chunk(slot, device))
            def _():
                own_copy(slot, group).start()

    def project_half(pair, part_of):
        lines_half = half * ROWS
        rows = [
            pl.ds(pl.multiple_of(side * lines_of + part_of * lines_half, lines_half), lines_half)
            for side in range(2)
        ]
        top = jnp.concatenate([high[0, row, :] for row in rows], axis=0)
        rest = jnp.concatenate([low[0, row, :] for row in rows], axis=0)
        product = jnp.dot(top, field_high[pair], preferred_element_type=jnp.float32)
        product += jnp.dot(top, field_low[pair], preferred_element_type=jnp.float32)
        product += jnp.dot(rest, field_high[pair], preferred_element_type=jnp.float32)
        return product

    def turn_half(product, pair, part_of):
        lines_half = half * ROWS
        for side in range(2):
            for row in range(2):
                at = part_of * lines_half * ROWS + 2 * pair + row
                turned[side, pl.ds(at, lines_half, stride=ROWS), :] = product[
                    side * lines_half : (side + 1) * lines_half, row * LANES : (row + 1) * LANES
                ]

    for row in range(2):
        take_row(row, halves[row])
    for copy in table_copies(0):
        copy.wait()
    other = (me // half + 1) % 2
    for pair in range(ROWS // 2):
        following = range(2 * pair + 2, 2 * pair + 4) if pair + 1 < ROWS // 2 else ()
        for place in following:
            row_copy(place).wait()
        product = project_half(pair, other)
        for place in following:
            split_row(place, halves[place % 2])
        turn_half(product, pair, other)
        for place in following:
            if place + ROWS < band:
                row_copy(place + ROWS).start()
    pl.semaphore_wait(barrier, count - 1)
    send_group(0, 0, 0, half)

    @pl.loop(0, ROWS // 2)
    def _(pair):
        turn_half(project_half(pair, 1 - other), pair, 1 - other)

    send_group(0, 0, half, count)

    def transform(step):
        slot, group = step // groups, step % groups

        @pl.when(step == 1)
        def _():
            pl.loop(1, groups)(take_group)
            moments_all[me] = moments[...]

            @pl.loop(1, count)
            def _(ahead):
                moment_copy((me + ahead) % count).start()

        @pl.when((step == 2 * groups - 1) | (step == 2 * groups))
        def _():
            for copy in table_copies(slot):
                copy.wait()

        @pl.loop(0, ROWS // 2)
        def _(pair):
            turn(project(slot, group * (ROWS // 2) + pair), pair)

        @pl.when(slot == CHUNKS - 1)
        def _():
            at = zero_owner * ROWS * ROWS
            turned[0, at : at + ROWS, :] -= scales[1:2, :LANES]

        folded = (group == groups - 1) & (slot < CHUNKS - 1)

        @pl.when(jnp.logical_not(folded))
        def _():
            send_group(slot, group, 0, count)

        @pl.when(folded)
        def _():
            fold_last()

            @pl.when(slot == 0)
            def _():
                held[...] = turned[...]

            @pl.when(slot > 0)
            def _():
                send_pairs()

    @pl.loop(1, groups + 2)
    def _(turn_at):
        tail = groups + (groups - 1) * (groups + 1 - turn_at)
        transform(jnp.where(turn_at < groups, turn_at, tail))

    blank[...] = jnp.zeros_like(blank)

    @pl.loop(0, out_ref.shape[0])
    def _(chunk):
        low_line = chunk * ROWS - me * DEG_DEV

        @pl.when(low_line >= DEG_DEV)
        def _():
            pltpu.make_async_copy(blank, out_ref.at[chunk], recv_two.at[chunk]).start()

        for lines_off in range(2, DEG_DEV, 2):

            @pl.when(low_line == lines_off)
            def _():
                blank_copy(chunk, lines_off).start()

    chunk_of = [owner_chunk(me, slot, count) for slot in range(CHUNKS)]
    lines_in = lax.broadcasted_iota(jnp.int32, (ROWS, width), 0)
    orders = jnp.concatenate(
        [(chunk * ROWS + lines_in).astype(jnp.float32) for chunk in chunk_of], axis=0
    )
    start = jnp.concatenate(
        [start_ref[pl.ds(pl.multiple_of(chunk * ROWS, ROWS), ROWS), :] for chunk in chunk_of], axis=0
    )
    start = jnp.broadcast_to(start, (CHUNKS * ROWS, width))

    def widen(value):
        return jnp.concatenate([value] * (width // LANES), axis=1)

    log_diag = start + orders * logsine_ref[...]
    start_exp = 64.0 * jnp.floor(log_diag / (64.0 * math.log(2.0)))
    exp_ref[...] = start_exp
    mant_ref[...] = jnp.exp(log_diag - start_exp * math.log(2.0))
    prev_ref[...] = jnp.zeros_like(prev_ref)
    early_ref[...] = jnp.zeros_like(early_ref)
    grow_ref[...] = jnp.zeros_like(grow_ref)
    order_lines = CHUNKS * ROWS

    @pl.loop(0, degrees // BLOCK)
    def _(block):
        narrow = orders[:, :LANES]
        order_sq = narrow * narrow
        cosine = cosine_ref[...]
        weights = weight_ref[...]
        limit = 2.0**64
        shrink = 2.0 ** (-64)
        previous, earlier, exponent = prev_ref[...], early_ref[...], grow_ref[...]
        first = (block * BLOCK).astype(jnp.float32)
        for step in range(BLOCK):
            degree = first + float(step)
            upper = jnp.sqrt(
                (4.0 * degree * degree - 1.0) / jnp.maximum(degree * degree - order_sq, 1.0)
            )
            below = degree - 1.0
            lower = jnp.sqrt(
                jnp.maximum(below * below - order_sq, 0.0)
                / jnp.maximum(jnp.full_like(order_sq, 4.0 * below * below - 1.0), 1.0)
            )
            recurred = widen(upper) * (cosine * previous - widen(lower) * earlier)
            at_start = orders == degree
            current = jnp.where(at_start, mant_ref[...], jnp.where(orders < degree, recurred, 0.0))
            exponent = jnp.where(at_start, exp_ref[...], exponent)
            value = weights * (current * jnp.exp2(exponent))
            for lane in range(width // LANES):
                lines[lane, step * order_lines : (step + 1) * order_lines, :] = value[
                    :, lane * LANES : (lane + 1) * LANES
                ]
            large = jnp.abs(current) > limit
            earlier = jnp.where(large, previous * shrink, previous)
            previous = jnp.where(large, current * shrink, current)
            exponent = jnp.where(large, exponent + 64.0, exponent)
        prev_ref[...] = previous
        early_ref[...] = earlier
        grow_ref[...] = exponent
        rows = pl.ds(pl.multiple_of(block * BLOCK, BLOCK), BLOCK)
        for order in range(order_lines):
            for lane in range(0, width, LANES):
                cut = min(LANES, kept - lane)
                part_of = lines[lane // LANES, pl.ds(order, BLOCK, stride=order_lines), :]
                table[order, rows, lane : lane + cut] = part_of[:, :cut].astype(table.dtype)

    def rows_from(device, lines_off):
        base = pl.multiple_of(device * block_rows + lines_off * ROWS, 2 * ROWS)
        return pl.ds(base, block_rows - lines_off * ROWS)

    def degree_copy(slot, device, lines_off=0):
        chunk = owner_chunk(me, slot, count)
        return pltpu.make_async_remote_copy(
            sums_out.at[slot, rows_from(device, lines_off)],
            out_ref.at[chunk, rows_from(0, lines_off)],
            send_two.at[slot, device],
            recv_two.at[chunk],
            device_id=(part, device),
            device_id_type=MESH,
        )

    def own_degrees(slot, lines_off=0):
        chunk = owner_chunk(me, slot, count)
        return pltpu.make_async_copy(
            sums_out.at[slot, rows_from(me, lines_off)],
            out_ref.at[chunk, rows_from(0, lines_off)],
            recv_two.at[chunk],
        )

    def each_target(slot, chosen, remote, local):
        first_line = owner_chunk(me, slot, count) * ROWS

        @pl.loop(1, count)
        def _(ahead):
            device = (me + ahead) % count

            @pl.when((first_line <= device * DEG_DEV) & chosen(device))
            def _():
                remote(slot, device, 0)

        @pl.when((first_line <= me * DEG_DEV) & chosen(me))
        def _():
            local(slot, 0)

        device = first_line // DEG_DEV
        for lines_off in range(2, DEG_DEV, 2):
            hit = (first_line - device * DEG_DEV == lines_off) & chosen(device)

            @pl.when(hit & (device != me))
            def _():
                remote(slot, device, lines_off)

            @pl.when(hit & (device == me))
            def _():
                local(slot, lines_off)

    def send_degrees(slot, chosen):
        each_target(
            slot,
            chosen,
            lambda *where: degree_copy(*where).start(),
            lambda *where: own_degrees(*where).start(),
        )

    degree_line = lax.broadcasted_iota(jnp.int32, (degrees, 1), 0)
    sign_even = jnp.where(degree_line % 2 == 0, 1.0, -1.0).astype(jnp.float32)

    def unfold():
        blocks = landed_pair.at[pl.ds(0, count - 1)]
        pltpu.make_async_copy(blocks, blocks, pair_sems.at[1]).wait()
        own_pair().wait()
        spread_out[...] = jnp.zeros_like(spread_out)

        @pl.loop(0, count)
        def _(source):
            value = landed_pair[source].astype(jnp.float32)
            for lane in range(2):
                spread_out[lane, : 2 * short, :] = value[:, lane * LANES : (lane + 1) * LANES]
            for slot in range(2):
                last = jnp.concatenate(
                    [
                        spread_out[lane, pl.ds(slot * short + ROWS - 1, ROWS, stride=ROWS), :]
                        for lane in range(2)
                    ],
                    axis=1,
                )
                landed[slot, source, groups - 1] = jnp.concatenate(
                    [value[slot * short : (slot + 1) * short], last], axis=0
                ).astype(landed.dtype)

    def analyse(slot):
        def wait_landed(parts):
            blocks = landed.at[slot, pl.ds(0, count - 1), pl.ds(0, parts)]
            pltpu.make_async_copy(blocks, blocks, recv_sem.at[slot]).wait()
            for group in range(parts):
                own_copy(slot, group).wait()

        @pl.when(slot < CHUNKS - 1)
        def _():
            wait_landed(groups - 1)

        @pl.when(slot == CHUNKS - 1)
        def _():
            wait_landed(groups)

        @pl.when(slot == 0)
        def _():
            unfold()

        @pl.loop(0, ROWS // 2)
        def _(pair):
            rows = pl.ds(pl.multiple_of(pair * 2 * ROWS, 2 * ROWS), 2 * ROWS)
            both = landed[slot, :, :, rows, :].astype(jnp.float32)
            both = both.reshape(count * groups, 2, ROWS, WIDE)
            for odd in range(2):
                rhs = both[:, odd].reshape(count * places, WIDE).astype(jnp.bfloat16)
                lhs = table[slot * ROWS + 2 * pair + odd]
                north = jnp.dot(lhs, rhs[:kept], preferred_element_type=jnp.float32)
                mirror = jnp.dot(lhs, rhs[kept:], preferred_element_type=jnp.float32)
                sign = sign_even if odd == 0 else -sign_even
                result = (north + sign * mirror) * scales[:1]
                for lane in range(2):
                    sums[lane, pl.ds(2 * pair + odd, degrees, stride=ROWS), :] = result[
                        :, lane * LANES : (lane + 1) * LANES
                    ]

        @pl.loop(0, count)
        def _(device):
            rows = pl.ds(pl.multiple_of(device * block_rows, block_rows), block_rows)
            sums_out[slot, rows, :] = jnp.concatenate(
                [sums[0, rows, :], sums[1, rows, :]], axis=1
            ).astype(jnp.bfloat16)

    pltpu.make_async_copy(
        moments_all.at[pl.ds(0, count - 1)],
        moments_all.at[pl.ds(0, count - 1)],
        moment_recv,
    ).wait()
    gathered = jnp.sum(moments_all[...], axis=0)
    first = jnp.sum(gathered[:ROWS], axis=0, keepdims=True) / (longitudes * total_sine)
    second = jnp.sum(gathered[ROWS:], axis=0, keepdims=True) / (longitudes * total_sine)
    spread = jnp.sqrt(second - first * first + 1e-05)
    gain = gain_ref[...]
    factor = jnp.concatenate([gain] * S, axis=1) / spread
    scales[:1] = jnp.concatenate([factor, factor], axis=1)
    scales[1:2] = jnp.concatenate([longitudes * first, jnp.zeros_like(first)], axis=1)

    @pl.loop(0, 2 * groups - 2)
    def _(turn_at):
        late = turn_at < groups - 2
        transform(jnp.where(late, turn_at + groups + 1, turn_at + groups + 2))

    @pl.loop(0, CHUNKS)
    def _(slot):
        @pl.when((slot < CHUNKS - 1) | has_last)
        def _():
            analyse(slot)
            send_degrees(slot, crosses)

        @pl.when(slot == 1)
        def _():
            send_degrees(0, lambda device: jnp.logical_not(crosses(device)))

        @pl.when(((slot < CHUNKS - 1) | has_last) & (slot > 0))
        def _():
            send_degrees(slot, lambda device: jnp.logical_not(crosses(device)))

    pltpu.make_async_copy(
        moments_all.at[pl.ds(0, count - 1)], moments_all.at[pl.ds(0, count - 1)], moment_send
    ).wait()

    def wait_orders(step, devices):
        rows = pl.ds(0, devices * ROWS * ROWS)
        pltpu.make_async_copy(
            outgoing.at[step, rows], outgoing.at[step, rows], send_sem.at[step]
        ).wait()

    for slot in range(CHUNKS - 1):
        for group in range(groups - 1):
            wait_orders(slot * groups + group, count - 1)
    blocks = paired.at[pl.ds(0, count - 1)]
    pltpu.make_async_copy(blocks, blocks, pair_sems.at[0]).wait()

    last_owners = count - count // PLANE

    @pl.loop((CHUNKS - 1) * groups, CHUNKS * groups)
    def _(step):
        @pl.when(has_last)
        def _():
            wait_orders(step, last_owners - 1)

        @pl.when(jnp.logical_not(has_last))
        def _():
            wait_orders(step, last_owners)

    @pl.loop(0, CHUNKS)
    def _(slot):
        @pl.when(has_chunk(slot, me))
        def _():
            each_target(
                slot,
                lambda device: device >= 0,
                lambda *where: degree_copy(*where).wait_send(),
                lambda *where: None,
            )

    @pl.loop(0, out_ref.shape[0])
    def _(chunk):
        low_line = chunk * ROWS - me * DEG_DEV

        @pl.when((low_line <= 0) | (low_line >= DEG_DEV))
        def _():
            pltpu.make_async_copy(blank, out_ref.at[chunk], recv_two.at[chunk]).wait()

        for lines_off in range(2, DEG_DEV, 2):

            @pl.when(low_line == lines_off)
            def _():
                blank_copy(chunk, lines_off).wait()
                rows = rows_from(0, lines_off)
                pltpu.make_async_copy(
                    blank.at[rows], out_ref.at[chunk, rows], recv_two.at[chunk]
                ).wait()


def scratch_of(count, band, longitudes):
    groups = -(-band // ROWS)
    places = groups * ROWS
    degrees = DEG_DEV * count
    lines_of = count * ROWS
    kept = count // 2 * places
    width = round_up(kept, LANES)
    order_lines = CHUNKS * ROWS
    state = (order_lines, width)
    bf16, f32 = jnp.bfloat16, jnp.float32
    return [
        ((CHUNKS, 2 * lines_of, longitudes), bf16),
        ((CHUNKS, 2 * lines_of, longitudes), bf16),
        ((ROWS, longitudes, LANES), f32),
        ((places // 2, longitudes, WIDE), bf16),
        ((places // 2, longitudes, WIDE), bf16),
        ((2, lines_of * ROWS, LANES), f32),
        ((CHUNKS * groups, lines_of * ROWS, WIDE), bf16),
        ((CHUNKS, count, groups, ROWS * ROWS, WIDE), bf16),
        ((2 * ROWS, LANES), f32),
        ((count, 2 * ROWS, LANES), f32),
        ((ROWS, WIDE), f32),
        ((order_lines, degrees, kept), bf16),
        (state, f32),
        (state, f32),
        (state, f32),
        (state, f32),
        (state, f32),
        ((width // LANES, BLOCK * order_lines, LANES), f32),
        ((2, degrees * ROWS, LANES), f32),
        ((CHUNKS, degrees * ROWS, WIDE), bf16),
        ((DEG_DEV * ROWS, WIDE), bf16),
        ((2, lines_of * ROWS, LANES), f32),
        ((count, 2 * ROWS * (ROWS - 1), WIDE), bf16),
        ((count, 2 * ROWS * (ROWS - 1), WIDE), bf16),
        ((2, 2 * ROWS * ROWS, LANES), f32),
    ]


def scratch_bytes(shapes):
    total = 0
    for shape, dtype in shapes:
        size = math.prod(shape[:-1]) * round_up(shape[-1], LANES)
        total += size * jnp.dtype(dtype).itemsize
    return total


def coefficients_of(grid_field, norm_gain, count):
    band, longitudes, columns = grid_field.shape
    groups = -(-band // ROWS)
    places = groups * ROWS
    order_count = DEG_DEV * count
    high, low = transform_tables(count, longitudes)
    sine, cosine, weight, logsine, total_sine = angle_tables(count, band, places)
    weight_scale = math.pi**1.5 / math.sqrt(count * band * longitudes)
    shapes = scratch_of(count, band, longitudes)
    dma = pltpu.SemaphoreType.DMA
    vmem = pl.BlockSpec(memory_space=pltpu.VMEM)
    anywhere = pl.BlockSpec(memory_space=pl.ANY)
    return pl.pallas_call(
        functools.partial(spectral_kernel, (count, band, longitudes, total_sine)),
        out_shape=jax.ShapeDtypeStruct((order_count // ROWS, DEG_DEV * ROWS, WIDE), jnp.bfloat16),
        in_specs=[
            anywhere,
            vmem,
            anywhere,
            anywhere,
            pl.BlockSpec(memory_space=pltpu.SMEM),
            vmem,
            vmem,
            vmem,
            vmem,
        ],
        out_specs=anywhere,
        scratch_shapes=[pltpu.VMEM(shape, dtype) for shape, dtype in shapes]
        + [
            dma((3,)),
            dma((2, CHUNKS)),
            dma((ROWS,)),
            dma,
            dma,
            dma((CHUNKS * groups,)),
            dma((CHUNKS,)),
            dma((CHUNKS * groups,)),
            dma((CHUNKS, count)),
            dma((order_count // ROWS,)),
            dma((order_count // ROWS,)),
        ],
        cost_estimate=pl.CostEstimate(
            flops=20 * 10**9, bytes_accessed=40 * 10**6, transcendentals=10**6
        ),
        compiler_params=pltpu.CompilerParams(
            collective_id=0, has_side_effects=True, vmem_limit_bytes=VMEM_CAP
        ),
    )(
        grid_field,
        norm_gain[None, :],
        jnp.asarray(high),
        jnp.asarray(low),
        jnp.asarray(sine),
        jnp.asarray(cosine),
        jnp.asarray((weight * weight_scale).astype(np.float32)),
        jnp.asarray(logsine),
        jnp.asarray(log_starts(order_count)),
    )


def filter_kernel(coef_ref, weight_ref, out_ref, coefs, outs, full_ref, in_sem, out_sem):
    pairs = coefs.shape[0]
    chunks = coefs.shape[1]
    orders = chunks * ROWS

    def fetch(pair):
        rows = pl.ds(pl.multiple_of(pair * 2 * ROWS, 2 * ROWS), 2 * ROWS)
        return pltpu.make_async_copy(coef_ref.at[:, rows, :], coefs.at[pair], in_sem.at[pair])

    def store(pair):
        return pltpu.make_async_copy(
            outs.at[pair], out_ref.at[pl.ds(2 * pair, 2)], out_sem.at[pair]
        )

    for pair in range(pairs):
        fetch(pair).start()

    full_ref[...] = jnp.zeros_like(full_ref)
    for pair in range(pairs):
        for odd in range(2):
            degree = 2 * pair + odd
            real, imag = weight_ref[degree, 0], weight_ref[degree, 1]
            for sample in range(S):
                for side, halves in enumerate(((real, imag), (-imag, real))):
                    for target, block in enumerate(halves):
                        row = side * S * C + sample * C
                        lane = target * S * C + sample * C
                        full_ref[degree, row : row + C, lane : lane + C] = block
        fetch(pair).wait()
        both = coefs[pair].astype(jnp.float32).reshape(chunks, 2, ROWS, WIDE)
        for odd in range(2):
            value = both[:, odd].reshape(orders, WIDE).astype(jnp.bfloat16)
            outs[pair, odd] = jnp.dot(
                value, full_ref[2 * pair + odd], preferred_element_type=jnp.float32
            ).astype(outs.dtype)
        store(pair).start()

    @pl.loop(0, pairs)
    def _(pair):
        store(pair).wait()


def apply_filter(coefficients, filter_weight):
    chunks = coefficients.shape[0]
    degrees = filter_weight.shape[0]
    pairs = degrees // 2
    orders = chunks * ROWS
    anywhere = pl.BlockSpec(memory_space=pl.ANY)
    return pl.pallas_call(
        filter_kernel,
        out_shape=jax.ShapeDtypeStruct((degrees, orders, WIDE), jnp.bfloat16),
        in_specs=[anywhere, pl.BlockSpec(memory_space=pltpu.VMEM)],
        out_specs=anywhere,
        scratch_shapes=[
            pltpu.VMEM((pairs, chunks, 2 * ROWS, WIDE), jnp.bfloat16),
            pltpu.VMEM((pairs, 2, orders, WIDE), jnp.bfloat16),
            pltpu.VMEM((degrees, WIDE, WIDE), jnp.bfloat16),
            pltpu.SemaphoreType.DMA((pairs,)),
            pltpu.SemaphoreType.DMA((pairs,)),
        ],
        compiler_params=pltpu.CompilerParams(vmem_limit_bytes=VMEM_CAP),
    )(coefficients, filter_weight)


def body(grid_field, norm_gain, filter_weight):
    count = lax.axis_size("lat")
    band, longitudes, columns = grid_field.shape
    fits = scratch_bytes(scratch_of(count, band, longitudes)) < VMEM_CAP - 3 * 1024 * 1024
    if count % PLANE or band % ROWS != ROWS - 1 or band < 2 * ROWS or not fits:
        return plain_body(grid_field, norm_gain, filter_weight)
    coefficients = coefficients_of(grid_field, norm_gain, count)
    return apply_filter(coefficients, filter_weight)


def solution(mesh):
    in_specs = (P("lat", None, "parts"), P("parts"), P("lat", None, None, "parts"))
    out_specs = P("lat", None, "parts")
    return jax.shard_map(body, mesh=mesh, in_specs=in_specs, out_specs=out_specs, check_vma=False)
```

```python
import functools
import math

import jax
import jax.numpy as jnp
import numpy as np
from jax import lax
from jax.experimental import pallas as pl
from jax.experimental.pallas import tpu as pltpu
from jax.sharding import PartitionSpec as P

C = 64
S = 2
DEG_DEV = 22
ORDER_PAD = 24
BLOCK = 16
LANES = 128


def round_up(value, step):
    return -(-value // step) * step


def legendre_kernel(
    orders_ref, cosine_ref, weights_ref, mant_ref, exp_ref, out_ref, prev_ref, early_ref, grow_ref, rows_ref
):
    block = pl.program_id(0)
    width = cosine_ref.shape[1]
    kept_width = out_ref.shape[2]

    @pl.when(block == 0)
    def _():
        prev_ref[...] = jnp.zeros_like(prev_ref)
        early_ref[...] = jnp.zeros_like(early_ref)
        grow_ref[...] = jnp.zeros_like(grow_ref)

    orders = orders_ref[...]
    narrow = orders[:, :LANES]
    order_sq = narrow * narrow
    cosine = cosine_ref[...]
    weights = weights_ref[...]
    limit = 2.0**64
    shrink = 2.0 ** (-64)
    previous, earlier, exponent = prev_ref[...], early_ref[...], grow_ref[...]
    first = (block * BLOCK).astype(jnp.float32)

    def widen(value):
        return jnp.concatenate([value] * (width // LANES), axis=1)

    for step in range(BLOCK):
        degree = first + float(step)
        upper = jnp.sqrt(
            (4.0 * degree * degree - 1.0) / jnp.maximum(degree * degree - order_sq, 1.0)
        )
        below = degree - 1.0
        lower = jnp.sqrt(
            jnp.maximum(below * below - order_sq, 0.0)
            / jnp.maximum(jnp.full_like(order_sq, 4.0 * below * below - 1.0), 1.0)
        )
        recurred = widen(upper) * (cosine * previous - widen(lower) * earlier)
        at_start = orders == degree
        current = jnp.where(at_start, mant_ref[...], jnp.where(orders < degree, recurred, 0.0))
        exponent = jnp.where(at_start, exp_ref[...], exponent)
        value = weights * (current * jnp.exp2(exponent))
        for lane in range(width // LANES):
            rows_ref[lane, step * ORDER_PAD : (step + 1) * ORDER_PAD, :] = value[
                :, lane * LANES : (lane + 1) * LANES
            ]
        large = jnp.abs(current) > limit
        earlier = jnp.where(large, previous * shrink, previous)
        previous = jnp.where(large, current * shrink, current)
        exponent = jnp.where(large, exponent + 64.0, exponent)

    prev_ref[...] = previous
    early_ref[...] = earlier
    grow_ref[...] = exponent
    for order in range(DEG_DEV):
        for lane in range(0, width, LANES):
            cut = min(LANES, kept_width - lane)
            piece = rows_ref[lane // LANES, pl.ds(order, BLOCK, stride=ORDER_PAD), :]
            out_ref[order, :, lane : lane + cut] = piece[:, :cut].astype(out_ref.dtype)


def legendre_table(colatitude, first_order, degrees, weight_scale):
    rows = colatitude.shape[0]
    width = round_up(rows, LANES)
    colat = jnp.concatenate([colatitude, jnp.full((width - rows,), 0.5 * math.pi, jnp.float32)])
    orders = (first_order + jnp.arange(ORDER_PAD, dtype=jnp.int32)).astype(jnp.float32)
    sine_rows = jnp.sin(colat)
    log_start = 0.5 * jnp.log((2.0 * orders + 1.0) / (4.0 * math.pi)) + 0.5 * (
        lax.lgamma(orders + 0.5) - lax.lgamma(orders + 1.0) - 0.5 * math.log(math.pi)
    )
    log_diag = log_start[:, None] + orders[:, None] * jnp.log(sine_rows)[None, :]
    start_exp = 64.0 * jnp.floor(log_diag / (64.0 * math.log(2.0)))
    start_mant = jnp.exp(log_diag - start_exp * math.log(2.0))
    state = (ORDER_PAD, width)
    whole = pl.BlockSpec(state, lambda i: (0, 0))
    line = pl.BlockSpec((1, width), lambda i: (0, 0))
    return pl.pallas_call(
        legendre_kernel,
        grid=(degrees // BLOCK,),
        out_shape=jax.ShapeDtypeStruct((DEG_DEV, degrees, rows), jnp.bfloat16),
        in_specs=[whole, line, line, whole, whole],
        out_specs=pl.BlockSpec((DEG_DEV, BLOCK, rows), lambda i: (0, i, 0)),
        scratch_shapes=[
            pltpu.VMEM(state, jnp.float32),
            pltpu.VMEM(state, jnp.float32),
            pltpu.VMEM(state, jnp.float32),
            pltpu.VMEM((width // LANES, BLOCK * ORDER_PAD, LANES), jnp.float32),
        ],
        cost_estimate=pl.CostEstimate(
            flops=degrees * ORDER_PAD * width * 2000,
            bytes_accessed=DEG_DEV * degrees * rows * 2,
            transcendentals=degrees * ORDER_PAD * width,
        ),
        compiler_params=pltpu.CompilerParams(vmem_limit_bytes=24 * 1024 * 1024),
    )(
        jnp.broadcast_to(orders[:, None], state),
        jnp.cos(colat)[None, :],
        (weight_scale * sine_rows)[None, :],
        start_mant,
        start_exp,
    )


def expand_filter(filter_weight):
    real_part = filter_weight[:, 0]
    imag_part = filter_weight[:, 1]
    from_real = jnp.stack([real_part, imag_part], axis=1)
    from_imag = jnp.stack([-imag_part, real_part], axis=1)
    mixing = jnp.stack([from_real, from_imag], axis=1)
    same = jnp.eye(S, dtype=filter_weight.dtype)
    full = mixing.transpose(0, 1, 3, 2, 4)[:, :, None, :, :, None, :] * same[None, None, :, None, None, :, None]
    return full.reshape(filter_weight.shape[0], 2 * S * C, 2 * S * C)


def mix_kernel(sin_ref, cos_ref, weight_ref, out_ref, rows_ref):
    sources, degrees, orders, half = cos_ref.shape
    for degree in range(degrees):
        for source in range(sources):
            rows = slice(source * orders, (source + 1) * orders)
            rows_ref[degree, rows, :half] = cos_ref[source, degree].astype(jnp.float32)
            rows_ref[degree, rows, half:] = sin_ref[source, degree].astype(jnp.float32)
        out_ref[degree] = jnp.dot(
            rows_ref[degree].astype(jnp.bfloat16),
            weight_ref[degree],
            preferred_element_type=jnp.float32,
        ).astype(out_ref.dtype)


def mix(coef_sin, coef_cos, weights):
    sources, degrees, orders, half = coef_cos.shape
    wide = weights.shape[2]
    step = 2
    piece = pl.BlockSpec((sources, step, orders, half), lambda i: (0, i, 0, 0))
    return pl.pallas_call(
        mix_kernel,
        grid=(degrees // step,),
        out_shape=jax.ShapeDtypeStruct((degrees, sources * orders, wide), jnp.bfloat16),
        in_specs=[piece, piece, pl.BlockSpec((step, 2 * half, wide), lambda i: (i, 0, 0))],
        out_specs=pl.BlockSpec((step, sources * orders, wide), lambda i: (i, 0, 0)),
        scratch_shapes=[pltpu.VMEM((step, sources * orders, 2 * half), jnp.float32)],
        compiler_params=pltpu.CompilerParams(vmem_limit_bytes=24 * 1024 * 1024),
    )(coef_sin, coef_cos, weights)


def fourier_matrix(orders, longitudes):
    phases = (np.arange(orders)[:, None] * np.arange(longitudes)[None, :]) % longitudes
    angles = 2.0 * np.pi * phases / longitudes
    return np.stack([np.cos(angles), -np.sin(angles)]).astype(np.float32)


def plain_body(grid_field, norm_gain, filter_weight):
    device_index = lax.axis_index("lat")
    lat_count = lax.axis_size("lat")
    band_rows, longitudes, columns = grid_field.shape
    total_lat = band_rows * lat_count
    order_count = DEG_DEV * lat_count
    all_rows = jnp.arange(total_lat, dtype=jnp.int32)
    colat_all = math.pi * (all_rows.astype(jnp.float32) + 0.5) / total_lat
    sine_all = jnp.sin(colat_all)
    own_rows = device_index * band_rows + jnp.arange(band_rows, dtype=jnp.int32)
    sine_own = jnp.sin(math.pi * (own_rows.astype(jnp.float32) + 0.5) / total_lat)

    first = jnp.einsum("j,jnx->x", sine_own, grid_field, precision=lax.Precision.HIGHEST)
    second = jnp.einsum(
        "j,jnx->x", sine_own, grid_field * grid_field, precision=lax.Precision.HIGHEST
    )
    band_mean = first / (longitudes * jnp.sum(sine_own))
    denominator_rows = jnp.float32(longitudes)
    cos_table, sin_table = fourier_matrix(order_count, longitudes)

    def transform(table):
        return jnp.einsum(
            "mn,jnx->mjx", jnp.asarray(table), grid_field, precision=lax.Precision.HIGH
        )

    def to_orders(raw):
        return lax.all_to_all(
            raw.astype(jnp.bfloat16), "lat", split_axis=0, concat_axis=1, tiled=True
        )

    def to_degrees(sums):
        return lax.all_to_all(
            sums, "lat", split_axis=0, concat_axis=0
        )

    received_sin = to_orders(transform(sin_table))
    constant = jnp.arange(order_count) == 0
    shift = jnp.where(constant[:, None, None], denominator_rows * band_mean, 0.0)
    received_cos = to_orders(transform(cos_table) - shift)

    weight_scale = math.pi**1.5 / math.sqrt(total_lat * longitudes)
    legendre = legendre_table(colat_all, device_index * DEG_DEV, order_count, weight_scale)

    def analyse(received):
        return jnp.einsum("mlj,mjx->mlx", legendre, received, preferred_element_type=jnp.float32)

    def by_degree(sums):
        ordered = sums.astype(jnp.bfloat16).transpose(1, 0, 2)
        return ordered.reshape(lat_count, DEG_DEV, DEG_DEV, columns)

    sums_sin = by_degree(analyse(received_sin))
    moments, sums_sin = lax.optimization_barrier(
        (jnp.stack([first, second, band_mean]), sums_sin)
    )
    gathered, sums_sin = lax.optimization_barrier((lax.all_gather(moments, "lat"), sums_sin))
    denominator = longitudes * jnp.sum(sine_all)
    average = jnp.sum(gathered[:, 0], axis=0) / denominator
    mean_square = jnp.sum(gathered[:, 1], axis=0) / denominator
    spread = jnp.sqrt(mean_square - average * average + 1e-05)
    factor = jnp.tile(norm_gain, S) / spread
    coef_sin = to_degrees(sums_sin)
    band_sums = jnp.sum(
        legendre[0].astype(jnp.float32).reshape(order_count, lat_count, band_rows), axis=2
    )
    level = jnp.dot(
        band_sums,
        denominator_rows * (gathered[:, 2] - average),
        precision=lax.Precision.HIGHEST,
    )
    here = (device_index == 0) & (jnp.arange(DEG_DEV) == 0)
    coef_cos = to_degrees(
        by_degree(analyse(received_cos) + jnp.where(here[:, None, None], level[None], 0.0))
    )

    expanded = expand_filter(filter_weight)
    expanded = (expanded * jnp.tile(factor, 2)[None, :, None]).astype(jnp.bfloat16)

    return mix(coef_sin, coef_cos, expanded)


MESH = pl.DeviceIdType.MESH
ROWS = 8
WIDE = 2 * LANES
CHUNKS = 3
PLANE = 4
PLANE_CHUNKS = PLANE * CHUNKS - 1
VMEM_CAP = 60 * 1024 * 1024


def owns_last(device):
    return device % PLANE != 1


def owner_chunk(device, slot, count):
    plane, inner = count // PLANE - 1 - device // PLANE, device % PLANE
    first = 1 // (plane + inner + 1)
    at = slot + first * (CHUNKS - 1 - 2 * slot)
    return PLANE_CHUNKS * plane + PLANE * at + inner - (at // (CHUNKS - 1)) * ((inner + 2) // PLANE)


def transform_tables(count, longitudes):
    table = np.zeros((CHUNKS, 2, count, ROWS, longitudes), np.float64)
    for slot in range(CHUNKS):
        for device in range(count):
            if slot == CHUNKS - 1 and not owns_last(device):
                continue
            orders = owner_chunk(device, slot, count) * ROWS + np.arange(ROWS)
            phases = (orders[:, None] * np.arange(longitudes)[None, :]) % longitudes
            angles = 2.0 * np.pi * phases / longitudes
            table[slot, 0, device] = np.cos(angles)
            table[slot, 1, device] = -np.sin(angles)
    table = table.reshape(CHUNKS, 2 * count * ROWS, longitudes).astype(np.float32)
    high = table.astype(jnp.bfloat16)
    low = (table - high.astype(np.float32)).astype(jnp.bfloat16)
    return high, low


def angle_tables(count, band, places):
    colat = np.pi * (np.arange(count * band) + 0.5) / (count * band)
    by_place = np.full((count, places), 0.5 * np.pi)
    valid = np.zeros((count, places))
    for device in range(count):
        rows = colat[device * band : (device + 1) * band]
        by_place[device, :band] = rows if device < count // 2 else rows[::-1]
        valid[device, :band] = 1.0
    sine_places = np.sin(by_place) * valid
    north = by_place[: count // 2].reshape(1, -1)
    weight = sine_places[: count // 2].reshape(1, -1)
    width = round_up(north.shape[1], LANES)
    north = np.pad(north, ((0, 0), (0, width - north.shape[1])), constant_values=0.5 * np.pi)
    weight = np.pad(weight, ((0, 0), (0, width - weight.shape[1])))
    return (
        sine_places.reshape(-1).astype(np.float32),
        np.cos(north).astype(np.float32),
        weight,
        np.log(np.sin(north)).astype(np.float32),
        float(np.sum(np.sin(colat))),
    )


def log_starts(order_count):
    values = [
        0.5 * math.log((2.0 * m + 1.0) / (4.0 * math.pi))
        + 0.5 * (math.lgamma(m + 0.5) - math.lgamma(m + 1.0) - 0.5 * math.log(math.pi))
        for m in range(order_count)
    ]
    return np.asarray(values, np.float32)[:, None]


def spectral_kernel(
    sizes,
    field_ref,
    gain_ref,
    high_ref,
    low_ref,
    sine_ref,
    cosine_ref,
    weight_ref,
    logsine_ref,
    start_ref,
    out_ref,
    high,
    low,
    stage,
    field_high,
    field_low,
    turned,
    outgoing,
    landed,
    moments,
    moments_all,
    scales,
    table,
    prev_ref,
    early_ref,
    grow_ref,
    mant_ref,
    exp_ref,
    lines,
    sums,
    sums_out,
    blank,
    held,
    paired,
    landed_pair,
    spread_out,
    pair_sems,
    table_sem,
    stage_sem,
    moment_send,
    moment_recv,
    send_sem,
    recv_sem,
    local_sem,
    send_two,
    recv_two,
    blank_sem,
):
    count, band, longitudes, total_sine = sizes
    me = lax.axis_index("lat")
    part = lax.axis_index("parts")
    half = count // 2
    south = me // half
    slot_of_me = me + south * (half + count - 1 - 2 * me)
    groups = outgoing.shape[0] // CHUNKS
    places = groups * ROWS
    degrees = table.shape[1]
    kept = table.shape[2]
    width = cosine_ref.shape[1]
    block_rows = DEG_DEV * ROWS
    zero_owner = count - PLANE
    has_last = owns_last(me)

    def has_chunk(slot, device):
        return (slot < CHUNKS - 1) | owns_last(device)

    def table_copies(slot):
        return (
            pltpu.make_async_copy(high_ref.at[slot], high.at[slot], table_sem.at[0, slot]),
            pltpu.make_async_copy(low_ref.at[slot], low.at[slot], table_sem.at[1, slot]),
        )

    def row_copy(place):
        row = place + south * (band - 1 - 2 * place)
        at = place % ROWS
        return pltpu.make_async_copy(field_ref.at[row], stage.at[at], stage_sem.at[at])

    for place in range(2):
        row_copy(place).start()
    for copy in table_copies(0):
        copy.start()
    for place in range(2, ROWS):
        row_copy(place).start()
    for slot in range(1, CHUNKS):
        for copy in table_copies(slot):
            copy.start()

    barrier = pltpu.get_barrier_semaphore()

    @pl.loop(1, count)
    def _(step):
        pl.semaphore_signal(
            barrier, inc=1, device_id=(part, (me + step) % count), device_id_type=MESH
        )

    moments[...] = jnp.zeros_like(moments)
    for place in range(band, places):
        lanes = slice((place % 2) * LANES, (place % 2 + 1) * LANES)
        field_high[place // 2, :, lanes] = jnp.zeros((longitudes, LANES), jnp.bfloat16)
        field_low[place // 2, :, lanes] = jnp.zeros((longitudes, LANES), jnp.bfloat16)

    piece = longitudes // 6

    def split_row(place, lanes):
        at = place % ROWS
        pair = place // 2
        total = jnp.zeros((ROWS, LANES), jnp.float32)
        square = jnp.zeros((ROWS, LANES), jnp.float32)
        for first in range(0, longitudes, piece):
            value = stage[at, first : first + piece, :]
            top = value.astype(jnp.bfloat16)
            field_high[pair, first : first + piece, lanes] = top
            field_low[pair, first : first + piece, lanes] = (
                value - top.astype(jnp.float32)
            ).astype(jnp.bfloat16)
            total += jnp.sum(value.reshape(-1, ROWS, LANES), axis=0)
            square += jnp.sum((value * value).reshape(-1, ROWS, LANES), axis=0)
        sine = sine_ref[me * places + place]
        moments[:ROWS] += sine * total
        moments[ROWS:] += sine * square

    def take_row(place, lanes):
        row_copy(place).wait()
        split_row(place, lanes)

        @pl.when(place + ROWS < band)
        def _():
            row_copy(place + ROWS).start()

    def take_group(group):
        @pl.loop(0, ROWS // 2)
        def _(pair):
            place = group * ROWS + 2 * pair
            take_row(place, slice(0, LANES))

            @pl.when(place + 1 < band)
            def _():
                take_row(place + 1, slice(LANES, WIDE))

    halves = (slice(0, LANES), slice(LANES, WIDE))
    lines_of = count * ROWS

    def project(slot, at):
        product = jnp.dot(high[slot], field_high[at], preferred_element_type=jnp.float32)
        product += jnp.dot(high[slot], field_low[at], preferred_element_type=jnp.float32)
        product += jnp.dot(low[slot], field_high[at], preferred_element_type=jnp.float32)
        return product

    def turn(product, pair):
        for side in range(2):
            for row in range(2):
                turned[side, pl.ds(2 * pair + row, lines_of, stride=ROWS), :] = product[
                    side * lines_of : (side + 1) * lines_of, row * LANES : (row + 1) * LANES
                ]


    def blank_copy(chunk, lines_off):
        rows = pl.ds(0, lines_off * ROWS)
        return pltpu.make_async_copy(
            blank.at[rows], out_ref.at[chunk, rows], blank_sem.at[chunk]
        )

    def moment_copy(device):
        return pltpu.make_async_remote_copy(
            moments,
            moments_all.at[me],
            moment_send,
            moment_recv,
            device_id=(part, device),
            device_id_type=MESH,
        )

    def order_copy(slot, group, device):
        step = slot * groups + group
        rows = pl.ds(pl.multiple_of(device * ROWS * ROWS, ROWS * ROWS), ROWS * ROWS)
        return pltpu.make_async_remote_copy(
            outgoing.at[step, rows],
            landed.at[slot, slot_of_me, group],
            send_sem.at[step],
            recv_sem.at[slot],
            device_id=(part, device),
            device_id_type=MESH,
        )

    def own_copy(slot, group):
        step = slot * groups + group
        rows = pl.ds(pl.multiple_of(me * ROWS * ROWS, ROWS * ROWS), ROWS * ROWS)
        return pltpu.make_async_copy(
            outgoing.at[step, rows], landed.at[slot, slot_of_me, group], local_sem.at[step]
        )

    short = ROWS * (ROWS - 1)

    def pair_copy(device):
        return pltpu.make_async_remote_copy(
            paired.at[device],
            landed_pair.at[slot_of_me],
            pair_sems.at[0],
            pair_sems.at[1],
            device_id=(part, device),
            device_id_type=MESH,
        )

    def own_pair():
        return pltpu.make_async_copy(
            paired.at[me], landed_pair.at[slot_of_me], pair_sems.at[2]
        )

    def fold_last():
        @pl.loop(0, count)
        def _(device):
            first = device * ROWS * ROWS
            for side in range(2):
                last = turned[side, pl.ds(pl.multiple_of(first + short, ROWS), ROWS), :]
                turned[side, pl.ds(first + ROWS - 1, ROWS, stride=ROWS), :] = last

    def send_pairs():
        @pl.loop(0, count)
        def _(ahead):
            device = ((me // half + 1 + ahead // half) % 2) * half + (me + ahead) % half
            rows = pl.ds(pl.multiple_of(device * ROWS * ROWS, ROWS), short)
            paired[device] = jnp.concatenate(
                [
                    jnp.concatenate([source[0, rows, :], source[1, rows, :]], axis=1)
                    for source in (held, turned)
                ],
                axis=0,
            ).astype(jnp.bfloat16)

            @pl.when(device != me)
            def _():
                pair_copy(device).start()

            @pl.when(device == me)
            def _():
                own_pair().start()

    upper = count - count // PLANE

    def crosses(device):
        return (device >= upper) != (me >= upper)

    def send_group(slot, group, first, last):
        @pl.loop(first, last)
        def _(ahead):
            device = ((me // half + 1 + ahead // half) % 2) * half + (me + ahead) % half
            rows = pl.ds(pl.multiple_of(device * ROWS * ROWS, ROWS * ROWS), ROWS * ROWS)
            outgoing[slot * groups + group, rows, :] = jnp.concatenate(
                [turned[0, rows, :], turned[1, rows, :]], axis=1
            ).astype(jnp.bfloat16)

            @pl.when((device != me) & has_chunk(slot, device))
            def _():
                order_copy(slot, group, device).start()

            @pl.when((device == me) & has_chunk(slot, device))
            def _():
                own_copy(slot, group).start()

    def project_half(pair, part_of):
        lines_half = half * ROWS
        rows = [
            pl.ds(pl.multiple_of(side * lines_of + part_of * lines_half, lines_half), lines_half)
            for side in range(2)
        ]
        top = jnp.concatenate([high[0, row, :] for row in rows], axis=0)
        rest = jnp.concatenate([low[0, row, :] for row in rows], axis=0)
        product = jnp.dot(top, field_high[pair], preferred_element_type=jnp.float32)
        product += jnp.dot(top, field_low[pair], preferred_element_type=jnp.float32)
        product += jnp.dot(rest, field_high[pair], preferred_element_type=jnp.float32)
        return product

    def turn_half(product, pair, part_of):
        lines_half = half * ROWS
        for side in range(2):
            for row in range(2):
                at = part_of * lines_half * ROWS + 2 * pair + row
                turned[side, pl.ds(at, lines_half, stride=ROWS), :] = product[
                    side * lines_half : (side + 1) * lines_half, row * LANES : (row + 1) * LANES
                ]

    for row in range(2):
        take_row(row, halves[row])
    for copy in table_copies(0):
        copy.wait()
    other = (me // half + 1) % 2
    for pair in range(ROWS // 2):
        following = range(2 * pair + 2, 2 * pair + 4) if pair + 1 < ROWS // 2 else ()
        for place in following:
            row_copy(place).wait()
        product = project_half(pair, other)
        for place in following:
            split_row(place, halves[place % 2])
        turn_half(product, pair, other)
        for place in following:
            if place + ROWS < band:
                row_copy(place + ROWS).start()
    pl.semaphore_wait(barrier, count - 1)
    send_group(0, 0, 0, half)

    @pl.loop(0, ROWS // 2)
    def _(pair):
        turn_half(project_half(pair, 1 - other), pair, 1 - other)

    send_group(0, 0, half, count)

    def transform(step):
        slot, group = step // groups, step % groups

        @pl.when(step == 1)
        def _():
            pl.loop(1, groups)(take_group)
            moments_all[me] = moments[...]

            @pl.loop(1, count)
            def _(ahead):
                moment_copy((me + ahead) % count).start()

        @pl.when((step == 2 * groups - 1) | (step == 2 * groups))
        def _():
            for copy in table_copies(slot):
                copy.wait()

        @pl.loop(0, ROWS // 2)
        def _(pair):
            turn(project(slot, group * (ROWS // 2) + pair), pair)

        @pl.when(slot == CHUNKS - 1)
        def _():
            at = zero_owner * ROWS * ROWS
            turned[0, at : at + ROWS, :] -= scales[1:2, :LANES]

        folded = (group == groups - 1) & (slot < CHUNKS - 1)

        @pl.when(jnp.logical_not(folded))
        def _():
            send_group(slot, group, 0, count)

        @pl.when(folded)
        def _():
            fold_last()

            @pl.when(slot == 0)
            def _():
                held[...] = turned[...]

            @pl.when(slot > 0)
            def _():
                send_pairs()

    @pl.loop(1, groups + 2)
    def _(turn_at):
        tail = groups + (groups - 1) * (groups + 1 - turn_at)
        transform(jnp.where(turn_at < groups, turn_at, tail))

    blank[...] = jnp.zeros_like(blank)

    @pl.loop(0, out_ref.shape[0])
    def _(chunk):
        low_line = chunk * ROWS - me * DEG_DEV

        @pl.when(low_line >= DEG_DEV)
        def _():
            pltpu.make_async_copy(blank, out_ref.at[chunk], recv_two.at[chunk]).start()

    @pl.loop(0, DEG_DEV // ROWS + 1)
    def _(ahead):
        chunk = me * DEG_DEV // ROWS + 1 + ahead
        low_line = chunk * ROWS - me * DEG_DEV
        for lines_off in range(2, DEG_DEV, 2):

            @pl.when(low_line == lines_off)
            def _():
                blank_copy(chunk, lines_off).start()

    chunk_of = [owner_chunk(me, slot, count) for slot in range(CHUNKS)]
    lines_in = lax.broadcasted_iota(jnp.int32, (ROWS, width), 0)
    orders = jnp.concatenate(
        [(chunk * ROWS + lines_in).astype(jnp.float32) for chunk in chunk_of], axis=0
    )
    start = jnp.concatenate(
        [start_ref[pl.ds(pl.multiple_of(chunk * ROWS, ROWS), ROWS), :] for chunk in chunk_of], axis=0
    )
    start = jnp.broadcast_to(start, (CHUNKS * ROWS, width))

    def widen(value):
        return jnp.concatenate([value] * (width // LANES), axis=1)

    log_diag = start + orders * logsine_ref[...]
    start_exp = 64.0 * jnp.floor(log_diag / (64.0 * math.log(2.0)))
    exp_ref[...] = start_exp
    mant_ref[...] = jnp.exp(log_diag - start_exp * math.log(2.0))
    prev_ref[...] = jnp.zeros_like(prev_ref)
    early_ref[...] = jnp.zeros_like(early_ref)
    grow_ref[...] = jnp.zeros_like(grow_ref)
    order_lines = CHUNKS * ROWS

    @pl.loop(0, degrees // BLOCK)
    def _(block):
        narrow = orders[:, :LANES]
        order_sq = narrow * narrow
        cosine = cosine_ref[...]
        weights = weight_ref[...]
        limit = 2.0**64
        shrink = 2.0 ** (-64)
        previous, earlier, exponent = prev_ref[...], early_ref[...], grow_ref[...]
        first = (block * BLOCK).astype(jnp.float32)
        for step in range(BLOCK):
            degree = first + float(step)
            upper = jnp.sqrt(
                (4.0 * degree * degree - 1.0) / jnp.maximum(degree * degree - order_sq, 1.0)
            )
            below = degree - 1.0
            lower = jnp.sqrt(
                jnp.maximum(below * below - order_sq, 0.0)
                / jnp.maximum(jnp.full_like(order_sq, 4.0 * below * below - 1.0), 1.0)
            )
            recurred = widen(upper) * (cosine * previous - widen(lower) * earlier)
            at_start = orders == degree
            current = jnp.where(at_start, mant_ref[...], jnp.where(orders < degree, recurred, 0.0))
            exponent = jnp.where(at_start, exp_ref[...], exponent)
            value = weights * (current * jnp.exp2(exponent))
            for lane in range(width // LANES):
                lines[lane, step * order_lines : (step + 1) * order_lines, :] = value[
                    :, lane * LANES : (lane + 1) * LANES
                ]
            large = jnp.abs(current) > limit
            earlier = jnp.where(large, previous * shrink, previous)
            previous = jnp.where(large, current * shrink, current)
            exponent = jnp.where(large, exponent + 64.0, exponent)
        prev_ref[...] = previous
        early_ref[...] = earlier
        grow_ref[...] = exponent
        rows = pl.ds(pl.multiple_of(block * BLOCK, BLOCK), BLOCK)
        for order in range(order_lines):
            for lane in range(0, width, LANES):
                cut = min(LANES, kept - lane)
                part_of = lines[lane // LANES, pl.ds(order, BLOCK, stride=order_lines), :]
                table[order, rows, lane : lane + cut] = part_of[:, :cut].astype(table.dtype)

    def rows_from(device, lines_off):
        base = pl.multiple_of(device * block_rows + lines_off * ROWS, 2 * ROWS)
        return pl.ds(base, block_rows - lines_off * ROWS)

    def degree_copy(slot, device, lines_off=0):
        chunk = owner_chunk(me, slot, count)
        return pltpu.make_async_remote_copy(
            sums_out.at[slot, rows_from(device, lines_off)],
            out_ref.at[chunk, rows_from(0, lines_off)],
            send_two.at[slot, device],
            recv_two.at[chunk],
            device_id=(part, device),
            device_id_type=MESH,
        )

    def own_degrees(slot, lines_off=0):
        chunk = owner_chunk(me, slot, count)
        return pltpu.make_async_copy(
            sums_out.at[slot, rows_from(me, lines_off)],
            out_ref.at[chunk, rows_from(0, lines_off)],
            recv_two.at[chunk],
        )

    def each_target(slot, chosen, remote, local):
        first_line = owner_chunk(me, slot, count) * ROWS

        @pl.loop(1, count)
        def _(ahead):
            device = (me + ahead) % count

            @pl.when((first_line <= device * DEG_DEV) & chosen(device))
            def _():
                remote(slot, device, 0)

        @pl.when((first_line <= me * DEG_DEV) & chosen(me))
        def _():
            local(slot, 0)

        device = first_line // DEG_DEV
        for lines_off in range(2, DEG_DEV, 2):
            hit = (first_line - device * DEG_DEV == lines_off) & chosen(device)

            @pl.when(hit & (device != me))
            def _():
                remote(slot, device, lines_off)

            @pl.when(hit & (device == me))
            def _():
                local(slot, lines_off)

    def send_degrees(slot, chosen):
        each_target(
            slot,
            chosen,
            lambda *where: degree_copy(*where).start(),
            lambda *where: own_degrees(*where).start(),
        )

    degree_line = lax.broadcasted_iota(jnp.int32, (degrees, 1), 0)
    sign_even = jnp.where(degree_line % 2 == 0, 1.0, -1.0).astype(jnp.float32)

    def unfold():
        blocks = landed_pair.at[pl.ds(0, count - 1)]
        pltpu.make_async_copy(blocks, blocks, pair_sems.at[1]).wait()
        own_pair().wait()
        spread_out[...] = jnp.zeros_like(spread_out)

        @pl.loop(0, count)
        def _(source):
            value = landed_pair[source].astype(jnp.float32)
            for lane in range(2):
                spread_out[lane, : 2 * short, :] = value[:, lane * LANES : (lane + 1) * LANES]
            for slot in range(2):
                last = jnp.concatenate(
                    [
                        spread_out[lane, pl.ds(slot * short + ROWS - 1, ROWS, stride=ROWS), :]
                        for lane in range(2)
                    ],
                    axis=1,
                )
                landed[slot, source, groups - 1] = jnp.concatenate(
                    [value[slot * short : (slot + 1) * short], last], axis=0
                ).astype(landed.dtype)

    def analyse(slot):
        def wait_landed(parts):
            blocks = landed.at[slot, pl.ds(0, count - 1), pl.ds(0, parts)]
            pltpu.make_async_copy(blocks, blocks, recv_sem.at[slot]).wait()
            for group in range(parts):
                own_copy(slot, group).wait()

        @pl.when(slot < CHUNKS - 1)
        def _():
            wait_landed(groups - 1)

        @pl.when(slot == CHUNKS - 1)
        def _():
            wait_landed(groups)

        @pl.when(slot == 0)
        def _():
            unfold()

        @pl.loop(0, ROWS // 2)
        def _(pair):
            rows = pl.ds(pl.multiple_of(pair * 2 * ROWS, 2 * ROWS), 2 * ROWS)
            both = landed[slot, :, :, rows, :].astype(jnp.float32)
            both = both.reshape(count * groups, 2, ROWS, WIDE)
            for odd in range(2):
                rhs = both[:, odd].reshape(count * places, WIDE).astype(jnp.bfloat16)
                lhs = table[slot * ROWS + 2 * pair + odd]
                north = jnp.dot(lhs, rhs[:kept], preferred_element_type=jnp.float32)
                mirror = jnp.dot(lhs, rhs[kept:], preferred_element_type=jnp.float32)
                sign = sign_even if odd == 0 else -sign_even
                result = (north + sign * mirror) * scales[:1]
                for lane in range(2):
                    sums[lane, pl.ds(2 * pair + odd, degrees, stride=ROWS), :] = result[
                        :, lane * LANES : (lane + 1) * LANES
                    ]

        @pl.loop(0, count)
        def _(device):
            rows = pl.ds(pl.multiple_of(device * block_rows, block_rows), block_rows)
            sums_out[slot, rows, :] = jnp.concatenate(
                [sums[0, rows, :], sums[1, rows, :]], axis=1
            ).astype(jnp.bfloat16)

    pltpu.make_async_copy(
        moments_all.at[pl.ds(0, count - 1)],
        moments_all.at[pl.ds(0, count - 1)],
        moment_recv,
    ).wait()
    gathered = jnp.sum(moments_all[...], axis=0)
    first = jnp.sum(gathered[:ROWS], axis=0, keepdims=True) / (longitudes * total_sine)
    second = jnp.sum(gathered[ROWS:], axis=0, keepdims=True) / (longitudes * total_sine)
    spread = jnp.sqrt(second - first * first + 1e-05)
    gain = gain_ref[...]
    factor = jnp.concatenate([gain] * S, axis=1) / spread
    scales[:1] = jnp.concatenate([factor, factor], axis=1)
    scales[1:2] = jnp.concatenate([longitudes * first, jnp.zeros_like(first)], axis=1)

    pl.loop(groups + 1, 2 * groups - 1)(transform)

    @pl.loop(0, CHUNKS)
    def _(slot):
        @pl.when((slot < CHUNKS - 1) | has_last)
        def _():
            analyse(slot)
            send_degrees(slot, crosses)

        @pl.when(slot == 0)
        def _():
            pl.loop(2 * groups, CHUNKS * groups)(transform)

        @pl.when(slot == 1)
        def _():
            send_degrees(0, lambda device: jnp.logical_not(crosses(device)))

        @pl.when(((slot < CHUNKS - 1) | has_last) & (slot > 0))
        def _():
            send_degrees(slot, lambda device: jnp.logical_not(crosses(device)))

    pltpu.make_async_copy(
        moments_all.at[pl.ds(0, count - 1)], moments_all.at[pl.ds(0, count - 1)], moment_send
    ).wait()

    def wait_orders(step, devices):
        rows = pl.ds(0, devices * ROWS * ROWS)
        pltpu.make_async_copy(
            outgoing.at[step, rows], outgoing.at[step, rows], send_sem.at[step]
        ).wait()

    for slot in range(CHUNKS - 1):
        for group in range(groups - 1):
            wait_orders(slot * groups + group, count - 1)
    blocks = paired.at[pl.ds(0, count - 1)]
    pltpu.make_async_copy(blocks, blocks, pair_sems.at[0]).wait()

    last_owners = count - count // PLANE

    @pl.loop((CHUNKS - 1) * groups, CHUNKS * groups)
    def _(step):
        @pl.when(has_last)
        def _():
            wait_orders(step, last_owners - 1)

        @pl.when(jnp.logical_not(has_last))
        def _():
            wait_orders(step, last_owners)

    @pl.loop(0, CHUNKS)
    def _(slot):
        @pl.when(has_chunk(slot, me))
        def _():
            each_target(
                slot,
                lambda device: device >= 0,
                lambda *where: degree_copy(*where).wait_send(),
                lambda *where: None,
            )

    @pl.loop(0, out_ref.shape[0])
    def _(chunk):
        low_line = chunk * ROWS - me * DEG_DEV

        @pl.when((low_line <= 0) | (low_line >= DEG_DEV))
        def _():
            pltpu.make_async_copy(blank, out_ref.at[chunk], recv_two.at[chunk]).wait()

    @pl.loop(0, DEG_DEV // ROWS + 1)
    def _(ahead):
        chunk = me * DEG_DEV // ROWS + 1 + ahead
        low_line = chunk * ROWS - me * DEG_DEV
        for lines_off in range(2, DEG_DEV, 2):

            @pl.when(low_line == lines_off)
            def _():
                blank_copy(chunk, lines_off).wait()
                rows = rows_from(0, lines_off)
                pltpu.make_async_copy(
                    blank.at[rows], out_ref.at[chunk, rows], recv_two.at[chunk]
                ).wait()


def scratch_of(count, band, longitudes):
    groups = -(-band // ROWS)
    places = groups * ROWS
    degrees = DEG_DEV * count
    lines_of = count * ROWS
    kept = count // 2 * places
    width = round_up(kept, LANES)
    order_lines = CHUNKS * ROWS
    state = (order_lines, width)
    bf16, f32 = jnp.bfloat16, jnp.float32
    return [
        ((CHUNKS, 2 * lines_of, longitudes), bf16),
        ((CHUNKS, 2 * lines_of, longitudes), bf16),
        ((ROWS, longitudes, LANES), f32),
        ((places // 2, longitudes, WIDE), bf16),
        ((places // 2, longitudes, WIDE), bf16),
        ((2, lines_of * ROWS, LANES), f32),
        ((CHUNKS * groups, lines_of * ROWS, WIDE), bf16),
        ((CHUNKS, count, groups, ROWS * ROWS, WIDE), bf16),
        ((2 * ROWS, LANES), f32),
        ((count, 2 * ROWS, LANES), f32),
        ((ROWS, WIDE), f32),
        ((order_lines, degrees, kept), bf16),
        (state, f32),
        (state, f32),
        (state, f32),
        (state, f32),
        (state, f32),
        ((width // LANES, BLOCK * order_lines, LANES), f32),
        ((2, degrees * ROWS, LANES), f32),
        ((CHUNKS, degrees * ROWS, WIDE), bf16),
        ((DEG_DEV * ROWS, WIDE), bf16),
        ((2, lines_of * ROWS, LANES), f32),
        ((count, 2 * ROWS * (ROWS - 1), WIDE), bf16),
        ((count, 2 * ROWS * (ROWS - 1), WIDE), bf16),
        ((2, 2 * ROWS * ROWS, LANES), f32),
    ]


def scratch_bytes(shapes):
    total = 0
    for shape, dtype in shapes:
        size = math.prod(shape[:-1]) * round_up(shape[-1], LANES)
        total += size * jnp.dtype(dtype).itemsize
    return total


def coefficients_of(grid_field, norm_gain, count):
    band, longitudes, columns = grid_field.shape
    groups = -(-band // ROWS)
    places = groups * ROWS
    order_count = DEG_DEV * count
    high, low = transform_tables(count, longitudes)
    sine, cosine, weight, logsine, total_sine = angle_tables(count, band, places)
    weight_scale = math.pi**1.5 / math.sqrt(count * band * longitudes)
    shapes = scratch_of(count, band, longitudes)
    dma = pltpu.SemaphoreType.DMA
    vmem = pl.BlockSpec(memory_space=pltpu.VMEM)
    anywhere = pl.BlockSpec(memory_space=pl.ANY)
    return pl.pallas_call(
        functools.partial(spectral_kernel, (count, band, longitudes, total_sine)),
        out_shape=jax.ShapeDtypeStruct((order_count // ROWS, DEG_DEV * ROWS, WIDE), jnp.bfloat16),
        in_specs=[
            anywhere,
            vmem,
            anywhere,
            anywhere,
            pl.BlockSpec(memory_space=pltpu.SMEM),
            vmem,
            vmem,
            vmem,
            vmem,
        ],
        out_specs=anywhere,
        scratch_shapes=[pltpu.VMEM(shape, dtype) for shape, dtype in shapes]
        + [
            dma((3,)),
            dma((2, CHUNKS)),
            dma((ROWS,)),
            dma,
            dma,
            dma((CHUNKS * groups,)),
            dma((CHUNKS,)),
            dma((CHUNKS * groups,)),
            dma((CHUNKS, count)),
            dma((order_count // ROWS,)),
            dma((order_count // ROWS,)),
        ],
        cost_estimate=pl.CostEstimate(
            flops=20 * 10**9, bytes_accessed=40 * 10**6, transcendentals=10**6
        ),
        compiler_params=pltpu.CompilerParams(
            collective_id=0, has_side_effects=True, vmem_limit_bytes=VMEM_CAP
        ),
    )(
        grid_field,
        norm_gain[None, :],
        jnp.asarray(high),
        jnp.asarray(low),
        jnp.asarray(sine),
        jnp.asarray(cosine),
        jnp.asarray((weight * weight_scale).astype(np.float32)),
        jnp.asarray(logsine),
        jnp.asarray(log_starts(order_count)),
    )


def filter_kernel(coef_ref, weight_ref, out_ref, coefs, outs, full_ref, in_sem, out_sem):
    pairs = coefs.shape[0]
    chunks = coefs.shape[1]
    orders = chunks * ROWS

    def fetch(pair):
        rows = pl.ds(pl.multiple_of(pair * 2 * ROWS, 2 * ROWS), 2 * ROWS)
        return pltpu.make_async_copy(coef_ref.at[:, rows, :], coefs.at[pair], in_sem.at[pair])

    def store(pair):
        return pltpu.make_async_copy(
            outs.at[pair], out_ref.at[pl.ds(2 * pair, 2)], out_sem.at[pair]
        )

    for pair in range(pairs):
        fetch(pair).start()

    full_ref[...] = jnp.zeros_like(full_ref)
    for pair in range(pairs):
        for odd in range(2):
            degree = 2 * pair + odd
            real, imag = weight_ref[degree, 0], weight_ref[degree, 1]
            for sample in range(S):
                for side, halves in enumerate(((real, imag), (-imag, real))):
                    for target, block in enumerate(halves):
                        row = side * S * C + sample * C
                        lane = target * S * C + sample * C
                        full_ref[degree, row : row + C, lane : lane + C] = block
        fetch(pair).wait()
        both = coefs[pair].astype(jnp.float32).reshape(chunks, 2, ROWS, WIDE)
        for odd in range(2):
            value = both[:, odd].reshape(orders, WIDE).astype(jnp.bfloat16)
            outs[pair, odd] = jnp.dot(
                value, full_ref[2 * pair + odd], preferred_element_type=jnp.float32
            ).astype(outs.dtype)
        store(pair).start()

    @pl.loop(0, pairs)
    def _(pair):
        store(pair).wait()


def apply_filter(coefficients, filter_weight):
    chunks = coefficients.shape[0]
    degrees = filter_weight.shape[0]
    pairs = degrees // 2
    orders = chunks * ROWS
    anywhere = pl.BlockSpec(memory_space=pl.ANY)
    return pl.pallas_call(
        filter_kernel,
        out_shape=jax.ShapeDtypeStruct((degrees, orders, WIDE), jnp.bfloat16),
        in_specs=[anywhere, pl.BlockSpec(memory_space=pltpu.VMEM)],
        out_specs=anywhere,
        scratch_shapes=[
            pltpu.VMEM((pairs, chunks, 2 * ROWS, WIDE), jnp.bfloat16),
            pltpu.VMEM((pairs, 2, orders, WIDE), jnp.bfloat16),
            pltpu.VMEM((degrees, WIDE, WIDE), jnp.bfloat16),
            pltpu.SemaphoreType.DMA((pairs,)),
            pltpu.SemaphoreType.DMA((pairs,)),
        ],
        compiler_params=pltpu.CompilerParams(vmem_limit_bytes=VMEM_CAP),
    )(coefficients, filter_weight)


def body(grid_field, norm_gain, filter_weight):
    count = lax.axis_size("lat")
    band, longitudes, columns = grid_field.shape
    fits = scratch_bytes(scratch_of(count, band, longitudes)) < VMEM_CAP - 3 * 1024 * 1024
    if count % PLANE or band % ROWS != ROWS - 1 or band < 2 * ROWS or not fits:
        return plain_body(grid_field, norm_gain, filter_weight)
    coefficients = coefficients_of(grid_field, norm_gain, count)
    return apply_filter(coefficients, filter_weight)


def solution(mesh):
    in_specs = (P("lat", None, "parts"), P("parts"), P("lat", None, None, "parts"))
    out_specs = P("lat", None, "parts")
    return jax.shard_map(body, mesh=mesh, in_specs=in_specs, out_specs=out_specs, check_vma=False)
```

```python
import functools
import math

import jax
import jax.numpy as jnp
import numpy as np
from jax import lax
from jax.experimental import pallas as pl
from jax.experimental.pallas import tpu as pltpu
from jax.sharding import PartitionSpec as P

C = 64
S = 2
DEG_DEV = 22
ORDER_PAD = 24
BLOCK = 16
LANES = 128


def round_up(value, step):
    return -(-value // step) * step


def legendre_kernel(
    orders_ref, cosine_ref, weights_ref, mant_ref, exp_ref, out_ref, prev_ref, early_ref, grow_ref, rows_ref
):
    block = pl.program_id(0)
    width = cosine_ref.shape[1]
    kept_width = out_ref.shape[2]

    @pl.when(block == 0)
    def _():
        prev_ref[...] = jnp.zeros_like(prev_ref)
        early_ref[...] = jnp.zeros_like(early_ref)
        grow_ref[...] = jnp.zeros_like(grow_ref)

    orders = orders_ref[...]
    narrow = orders[:, :LANES]
    order_sq = narrow * narrow
    cosine = cosine_ref[...]
    weights = weights_ref[...]
    limit = 2.0**64
    shrink = 2.0 ** (-64)
    previous, earlier, exponent = prev_ref[...], early_ref[...], grow_ref[...]
    first = (block * BLOCK).astype(jnp.float32)

    def widen(value):
        return jnp.concatenate([value] * (width // LANES), axis=1)

    for step in range(BLOCK):
        degree = first + float(step)
        upper = jnp.sqrt(
            (4.0 * degree * degree - 1.0) / jnp.maximum(degree * degree - order_sq, 1.0)
        )
        below = degree - 1.0
        lower = jnp.sqrt(
            jnp.maximum(below * below - order_sq, 0.0)
            / jnp.maximum(jnp.full_like(order_sq, 4.0 * below * below - 1.0), 1.0)
        )
        recurred = widen(upper) * (cosine * previous - widen(lower) * earlier)
        at_start = orders == degree
        current = jnp.where(at_start, mant_ref[...], jnp.where(orders < degree, recurred, 0.0))
        exponent = jnp.where(at_start, exp_ref[...], exponent)
        value = weights * (current * jnp.exp2(exponent))
        for lane in range(width // LANES):
            rows_ref[lane, step * ORDER_PAD : (step + 1) * ORDER_PAD, :] = value[
                :, lane * LANES : (lane + 1) * LANES
            ]
        large = jnp.abs(current) > limit
        earlier = jnp.where(large, previous * shrink, previous)
        previous = jnp.where(large, current * shrink, current)
        exponent = jnp.where(large, exponent + 64.0, exponent)

    prev_ref[...] = previous
    early_ref[...] = earlier
    grow_ref[...] = exponent
    for order in range(DEG_DEV):
        for lane in range(0, width, LANES):
            cut = min(LANES, kept_width - lane)
            piece = rows_ref[lane // LANES, pl.ds(order, BLOCK, stride=ORDER_PAD), :]
            out_ref[order, :, lane : lane + cut] = piece[:, :cut].astype(out_ref.dtype)


def legendre_table(colatitude, first_order, degrees, weight_scale):
    rows = colatitude.shape[0]
    width = round_up(rows, LANES)
    colat = jnp.concatenate([colatitude, jnp.full((width - rows,), 0.5 * math.pi, jnp.float32)])
    orders = (first_order + jnp.arange(ORDER_PAD, dtype=jnp.int32)).astype(jnp.float32)
    sine_rows = jnp.sin(colat)
    log_start = 0.5 * jnp.log((2.0 * orders + 1.0) / (4.0 * math.pi)) + 0.5 * (
        lax.lgamma(orders + 0.5) - lax.lgamma(orders + 1.0) - 0.5 * math.log(math.pi)
    )
    log_diag = log_start[:, None] + orders[:, None] * jnp.log(sine_rows)[None, :]
    start_exp = 64.0 * jnp.floor(log_diag / (64.0 * math.log(2.0)))
    start_mant = jnp.exp(log_diag - start_exp * math.log(2.0))
    state = (ORDER_PAD, width)
    whole = pl.BlockSpec(state, lambda i: (0, 0))
    line = pl.BlockSpec((1, width), lambda i: (0, 0))
    return pl.pallas_call(
        legendre_kernel,
        grid=(degrees // BLOCK,),
        out_shape=jax.ShapeDtypeStruct((DEG_DEV, degrees, rows), jnp.bfloat16),
        in_specs=[whole, line, line, whole, whole],
        out_specs=pl.BlockSpec((DEG_DEV, BLOCK, rows), lambda i: (0, i, 0)),
        scratch_shapes=[
            pltpu.VMEM(state, jnp.float32),
            pltpu.VMEM(state, jnp.float32),
            pltpu.VMEM(state, jnp.float32),
            pltpu.VMEM((width // LANES, BLOCK * ORDER_PAD, LANES), jnp.float32),
        ],
        cost_estimate=pl.CostEstimate(
            flops=degrees * ORDER_PAD * width * 2000,
            bytes_accessed=DEG_DEV * degrees * rows * 2,
            transcendentals=degrees * ORDER_PAD * width,
        ),
        compiler_params=pltpu.CompilerParams(vmem_limit_bytes=24 * 1024 * 1024),
    )(
        jnp.broadcast_to(orders[:, None], state),
        jnp.cos(colat)[None, :],
        (weight_scale * sine_rows)[None, :],
        start_mant,
        start_exp,
    )


def expand_filter(filter_weight):
    real_part = filter_weight[:, 0]
    imag_part = filter_weight[:, 1]
    from_real = jnp.stack([real_part, imag_part], axis=1)
    from_imag = jnp.stack([-imag_part, real_part], axis=1)
    mixing = jnp.stack([from_real, from_imag], axis=1)
    same = jnp.eye(S, dtype=filter_weight.dtype)
    full = mixing.transpose(0, 1, 3, 2, 4)[:, :, None, :, :, None, :] * same[None, None, :, None, None, :, None]
    return full.reshape(filter_weight.shape[0], 2 * S * C, 2 * S * C)


def mix_kernel(sin_ref, cos_ref, weight_ref, out_ref, rows_ref):
    sources, degrees, orders, half = cos_ref.shape
    for degree in range(degrees):
        for source in range(sources):
            rows = slice(source * orders, (source + 1) * orders)
            rows_ref[degree, rows, :half] = cos_ref[source, degree].astype(jnp.float32)
            rows_ref[degree, rows, half:] = sin_ref[source, degree].astype(jnp.float32)
        out_ref[degree] = jnp.dot(
            rows_ref[degree].astype(jnp.bfloat16),
            weight_ref[degree],
            preferred_element_type=jnp.float32,
        ).astype(out_ref.dtype)


def mix(coef_sin, coef_cos, weights):
    sources, degrees, orders, half = coef_cos.shape
    wide = weights.shape[2]
    step = 2
    piece = pl.BlockSpec((sources, step, orders, half), lambda i: (0, i, 0, 0))
    return pl.pallas_call(
        mix_kernel,
        grid=(degrees // step,),
        out_shape=jax.ShapeDtypeStruct((degrees, sources * orders, wide), jnp.bfloat16),
        in_specs=[piece, piece, pl.BlockSpec((step, 2 * half, wide), lambda i: (i, 0, 0))],
        out_specs=pl.BlockSpec((step, sources * orders, wide), lambda i: (i, 0, 0)),
        scratch_shapes=[pltpu.VMEM((step, sources * orders, 2 * half), jnp.float32)],
        compiler_params=pltpu.CompilerParams(vmem_limit_bytes=24 * 1024 * 1024),
    )(coef_sin, coef_cos, weights)


def fourier_matrix(orders, longitudes):
    phases = (np.arange(orders)[:, None] * np.arange(longitudes)[None, :]) % longitudes
    angles = 2.0 * np.pi * phases / longitudes
    return np.stack([np.cos(angles), -np.sin(angles)]).astype(np.float32)


def plain_body(grid_field, norm_gain, filter_weight):
    device_index = lax.axis_index("lat")
    lat_count = lax.axis_size("lat")
    band_rows, longitudes, columns = grid_field.shape
    total_lat = band_rows * lat_count
    order_count = DEG_DEV * lat_count
    all_rows = jnp.arange(total_lat, dtype=jnp.int32)
    colat_all = math.pi * (all_rows.astype(jnp.float32) + 0.5) / total_lat
    sine_all = jnp.sin(colat_all)
    own_rows = device_index * band_rows + jnp.arange(band_rows, dtype=jnp.int32)
    sine_own = jnp.sin(math.pi * (own_rows.astype(jnp.float32) + 0.5) / total_lat)

    first = jnp.einsum("j,jnx->x", sine_own, grid_field, precision=lax.Precision.HIGHEST)
    second = jnp.einsum(
        "j,jnx->x", sine_own, grid_field * grid_field, precision=lax.Precision.HIGHEST
    )
    band_mean = first / (longitudes * jnp.sum(sine_own))
    denominator_rows = jnp.float32(longitudes)
    cos_table, sin_table = fourier_matrix(order_count, longitudes)

    def transform(table):
        return jnp.einsum(
            "mn,jnx->mjx", jnp.asarray(table), grid_field, precision=lax.Precision.HIGH
        )

    def to_orders(raw):
        return lax.all_to_all(
            raw.astype(jnp.bfloat16), "lat", split_axis=0, concat_axis=1, tiled=True
        )

    def to_degrees(sums):
        return lax.all_to_all(
            sums, "lat", split_axis=0, concat_axis=0
        )

    received_sin = to_orders(transform(sin_table))
    constant = jnp.arange(order_count) == 0
    shift = jnp.where(constant[:, None, None], denominator_rows * band_mean, 0.0)
    received_cos = to_orders(transform(cos_table) - shift)

    weight_scale = math.pi**1.5 / math.sqrt(total_lat * longitudes)
    legendre = legendre_table(colat_all, device_index * DEG_DEV, order_count, weight_scale)

    def analyse(received):
        return jnp.einsum("mlj,mjx->mlx", legendre, received, preferred_element_type=jnp.float32)

    def by_degree(sums):
        ordered = sums.astype(jnp.bfloat16).transpose(1, 0, 2)
        return ordered.reshape(lat_count, DEG_DEV, DEG_DEV, columns)

    sums_sin = by_degree(analyse(received_sin))
    moments, sums_sin = lax.optimization_barrier(
        (jnp.stack([first, second, band_mean]), sums_sin)
    )
    gathered, sums_sin = lax.optimization_barrier((lax.all_gather(moments, "lat"), sums_sin))
    denominator = longitudes * jnp.sum(sine_all)
    average = jnp.sum(gathered[:, 0], axis=0) / denominator
    mean_square = jnp.sum(gathered[:, 1], axis=0) / denominator
    spread = jnp.sqrt(mean_square - average * average + 1e-05)
    factor = jnp.tile(norm_gain, S) / spread
    coef_sin = to_degrees(sums_sin)
    band_sums = jnp.sum(
        legendre[0].astype(jnp.float32).reshape(order_count, lat_count, band_rows), axis=2
    )
    level = jnp.dot(
        band_sums,
        denominator_rows * (gathered[:, 2] - average),
        precision=lax.Precision.HIGHEST,
    )
    here = (device_index == 0) & (jnp.arange(DEG_DEV) == 0)
    coef_cos = to_degrees(
        by_degree(analyse(received_cos) + jnp.where(here[:, None, None], level[None], 0.0))
    )

    expanded = expand_filter(filter_weight)
    expanded = (expanded * jnp.tile(factor, 2)[None, :, None]).astype(jnp.bfloat16)

    return mix(coef_sin, coef_cos, expanded)


MESH = pl.DeviceIdType.MESH
ROWS = 8
WIDE = 2 * LANES
CHUNKS = 3
PLANE = 4
PLANE_CHUNKS = PLANE * CHUNKS - 1
VMEM_CAP = 60 * 1024 * 1024


def owns_last(device):
    return device % PLANE != 1


def owner_chunk(device, slot, count):
    plane, inner = count // PLANE - 1 - device // PLANE, device % PLANE
    first = 1 // (plane + inner + 1)
    at = slot + first * (CHUNKS - 1 - 2 * slot)
    return PLANE_CHUNKS * plane + PLANE * at + inner - (at // (CHUNKS - 1)) * ((inner + 2) // PLANE)


def transform_tables(count, longitudes):
    table = np.zeros((CHUNKS, 2, count, ROWS, longitudes), np.float64)
    for slot in range(CHUNKS):
        for device in range(count):
            if slot == CHUNKS - 1 and not owns_last(device):
                continue
            orders = owner_chunk(device, slot, count) * ROWS + np.arange(ROWS)
            phases = (orders[:, None] * np.arange(longitudes)[None, :]) % longitudes
            angles = 2.0 * np.pi * phases / longitudes
            table[slot, 0, device] = np.cos(angles)
            table[slot, 1, device] = -np.sin(angles)
    table = table.reshape(CHUNKS, 2 * count * ROWS, longitudes).astype(np.float32)
    high = table.astype(jnp.bfloat16)
    low = (table - high.astype(np.float32)).astype(jnp.bfloat16)
    return high, low


def angle_tables(count, band, places):
    colat = np.pi * (np.arange(count * band) + 0.5) / (count * band)
    by_place = np.full((count, places), 0.5 * np.pi)
    valid = np.zeros((count, places))
    for device in range(count):
        rows = colat[device * band : (device + 1) * band]
        by_place[device, :band] = rows if device < count // 2 else rows[::-1]
        valid[device, :band] = 1.0
    sine_places = np.sin(by_place) * valid
    north = by_place[: count // 2].reshape(1, -1)
    weight = sine_places[: count // 2].reshape(1, -1)
    width = round_up(north.shape[1], LANES)
    north = np.pad(north, ((0, 0), (0, width - north.shape[1])), constant_values=0.5 * np.pi)
    weight = np.pad(weight, ((0, 0), (0, width - weight.shape[1])))
    return (
        sine_places.reshape(-1).astype(np.float32),
        np.cos(north).astype(np.float32),
        weight,
        np.log(np.sin(north)).astype(np.float32),
        float(np.sum(np.sin(colat))),
    )


def log_starts(order_count):
    values = [
        0.5 * math.log((2.0 * m + 1.0) / (4.0 * math.pi))
        + 0.5 * (math.lgamma(m + 0.5) - math.lgamma(m + 1.0) - 0.5 * math.log(math.pi))
        for m in range(order_count)
    ]
    return np.asarray(values, np.float32)[:, None]


def spectral_kernel(
    sizes,
    field_ref,
    gain_ref,
    high_ref,
    low_ref,
    sine_ref,
    cosine_ref,
    weight_ref,
    logsine_ref,
    start_ref,
    out_ref,
    high,
    low,
    stage,
    field_high,
    field_low,
    turned,
    outgoing,
    landed,
    moments,
    moments_all,
    scales,
    table,
    prev_ref,
    early_ref,
    grow_ref,
    mant_ref,
    exp_ref,
    lines,
    sums,
    sums_out,
    blank,
    held,
    paired,
    landed_pair,
    spread_out,
    pair_sems,
    table_sem,
    stage_sem,
    moment_send,
    moment_recv,
    send_sem,
    recv_sem,
    local_sem,
    send_two,
    recv_two,
    blank_sem,
):
    count, band, longitudes, total_sine = sizes
    me = lax.axis_index("lat")
    part = lax.axis_index("parts")
    half = count // 2
    south = me // half
    slot_of_me = me + south * (half + count - 1 - 2 * me)
    groups = outgoing.shape[0] // CHUNKS
    places = groups * ROWS
    degrees = table.shape[1]
    kept = table.shape[2]
    width = cosine_ref.shape[1]
    block_rows = DEG_DEV * ROWS
    zero_owner = count - PLANE
    has_last = owns_last(me)

    def has_chunk(slot, device):
        return (slot < CHUNKS - 1) | owns_last(device)

    def table_copies(slot):
        return (
            pltpu.make_async_copy(high_ref.at[slot], high.at[slot], table_sem.at[0, slot]),
            pltpu.make_async_copy(low_ref.at[slot], low.at[slot], table_sem.at[1, slot]),
        )

    def row_copy(place):
        row = place + south * (band - 1 - 2 * place)
        at = place % ROWS
        return pltpu.make_async_copy(field_ref.at[row], stage.at[at], stage_sem.at[at])

    for place in range(2):
        row_copy(place).start()
    for copy in table_copies(0):
        copy.start()
    for place in range(2, ROWS):
        row_copy(place).start()
    for slot in range(1, CHUNKS):
        for copy in table_copies(slot):
            copy.start()

    barrier = pltpu.get_barrier_semaphore()

    @pl.loop(1, count)
    def _(step):
        pl.semaphore_signal(
            barrier, inc=1, device_id=(part, (me + step) % count), device_id_type=MESH
        )

    moments[...] = jnp.zeros_like(moments)
    for place in range(band, places):
        lanes = slice((place % 2) * LANES, (place % 2 + 1) * LANES)
        field_high[place // 2, :, lanes] = jnp.zeros((longitudes, LANES), jnp.bfloat16)
        field_low[place // 2, :, lanes] = jnp.zeros((longitudes, LANES), jnp.bfloat16)

    piece = longitudes // 6

    def split_row(place, lanes):
        at = place % ROWS
        pair = place // 2
        total = jnp.zeros((ROWS, LANES), jnp.float32)
        square = jnp.zeros((ROWS, LANES), jnp.float32)
        for first in range(0, longitudes, piece):
            value = stage[at, first : first + piece, :]
            top = value.astype(jnp.bfloat16)
            field_high[pair, first : first + piece, lanes] = top
            field_low[pair, first : first + piece, lanes] = (
                value - top.astype(jnp.float32)
            ).astype(jnp.bfloat16)
            total += jnp.sum(value.reshape(-1, ROWS, LANES), axis=0)
            square += jnp.sum((value * value).reshape(-1, ROWS, LANES), axis=0)
        sine = sine_ref[me * places + place]
        moments[:ROWS] += sine * total
        moments[ROWS:] += sine * square

    def take_row(place, lanes):
        row_copy(place).wait()
        split_row(place, lanes)

        @pl.when(place + ROWS < band)
        def _():
            row_copy(place + ROWS).start()

    def take_group(group):
        @pl.loop(0, ROWS // 2)
        def _(pair):
            place = group * ROWS + 2 * pair
            take_row(place, slice(0, LANES))

            @pl.when(place + 1 < band)
            def _():
                take_row(place + 1, slice(LANES, WIDE))

    halves = (slice(0, LANES), slice(LANES, WIDE))
    lines_of = count * ROWS

    def project(slot, at):
        product = jnp.dot(high[slot], field_high[at], preferred_element_type=jnp.float32)
        product += jnp.dot(high[slot], field_low[at], preferred_element_type=jnp.float32)
        product += jnp.dot(low[slot], field_high[at], preferred_element_type=jnp.float32)
        return product

    def turn(product, pair):
        for side in range(2):
            for row in range(2):
                turned[side, pl.ds(2 * pair + row, lines_of, stride=ROWS), :] = product[
                    side * lines_of : (side + 1) * lines_of, row * LANES : (row + 1) * LANES
                ]


    def blank_copy(chunk, lines_off):
        rows = pl.ds(0, lines_off * ROWS)
        return pltpu.make_async_copy(
            blank.at[rows], out_ref.at[chunk, rows], blank_sem.at[chunk]
        )

    def moment_copy(device):
        return pltpu.make_async_remote_copy(
            moments,
            moments_all.at[me],
            moment_send,
            moment_recv,
            device_id=(part, device),
            device_id_type=MESH,
        )

    def order_copy(slot, group, device):
        step = slot * groups + group
        rows = pl.ds(pl.multiple_of(device * ROWS * ROWS, ROWS * ROWS), ROWS * ROWS)
        return pltpu.make_async_remote_copy(
            outgoing.at[step, rows],
            landed.at[slot, slot_of_me, group],
            send_sem.at[step],
            recv_sem.at[slot],
            device_id=(part, device),
            device_id_type=MESH,
        )

    def own_copy(slot, group):
        step = slot * groups + group
        rows = pl.ds(pl.multiple_of(me * ROWS * ROWS, ROWS * ROWS), ROWS * ROWS)
        return pltpu.make_async_copy(
            outgoing.at[step, rows], landed.at[slot, slot_of_me, group], local_sem.at[step]
        )

    short = ROWS * (ROWS - 1)

    def pair_copy(device):
        return pltpu.make_async_remote_copy(
            paired.at[device],
            landed_pair.at[slot_of_me],
            pair_sems.at[0],
            pair_sems.at[1],
            device_id=(part, device),
            device_id_type=MESH,
        )

    def own_pair():
        return pltpu.make_async_copy(
            paired.at[me], landed_pair.at[slot_of_me], pair_sems.at[2]
        )

    def fold_last():
        @pl.loop(0, count)
        def _(device):
            first = device * ROWS * ROWS
            for side in range(2):
                last = turned[side, pl.ds(pl.multiple_of(first + short, ROWS), ROWS), :]
                turned[side, pl.ds(first + ROWS - 1, ROWS, stride=ROWS), :] = last

    def send_pairs():
        @pl.loop(0, count)
        def _(ahead):
            device = ((me // half + 1 + ahead // half) % 2) * half + (me + ahead) % half
            rows = pl.ds(pl.multiple_of(device * ROWS * ROWS, ROWS), short)
            paired[device] = jnp.concatenate(
                [
                    jnp.concatenate([source[0, rows, :], source[1, rows, :]], axis=1)
                    for source in (held, turned)
                ],
                axis=0,
            ).astype(jnp.bfloat16)

            @pl.when(device != me)
            def _():
                pair_copy(device).start()

            @pl.when(device == me)
            def _():
                own_pair().start()

    upper = count - count // PLANE

    def crosses(device):
        return (device >= upper) != (me >= upper)

    def send_group(slot, group, first, last):
        @pl.loop(first, last)
        def _(ahead):
            device = ((me // half + 1 + ahead // half) % 2) * half + (me + ahead) % half
            rows = pl.ds(pl.multiple_of(device * ROWS * ROWS, ROWS * ROWS), ROWS * ROWS)
            outgoing[slot * groups + group, rows, :] = jnp.concatenate(
                [turned[0, rows, :], turned[1, rows, :]], axis=1
            ).astype(jnp.bfloat16)

            @pl.when((device != me) & has_chunk(slot, device))
            def _():
                order_copy(slot, group, device).start()

            @pl.when((device == me) & has_chunk(slot, device))
            def _():
                own_copy(slot, group).start()

    def project_half(pair, part_of):
        lines_half = half * ROWS
        rows = [
            pl.ds(pl.multiple_of(side * lines_of + part_of * lines_half, lines_half), lines_half)
            for side in range(2)
        ]
        top = jnp.concatenate([high[0, row, :] for row in rows], axis=0)
        rest = jnp.concatenate([low[0, row, :] for row in rows], axis=0)
        product = jnp.dot(top, field_high[pair], preferred_element_type=jnp.float32)
        product += jnp.dot(top, field_low[pair], preferred_element_type=jnp.float32)
        product += jnp.dot(rest, field_high[pair], preferred_element_type=jnp.float32)
        return product

    def turn_half(product, pair, part_of):
        lines_half = half * ROWS
        for side in range(2):
            for row in range(2):
                at = part_of * lines_half * ROWS + 2 * pair + row
                turned[side, pl.ds(at, lines_half, stride=ROWS), :] = product[
                    side * lines_half : (side + 1) * lines_half, row * LANES : (row + 1) * LANES
                ]

    for row in range(2):
        take_row(row, halves[row])
    for copy in table_copies(0):
        copy.wait()
    other = (me // half + 1) % 2
    for pair in range(ROWS // 2):
        following = range(2 * pair + 2, 2 * pair + 4) if pair + 1 < ROWS // 2 else ()
        for place in following:
            row_copy(place).wait()
        product = project_half(pair, other)
        for place in following:
            split_row(place, halves[place % 2])
        turn_half(product, pair, other)
        for place in following:
            if place + ROWS < band:
                row_copy(place + ROWS).start()
    pl.semaphore_wait(barrier, count - 1)
    send_group(0, 0, 0, half)

    @pl.loop(0, ROWS // 2)
    def _(pair):
        turn_half(project_half(pair, 1 - other), pair, 1 - other)

    send_group(0, 0, half, count)

    def transform(step):
        slot, group = step // groups, step % groups

        @pl.when(step == 1)
        def _():
            pl.loop(1, groups)(take_group)
            moments_all[me] = moments[...]

            @pl.loop(1, count)
            def _(ahead):
                moment_copy((me + ahead) % count).start()

        @pl.when((step == 2 * groups - 1) | (step == 2 * groups))
        def _():
            for copy in table_copies(slot):
                copy.wait()

        @pl.loop(0, ROWS // 2)
        def _(pair):
            turn(project(slot, group * (ROWS // 2) + pair), pair)

        @pl.when(slot == CHUNKS - 1)
        def _():
            at = zero_owner * ROWS * ROWS
            turned[0, at : at + ROWS, :] -= scales[1:2, :LANES]

        folded = (group == groups - 1) & (slot < CHUNKS - 1)

        @pl.when(jnp.logical_not(folded))
        def _():
            send_group(slot, group, 0, count)

        @pl.when(folded)
        def _():
            fold_last()

            @pl.when(slot == 0)
            def _():
                held[...] = turned[...]

            @pl.when(slot > 0)
            def _():
                send_pairs()

    @pl.loop(1, groups + 2)
    def _(turn_at):
        tail = groups + (groups - 1) * (groups + 1 - turn_at)
        transform(jnp.where(turn_at < groups, turn_at, tail))

    blank[...] = jnp.zeros_like(blank)

    @pl.loop(0, out_ref.shape[0])
    def _(chunk):
        low_line = chunk * ROWS - me * DEG_DEV

        @pl.when(low_line >= DEG_DEV)
        def _():
            pltpu.make_async_copy(blank, out_ref.at[chunk], recv_two.at[chunk]).start()

    @pl.loop(0, DEG_DEV // ROWS + 1)
    def _(ahead):
        chunk = me * DEG_DEV // ROWS + 1 + ahead
        low_line = chunk * ROWS - me * DEG_DEV
        for lines_off in range(2, DEG_DEV, 2):

            @pl.when(low_line == lines_off)
            def _():
                blank_copy(chunk, lines_off).start()

    chunk_of = [owner_chunk(me, slot, count) for slot in range(CHUNKS)]
    lines_in = lax.broadcasted_iota(jnp.int32, (ROWS, width), 0)
    orders = jnp.concatenate(
        [(chunk * ROWS + lines_in).astype(jnp.float32) for chunk in chunk_of], axis=0
    )
    start = jnp.concatenate(
        [start_ref[pl.ds(pl.multiple_of(chunk * ROWS, ROWS), ROWS), :] for chunk in chunk_of], axis=0
    )
    start = jnp.broadcast_to(start, (CHUNKS * ROWS, width))

    def widen(value):
        return jnp.concatenate([value] * (width // LANES), axis=1)

    log_diag = start + orders * logsine_ref[...]
    start_exp = 64.0 * jnp.floor(log_diag / (64.0 * math.log(2.0)))
    exp_ref[...] = start_exp
    mant_ref[...] = jnp.exp(log_diag - start_exp * math.log(2.0))
    prev_ref[...] = jnp.zeros_like(prev_ref)
    early_ref[...] = jnp.zeros_like(early_ref)
    grow_ref[...] = jnp.zeros_like(grow_ref)
    order_lines = CHUNKS * ROWS

    @pl.loop(0, degrees // BLOCK)
    def _(block):
        narrow = orders[:, :LANES]
        order_sq = narrow * narrow
        cosine = cosine_ref[...]
        weights = weight_ref[...]
        limit = 2.0**64
        shrink = 2.0 ** (-64)
        previous, earlier, exponent = prev_ref[...], early_ref[...], grow_ref[...]
        first = (block * BLOCK).astype(jnp.float32)
        for step in range(BLOCK):
            degree = first + float(step)
            upper = jnp.sqrt(
                (4.0 * degree * degree - 1.0) / jnp.maximum(degree * degree - order_sq, 1.0)
            )
            below = degree - 1.0
            lower = jnp.sqrt(
                jnp.maximum(below * below - order_sq, 0.0)
                / jnp.maximum(jnp.full_like(order_sq, 4.0 * below * below - 1.0), 1.0)
            )
            recurred = widen(upper) * (cosine * previous - widen(lower) * earlier)
            at_start = orders == degree
            current = jnp.where(at_start, mant_ref[...], jnp.where(orders < degree, recurred, 0.0))
            exponent = jnp.where(at_start, exp_ref[...], exponent)
            value = weights * (current * jnp.exp2(exponent))
            for lane in range(width // LANES):
                lines[lane, step * order_lines : (step + 1) * order_lines, :] = value[
                    :, lane * LANES : (lane + 1) * LANES
                ]
            large = jnp.abs(current) > limit
            earlier = jnp.where(large, previous * shrink, previous)
            previous = jnp.where(large, current * shrink, current)
            exponent = jnp.where(large, exponent + 64.0, exponent)
        prev_ref[...] = previous
        early_ref[...] = earlier
        grow_ref[...] = exponent
        rows = pl.ds(pl.multiple_of(block * BLOCK, BLOCK), BLOCK)
        for order in range(order_lines):
            for lane in range(0, width, LANES):
                cut = min(LANES, kept - lane)
                part_of = lines[lane // LANES, pl.ds(order, BLOCK, stride=order_lines), :]
                table[order, rows, lane : lane + cut] = part_of[:, :cut].astype(table.dtype)

    def rows_from(device, lines_off):
        base = pl.multiple_of(device * block_rows + lines_off * ROWS, 2 * ROWS)
        return pl.ds(base, block_rows - lines_off * ROWS)

    def degree_copy(slot, device, lines_off=0):
        chunk = owner_chunk(me, slot, count)
        return pltpu.make_async_remote_copy(
            sums_out.at[slot, rows_from(device, lines_off)],
            out_ref.at[chunk, rows_from(0, lines_off)],
            send_two.at[slot, device],
            recv_two.at[chunk],
            device_id=(part, device),
            device_id_type=MESH,
        )

    def own_degrees(slot, lines_off=0):
        chunk = owner_chunk(me, slot, count)
        return pltpu.make_async_copy(
            sums_out.at[slot, rows_from(me, lines_off)],
            out_ref.at[chunk, rows_from(0, lines_off)],
            recv_two.at[chunk],
        )

    def each_target(slot, chosen, remote, local):
        first_line = owner_chunk(me, slot, count) * ROWS

        @pl.loop(0, count)
        def _(ahead):
            device = ((me // half + 1 + ahead // half) % 2) * half + (me + ahead) % half
            reached = first_line <= device * DEG_DEV

            @pl.when(reached & chosen(device) & (device != me))
            def _():
                remote(slot, device, 0)

        @pl.when((first_line <= me * DEG_DEV) & chosen(me))
        def _():
            local(slot, 0)

        device = first_line // DEG_DEV
        for lines_off in range(2, DEG_DEV, 2):
            hit = (first_line - device * DEG_DEV == lines_off) & chosen(device)

            @pl.when(hit & (device != me))
            def _():
                remote(slot, device, lines_off)

            @pl.when(hit & (device == me))
            def _():
                local(slot, lines_off)

    def send_degrees(slot, chosen):
        each_target(
            slot,
            chosen,
            lambda *where: degree_copy(*where).start(),
            lambda *where: own_degrees(*where).start(),
        )

    degree_line = lax.broadcasted_iota(jnp.int32, (degrees, 1), 0)
    sign_even = jnp.where(degree_line % 2 == 0, 1.0, -1.0).astype(jnp.float32)

    def unfold():
        blocks = landed_pair.at[pl.ds(0, count - 1)]
        pltpu.make_async_copy(blocks, blocks, pair_sems.at[1]).wait()
        own_pair().wait()
        spread_out[...] = jnp.zeros_like(spread_out)

        @pl.loop(0, count)
        def _(source):
            value = landed_pair[source].astype(jnp.float32)
            for lane in range(2):
                spread_out[lane, : 2 * short, :] = value[:, lane * LANES : (lane + 1) * LANES]
            for slot in range(2):
                last = jnp.concatenate(
                    [
                        spread_out[lane, pl.ds(slot * short + ROWS - 1, ROWS, stride=ROWS), :]
                        for lane in range(2)
                    ],
                    axis=1,
                )
                landed[slot, source, groups - 1] = jnp.concatenate(
                    [value[slot * short : (slot + 1) * short], last], axis=0
                ).astype(landed.dtype)

    def analyse(slot):
        def wait_landed(parts):
            blocks = landed.at[slot, pl.ds(0, count - 1), pl.ds(0, parts)]
            pltpu.make_async_copy(blocks, blocks, recv_sem.at[slot]).wait()
            for group in range(parts):
                own_copy(slot, group).wait()

        @pl.when(slot < CHUNKS - 1)
        def _():
            wait_landed(groups - 1)

        @pl.when(slot == CHUNKS - 1)
        def _():
            wait_landed(groups)

        @pl.when(slot == 0)
        def _():
            unfold()

        @pl.loop(0, ROWS // 2)
        def _(pair):
            rows = pl.ds(pl.multiple_of(pair * 2 * ROWS, 2 * ROWS), 2 * ROWS)
            both = landed[slot, :, :, rows, :].astype(jnp.float32)
            both = both.reshape(count * groups, 2, ROWS, WIDE)
            for odd in range(2):
                rhs = both[:, odd].reshape(count * places, WIDE).astype(jnp.bfloat16)
                lhs = table[slot * ROWS + 2 * pair + odd]
                north = jnp.dot(lhs, rhs[:kept], preferred_element_type=jnp.float32)
                mirror = jnp.dot(lhs, rhs[kept:], preferred_element_type=jnp.float32)
                sign = sign_even if odd == 0 else -sign_even
                result = (north + sign * mirror) * scales[:1]
                for lane in range(2):
                    sums[lane, pl.ds(2 * pair + odd, degrees, stride=ROWS), :] = result[
                        :, lane * LANES : (lane + 1) * LANES
                    ]

        @pl.loop(0, count)
        def _(device):
            rows = pl.ds(pl.multiple_of(device * block_rows, block_rows), block_rows)
            sums_out[slot, rows, :] = jnp.concatenate(
                [sums[0, rows, :], sums[1, rows, :]], axis=1
            ).astype(jnp.bfloat16)

    pltpu.make_async_copy(
        moments_all.at[pl.ds(0, count - 1)],
        moments_all.at[pl.ds(0, count - 1)],
        moment_recv,
    ).wait()
    gathered = jnp.sum(moments_all[...], axis=0)
    first = jnp.sum(gathered[:ROWS], axis=0, keepdims=True) / (longitudes * total_sine)
    second = jnp.sum(gathered[ROWS:], axis=0, keepdims=True) / (longitudes * total_sine)
    spread = jnp.sqrt(second - first * first + 1e-05)
    gain = gain_ref[...]
    factor = jnp.concatenate([gain] * S, axis=1) / spread
    scales[:1] = jnp.concatenate([factor, factor], axis=1)
    scales[1:2] = jnp.concatenate([longitudes * first, jnp.zeros_like(first)], axis=1)

    pl.loop(groups + 1, 2 * groups - 1)(transform)

    @pl.loop(0, CHUNKS)
    def _(slot):
        @pl.when((slot < CHUNKS - 1) | has_last)
        def _():
            analyse(slot)
            send_degrees(slot, crosses)

        @pl.when(slot == 0)
        def _():
            pl.loop(2 * groups, CHUNKS * groups)(transform)

        @pl.when(slot == 1)
        def _():
            send_degrees(0, lambda device: jnp.logical_not(crosses(device)))

        @pl.when(((slot < CHUNKS - 1) | has_last) & (slot > 0))
        def _():
            send_degrees(slot, lambda device: jnp.logical_not(crosses(device)))

    pltpu.make_async_copy(
        moments_all.at[pl.ds(0, count - 1)], moments_all.at[pl.ds(0, count - 1)], moment_send
    ).wait()

    def wait_orders(step, devices):
        rows = pl.ds(0, devices * ROWS * ROWS)
        pltpu.make_async_copy(
            outgoing.at[step, rows], outgoing.at[step, rows], send_sem.at[step]
        ).wait()

    for slot in range(CHUNKS - 1):
        for group in range(groups - 1):
            wait_orders(slot * groups + group, count - 1)
    blocks = paired.at[pl.ds(0, count - 1)]
    pltpu.make_async_copy(blocks, blocks, pair_sems.at[0]).wait()

    last_owners = count - count // PLANE

    @pl.loop((CHUNKS - 1) * groups, CHUNKS * groups)
    def _(step):
        @pl.when(has_last)
        def _():
            wait_orders(step, last_owners - 1)

        @pl.when(jnp.logical_not(has_last))
        def _():
            wait_orders(step, last_owners)

    @pl.loop(0, CHUNKS)
    def _(slot):
        @pl.when(has_chunk(slot, me))
        def _():
            each_target(
                slot,
                lambda device: device >= 0,
                lambda *where: degree_copy(*where).wait_send(),
                lambda *where: None,
            )

    @pl.loop(0, out_ref.shape[0])
    def _(chunk):
        low_line = chunk * ROWS - me * DEG_DEV

        @pl.when((low_line <= 0) | (low_line >= DEG_DEV))
        def _():
            pltpu.make_async_copy(blank, out_ref.at[chunk], recv_two.at[chunk]).wait()

    @pl.loop(0, DEG_DEV // ROWS + 1)
    def _(ahead):
        chunk = me * DEG_DEV // ROWS + 1 + ahead
        low_line = chunk * ROWS - me * DEG_DEV
        for lines_off in range(2, DEG_DEV, 2):

            @pl.when(low_line == lines_off)
            def _():
                blank_copy(chunk, lines_off).wait()
                rows = rows_from(0, lines_off)
                pltpu.make_async_copy(
                    blank.at[rows], out_ref.at[chunk, rows], recv_two.at[chunk]
                ).wait()


def scratch_of(count, band, longitudes):
    groups = -(-band // ROWS)
    places = groups * ROWS
    degrees = DEG_DEV * count
    lines_of = count * ROWS
    kept = count // 2 * places
    width = round_up(kept, LANES)
    order_lines = CHUNKS * ROWS
    state = (order_lines, width)
    bf16, f32 = jnp.bfloat16, jnp.float32
    return [
        ((CHUNKS, 2 * lines_of, longitudes), bf16),
        ((CHUNKS, 2 * lines_of, longitudes), bf16),
        ((ROWS, longitudes, LANES), f32),
        ((places // 2, longitudes, WIDE), bf16),
        ((places // 2, longitudes, WIDE), bf16),
        ((2, lines_of * ROWS, LANES), f32),
        ((CHUNKS * groups, lines_of * ROWS, WIDE), bf16),
        ((CHUNKS, count, groups, ROWS * ROWS, WIDE), bf16),
        ((2 * ROWS, LANES), f32),
        ((count, 2 * ROWS, LANES), f32),
        ((ROWS, WIDE), f32),
        ((order_lines, degrees, kept), bf16),
        (state, f32),
        (state, f32),
        (state, f32),
        (state, f32),
        (state, f32),
        ((width // LANES, BLOCK * order_lines, LANES), f32),
        ((2, degrees * ROWS, LANES), f32),
        ((CHUNKS, degrees * ROWS, WIDE), bf16),
        ((DEG_DEV * ROWS, WIDE), bf16),
        ((2, lines_of * ROWS, LANES), f32),
        ((count, 2 * ROWS * (ROWS - 1), WIDE), bf16),
        ((count, 2 * ROWS * (ROWS - 1), WIDE), bf16),
        ((2, 2 * ROWS * ROWS, LANES), f32),
    ]


def scratch_bytes(shapes):
    total = 0
    for shape, dtype in shapes:
        size = math.prod(shape[:-1]) * round_up(shape[-1], LANES)
        total += size * jnp.dtype(dtype).itemsize
    return total


def coefficients_of(grid_field, norm_gain, count):
    band, longitudes, columns = grid_field.shape
    groups = -(-band // ROWS)
    places = groups * ROWS
    order_count = DEG_DEV * count
    high, low = transform_tables(count, longitudes)
    sine, cosine, weight, logsine, total_sine = angle_tables(count, band, places)
    weight_scale = math.pi**1.5 / math.sqrt(count * band * longitudes)
    shapes = scratch_of(count, band, longitudes)
    dma = pltpu.SemaphoreType.DMA
    vmem = pl.BlockSpec(memory_space=pltpu.VMEM)
    anywhere = pl.BlockSpec(memory_space=pl.ANY)
    return pl.pallas_call(
        functools.partial(spectral_kernel, (count, band, longitudes, total_sine)),
        out_shape=jax.ShapeDtypeStruct((order_count // ROWS, DEG_DEV * ROWS, WIDE), jnp.bfloat16),
        in_specs=[
            anywhere,
            vmem,
            anywhere,
            anywhere,
            pl.BlockSpec(memory_space=pltpu.SMEM),
            vmem,
            vmem,
            vmem,
            vmem,
        ],
        out_specs=anywhere,
        scratch_shapes=[pltpu.VMEM(shape, dtype) for shape, dtype in shapes]
        + [
            dma((3,)),
            dma((2, CHUNKS)),
            dma((ROWS,)),
            dma,
            dma,
            dma((CHUNKS * groups,)),
            dma((CHUNKS,)),
            dma((CHUNKS * groups,)),
            dma((CHUNKS, count)),
            dma((order_count // ROWS,)),
            dma((order_count // ROWS,)),
        ],
        cost_estimate=pl.CostEstimate(
            flops=20 * 10**9, bytes_accessed=40 * 10**6, transcendentals=10**6
        ),
        compiler_params=pltpu.CompilerParams(
            collective_id=0, has_side_effects=True, vmem_limit_bytes=VMEM_CAP
        ),
    )(
        grid_field,
        norm_gain[None, :],
        jnp.asarray(high),
        jnp.asarray(low),
        jnp.asarray(sine),
        jnp.asarray(cosine),
        jnp.asarray((weight * weight_scale).astype(np.float32)),
        jnp.asarray(logsine),
        jnp.asarray(log_starts(order_count)),
    )


def filter_kernel(coef_ref, weight_ref, out_ref, coefs, outs, full_ref, in_sem, out_sem):
    pairs = coefs.shape[0]
    chunks = coefs.shape[1]
    orders = chunks * ROWS

    def fetch(pair):
        rows = pl.ds(pl.multiple_of(pair * 2 * ROWS, 2 * ROWS), 2 * ROWS)
        return pltpu.make_async_copy(coef_ref.at[:, rows, :], coefs.at[pair], in_sem.at[pair])

    def store(pair):
        return pltpu.make_async_copy(
            outs.at[pair], out_ref.at[pl.ds(2 * pair, 2)], out_sem.at[pair]
        )

    for pair in range(pairs):
        fetch(pair).start()

    full_ref[...] = jnp.zeros_like(full_ref)
    for pair in range(pairs):
        for odd in range(2):
            degree = 2 * pair + odd
            real, imag = weight_ref[degree, 0], weight_ref[degree, 1]
            for sample in range(S):
                for side, halves in enumerate(((real, imag), (-imag, real))):
                    for target, block in enumerate(halves):
                        row = side * S * C + sample * C
                        lane = target * S * C + sample * C
                        full_ref[degree, row : row + C, lane : lane + C] = block
        fetch(pair).wait()
        both = coefs[pair].astype(jnp.float32).reshape(chunks, 2, ROWS, WIDE)
        for odd in range(2):
            value = both[:, odd].reshape(orders, WIDE).astype(jnp.bfloat16)
            outs[pair, odd] = jnp.dot(
                value, full_ref[2 * pair + odd], preferred_element_type=jnp.float32
            ).astype(outs.dtype)
        store(pair).start()

    @pl.loop(0, pairs)
    def _(pair):
        store(pair).wait()


def apply_filter(coefficients, filter_weight):
    chunks = coefficients.shape[0]
    degrees = filter_weight.shape[0]
    pairs = degrees // 2
    orders = chunks * ROWS
    anywhere = pl.BlockSpec(memory_space=pl.ANY)
    return pl.pallas_call(
        filter_kernel,
        out_shape=jax.ShapeDtypeStruct((degrees, orders, WIDE), jnp.bfloat16),
        in_specs=[anywhere, pl.BlockSpec(memory_space=pltpu.VMEM)],
        out_specs=anywhere,
        scratch_shapes=[
            pltpu.VMEM((pairs, chunks, 2 * ROWS, WIDE), jnp.bfloat16),
            pltpu.VMEM((pairs, 2, orders, WIDE), jnp.bfloat16),
            pltpu.VMEM((degrees, WIDE, WIDE), jnp.bfloat16),
            pltpu.SemaphoreType.DMA((pairs,)),
            pltpu.SemaphoreType.DMA((pairs,)),
        ],
        compiler_params=pltpu.CompilerParams(vmem_limit_bytes=VMEM_CAP),
    )(coefficients, filter_weight)


def body(grid_field, norm_gain, filter_weight):
    count = lax.axis_size("lat")
    band, longitudes, columns = grid_field.shape
    fits = scratch_bytes(scratch_of(count, band, longitudes)) < VMEM_CAP - 3 * 1024 * 1024
    if count % PLANE or band % ROWS != ROWS - 1 or band < 2 * ROWS or not fits:
        return plain_body(grid_field, norm_gain, filter_weight)
    coefficients = coefficients_of(grid_field, norm_gain, count)
    return apply_filter(coefficients, filter_weight)


def solution(mesh):
    in_specs = (P("lat", None, "parts"), P("parts"), P("lat", None, None, "parts"))
    out_specs = P("lat", None, "parts")
    return jax.shard_map(body, mesh=mesh, in_specs=in_specs, out_specs=out_specs, check_vma=False)
```
